128 devices in a mesh: vol: 2 (over core), wide: 32 (over z_hi, x, y), narrow: 2 (over z_lo).
Axes of the slice: x: 4, y: 4, z: 4 (z_hi: 2, z_lo: 2; z = z_hi * 2 + z_lo), core: 2. Of those that a mesh axis runs over, the one named last changes fastest.
Arguments:
- forcing: float32 [2, 4, 384, 4096], P(None, 'vol', 'narrow', 'wide'), may hold values from -180 to 180
- material_ids: int32 [4, 384, 4096], P('vol', 'narrow', 'wide'), may hold values from 0 to 7
- materials: float32 [8], replicated, may hold values from 0.5 to 2
- boundary_operator: bfloat16 [4096, 131072], P('wide', 'narrow'), may hold values from -0.015625 to 0.015625
Outputs:
- pressure: float32 [2, 4, 384, 4096], P(None, 'vol', 'narrow', 'wide')
- traction: float32 [4096, 2], P(('wide', 'narrow'), 'vol')
The draws below stay inside these ranges and needn't reach their ends.
All inputs are finite; a program needn't handle non-finite values.
Results may differ from the reference program's by a relative error of at most 0.0031.
Values may be sent and summed in bfloat16 or wider, within the bound.
A program may use at most 128 MiB of HBM per device.

```python
import math
import jax
import jax.numpy as jnp
from jax import lax

K = 2
CY = 192
CX = 128
BY = 16
RY = 1
RX = 64
MAT = 8
ITERS = 2
SWEEPS = 2
NZ = 4
NY = 384
NX = 4096
NB = 131072
ROWS = 4096
N_WIDE = 32
N_NARROW = 2


def plant(result, rng, least, largest):
    extent = result.shape
    spot = [jax.random.randint(jax.random.fold_in(rng, axis), (), 0, extent[axis]) for axis in range(len(extent))]
    result = result.at[tuple(spot)].set(least)
    longest = extent.index(max(extent))
    spot[longest] = (spot[longest] + 1) % extent[longest]
    return result.at[tuple(spot)].set(largest)


def levels(key, shape, shards, smallest, largest):
    factor_of = 1.0
    for dim, shards_of in shards:
        draws = jax.random.uniform(jax.random.fold_in(jax.random.fold_in(key, 6), dim), (shards_of,), jnp.float32, smallest / len(shards), largest / len(shards))
        factor_of = factor_of * jnp.repeat(jnp.exp(draws), shape[dim] // shards_of).reshape((-1,) + (1,) * (len(shape) - 1 - dim))
    return factor_of


def bell_draw(stream_key, shape, scale, most, split=(), dtype=jnp.bfloat16):
    result = scale * jax.random.normal(stream_key, shape, jnp.float32)
    if split:
        result = result * levels(stream_key, shape, split, -0.22, 0.18)
    return jnp.clip(result, -most, most).astype(dtype)


def setup_inputs(seed: int = 0) -> dict:
    keys = jax.random.split(jax.random.key(seed), 5)
    return {
        "forcing": bell_draw(keys[0], (K, NZ, NY, NX), 30.0, 180.0, ((1, 2), (2, 2), (3, 32)), jnp.float32),
        "material_ids": plant(jax.random.randint(keys[1], (NZ, NY, NX), 0, MAT), jax.random.fold_in(keys[1], 1), 0, MAT - 1).astype(jnp.int32),
        "materials": jnp.clip(jnp.exp(jax.random.uniform(keys[2], (MAT,), jnp.float32, math.log(0.5), math.log(2.0))), 0.5, 2.0),
        "boundary_operator": bell_draw(keys[3], (ROWS, NB), NB ** -0.5, 0.015625, ((0, 32), (1, 2))),
    }


lower_edge = 0.25
upper_edge = 1.75
mass_ratio = 26.0
couple_gain = 40.0


def sweep_weights(count):
    middle = (upper_edge + lower_edge) / 2.0
    spread = (upper_edge - lower_edge) / 2.0
    center_ratio = middle / spread
    ratio_last = 1.0 / center_ratio
    weights = [(0.0, 1.0 / middle)]
    for number in range(1, count):
        ratio_next = 1.0 / (2.0 * center_ratio - ratio_last)
        weights.append((ratio_next * ratio_last, 2.0 * ratio_next / spread))
        ratio_last = ratio_next
    return weights


def box_sum(padded):
    along = padded[..., :-2] + padded[..., 1:-1] + padded[..., 2:]
    along = along[..., :-2, :] + along[..., 1:-1, :] + along[..., 2:, :]
    return along[..., :-2, :, :] + along[..., 1:-1, :, :] + along[..., 2:, :, :]


def apply_operator(padded, center, cond_pad, conductance, diagonal):
    neighbours = box_sum(padded) - center
    weighted = box_sum(padded * cond_pad) - conductance * center
    return diagonal * center - 0.5 * (conductance * neighbours + weighted)


def reference(forcing, material_ids, materials, boundary_operator):
    conductance = materials[material_ids]
    cond_pad = jnp.pad(conductance, 1)
    diagonal = 0.5 * (26.0 * conductance + (box_sum(cond_pad) - conductance)) + mass_ratio * conductance

    def relax_one(pair):
        vol_field, source = pair
        moved = jnp.zeros_like(vol_field)
        for keep_weight, gain_weight in sweep_weights(SWEEPS):
            padded = jnp.pad(vol_field, 1)
            scaled = (source - apply_operator(padded, vol_field, cond_pad, conductance, diagonal)) / diagonal
            moved = keep_weight * moved + gain_weight * scaled
            vol_field = vol_field + moved
        return vol_field

    stride = CY // BY
    pressure = jnp.zeros(forcing.shape, jnp.float32)
    source = forcing
    traction = jnp.zeros((ROWS, K), jnp.float32)
    for outer in range(ITERS):
        pressure = lax.map(relax_one, (pressure, source))
        outer_layer = pressure[:, NZ - 1].reshape(K, N_NARROW, CY, NX)[:, :, ::stride]
        trace = outer_layer.reshape(K, NB).astype(jnp.bfloat16)
        traction = jnp.dot(boundary_operator, jnp.transpose(trace), preferred_element_type=jnp.float32)
        if outer + 1 < ITERS:
            placed = traction.reshape(N_WIDE, N_NARROW, RY, RX, K).transpose(4, 1, 2, 0, 3)
            placed = jnp.pad(placed, ((0, 0), (0, 0), (0, CY - RY), (0, 0), (0, CX - RX))).reshape(K, NY, NX)
            source = forcing.at[:, NZ - 1].add(couple_gain * placed)
    return pressure, traction
```

```python
import functools

import jax
import jax.numpy as jnp
from jax import lax
from jax.experimental import pallas as pl
from jax.experimental.pallas import tpu as pltpu
from jax.sharding import PartitionSpec as P

MESH = pl.DeviceIdType.MESH

BY = 16
RX = 64
MAT = 8

lower_edge = 0.25
upper_edge = 1.75
couple_gain = 40.0

middle = (upper_edge + lower_edge) / 2.0
spread = (upper_edge - lower_edge) / 2.0
center_ratio = middle / spread
ratio_0 = 1.0 / center_ratio
ratio_1 = 1.0 / (2.0 * center_ratio - ratio_0)
gain0 = 1.0 / middle
keep1 = ratio_1 * ratio_0
gain1 = 2.0 * ratio_1 / spread

CY = 192
CX = 128
NZ = 4
PAD = 16
ROWS_ALL = PAD + CY + PAD
HALO = 8
CHUNK = 16
CHUNKS = (CY + 2 * HALO) // CHUNK
SLOT = 8
GROUPS = 4
GROUP_ROWS = CY // GROUPS


def select_materials(ids, materials):
    value = jnp.full(ids.shape, materials[0], jnp.float32)
    for number in range(1, MAT):
        value = jnp.where(ids == number, materials[number], value)
    return value


def kernel(
    wide_count,
    forcing,
    ids,
    materials,
    op,
    out_p,
    out_t,
    fv,
    iv,
    f,
    c,
    inv,
    m,
    pa,
    qa,
    pb,
    qb,
    strip,
    corner,
    got_strip,
    got_corner,
    opv,
    g1,
    g2,
    g3,
    part,
    got_part,
    last_part,
    got_last,
    local_sem,
    op_sem,
    s_send,
    s_recv,
    g_send,
    g_recv,
    x_send,
    x_recv,
    o_send,
    o_recv,
    o_local,
):
    v = lax.axis_index("vol")
    w = lax.axis_index("wide")
    n = lax.axis_index("narrow")
    other_v = 1 - v
    other_n = 1 - n
    right = lax.rem(w + 1, wide_count)
    left = lax.rem(w + wide_count - 1, wide_count)

    def device(vol, wide, narrow):
        return {"vol": vol, "wide": wide, "narrow": narrow}

    barrier = pltpu.get_barrier_semaphore()

    def greet(vol, wide, narrow):
        pl.semaphore_signal(
            barrier, inc=1, device_id=device(vol, wide, narrow), device_id_type=MESH
        )

    greet(other_v, w, n)
    for k in (0, 1):
        greet(k, w, other_n)
        for side in (left, right):
            greet(k, side, other_n)
    for side in (left, right):
        greet(other_v, side, n)

    def greet_wide(j, carry):
        greet(v, lax.rem(w + j, wide_count), n)
        return carry

    lax.fori_loop(1, wide_count, greet_wide, 0)

    load_ids = pltpu.make_async_copy(ids, iv, local_sem.at[0])
    load_f = pltpu.make_async_copy(forcing, fv, local_sem.at[1])
    load_own = pltpu.make_async_copy(
        forcing.at[v], f.at[0, pl.ds(2 * v, 2), pl.ds(PAD, CY), :], local_sem.at[2]
    )
    load_ids.start()
    load_f.start()
    load_own.start()

    zeros8 = jnp.zeros((8, CX), jnp.float32)
    for ref in (c, pa, qa, pb, qb):
        for t in (0, 1):
            for z in range(NZ):
                ref[t, z, 0:8, :] = zeros8
                ref[t, z, ROWS_ALL - 8 : ROWS_ALL, :] = zeros8
    outside = pl.multiple_of(PAD - HALO + other_n * 0 + n * (CY + HALO), 8)
    inside = pl.multiple_of(PAD - HALO + other_n * (CY + HALO), 8)
    for ref in (f, c):
        for t in (0, 1):
            for z in range(NZ):
                ref[t, z, pl.ds(outside, 8), :] = zeros8

    load_ids.wait()
    for layer in (0, 1):
        c[0, 2 * v + layer, PAD : PAD + CY, :] = select_materials(iv[layer], materials)
    load_f.wait()

    span = wide_count * CX

    def op_chunk(s):
        columns = pl.ds(pl.multiple_of(s * span, span), span)
        return pltpu.make_async_copy(op.at[:, columns], opv.at[:, columns], op_sem.at[s])

    edge_row = pl.multiple_of(other_n * (CY - 8), 8)
    lane = lax.broadcasted_iota(jnp.int32, (GROUP_ROWS, CX), 1)
    lane8 = lax.broadcasted_iota(jnp.int32, (8, CX), 1)
    for k in (0, 1):
        packed = jnp.zeros((GROUP_ROWS, CX), jnp.float32)
        edge = jnp.zeros((8, CX), jnp.float32)
        for field in range(4):
            for group in range(GROUPS):
                rows = pl.ds(group * GROUP_ROWS, GROUP_ROWS)
                if field < 2:
                    x = fv[k, field, rows, :]
                else:
                    x = c[0, 2 * v + field - 2, pl.ds(PAD + group * GROUP_ROWS, GROUP_ROWS), :]
                at = group * 4 * SLOT + field * SLOT
                x = pltpu.roll(x, (at + 4) % CX, 1)
                packed = jnp.where((lane >= at) & (lane < at + SLOT), x, packed)
            if field < 2:
                x = fv[k, field, pl.ds(edge_row, 8), :]
            else:
                x = c[0, 2 * v + field - 2, pl.ds(PAD + edge_row, 8), :]
            at = field * SLOT
            x = pltpu.roll(x, at + 4, 1)
            edge = jnp.where((lane8 >= at) & (lane8 < at + SLOT), x, edge)
        strip[k] = packed
        corner[k] = edge

    pl.semaphore_wait(barrier, wide_count - 1 + 9)

    sends = []

    def send(src, dst, send_sem, recv_sem, where):
        copy = pltpu.make_async_remote_copy(
            src_ref=src,
            dst_ref=dst,
            send_sem=send_sem,
            recv_sem=recv_sem,
            device_id=where,
            device_id_type=MESH,
        )
        copy.start()
        sends.append(copy)
        return copy

    own_layers = pl.ds(2 * v, 2)
    there_row = pl.multiple_of(PAD - HALO + n * (CY + HALO), 8)
    for k in (0, 1):
        for direction, side in ((0, right), (1, left)):
            send(
                strip.at[k],
                got_strip.at[direction, v],
                s_send.at[6 + 2 * direction + k],
                s_recv.at[6 + 2 * direction + v],
                device(k, side, n),
            )
    send(
        fv.at[other_v],
        f.at[0, own_layers, pl.ds(PAD, CY), :],
        s_send.at[0],
        s_recv.at[0],
        device(other_v, w, n),
    )
    own_block = c.at[0, own_layers, pl.ds(PAD, CY), :]
    send(own_block, own_block, s_send.at[1], s_recv.at[1], device(other_v, w, n))
    for k in (0, 1):
        send(
            fv.at[k, :, pl.ds(edge_row, 8), :],
            f.at[0, own_layers, pl.ds(there_row, 8), :],
            s_send.at[2 + k],
            s_recv.at[2 + v],
            device(k, w, other_n),
        )
        send(
            c.at[0, own_layers, pl.ds(pl.multiple_of(PAD + edge_row, 8), 8), :],
            c.at[0, own_layers, pl.ds(there_row, 8), :],
            s_send.at[4 + k],
            s_recv.at[4 + v],
            device(k, w, other_n),
        )
        for direction, side in ((0, right), (1, left)):
            send(
                corner.at[k],
                got_corner.at[direction, v],
                s_send.at[10 + 2 * direction + k],
                s_recv.at[10 + 2 * direction + v],
                device(k, side, other_n),
            )

    def start_op(s, carry):
        op_chunk(s).start()
        return carry

    lax.fori_loop(0, BY, start_op, 0)

    def wait_bytes(ref, sem):
        pltpu.make_async_copy(ref, ref, sem).wait()

    has_left = w > 0
    has_right = w < wide_count - 1
    for direction in (0, 1):
        for vol in (0, 1):
            wait_bytes(got_strip.at[direction, vol], s_recv.at[6 + 2 * direction + vol])
            wait_bytes(got_corner.at[direction, vol], s_recv.at[10 + 2 * direction + vol])
    keep_left = jnp.where(has_left, 1.0, 0.0)
    keep_right = jnp.where(has_right, 1.0, 0.0)
    for z in range(NZ):
        vol = z // 2
        from_left = lax.rem(lane, SLOT) < 4
        merged = jnp.where(
            from_left, got_strip[0, vol] * keep_left, got_strip[1, vol] * keep_right
        )
        from_left8 = lax.rem(lane8, SLOT) < 4
        merged8 = jnp.where(
            from_left8, got_corner[0, vol] * keep_left, got_corner[1, vol] * keep_right
        )
        for which, ref in ((0, f), (2, c)):
            field = which + z % 2
            for group in range(GROUPS):
                at = group * 4 * SLOT + field * SLOT
                x = pltpu.roll(merged, (CX - 4 - at) % CX, 1)
                x = jnp.where((lane < 4) | (lane >= CX - 4), x, 0.0)
                ref[1, z, pl.ds(PAD + group * GROUP_ROWS, GROUP_ROWS), :] = x
            at = field * SLOT
            x = pltpu.roll(merged8, (CX - 4 - at) % CX, 1)
            x = jnp.where((lane8 < 4) | (lane8 >= CX - 4), x, 0.0)
            ref[1, z, pl.ds(inside, 8), :] = x
    load_own.wait()
    wait_bytes(f.at[0, pl.ds(2 * other_v, 2), pl.ds(PAD, CY), :], s_recv.at[0])
    wait_bytes(c.at[0, pl.ds(2 * other_v, 2), pl.ds(PAD, CY), :], s_recv.at[1])
    for vol in (0, 1):
        wait_bytes(f.at[0, pl.ds(2 * vol, 2), pl.ds(inside, 8), :], s_recv.at[2 + vol])
        wait_bytes(c.at[0, pl.ds(2 * vol, 2), pl.ds(inside, 8), :], s_recv.at[4 + vol])

    lane_c = lax.broadcasted_iota(jnp.int32, (CHUNK, CX), 1)
    first = lane_c == 0
    final = lane_c == CX - 1

    def box(ref, r, tiles=2):
        ys = [
            [
                ref[t, z, pl.ds(r - 1, CHUNK), :]
                + ref[t, z, pl.ds(r, CHUNK), :]
                + ref[t, z, pl.ds(r + 1, CHUNK), :]
                for z in range(NZ)
            ]
            for t in (0, 1)
        ]
        sums = []
        for y in ys:
            low, high = y[0] + y[1], y[2] + y[3]
            sums.append((low, low + y[2], y[1] + high, high))
        result = [[], []]
        for z in range(NZ):
            center, side = sums[0][z], sums[1][z]
            center_up, side_up = pltpu.roll(center, 1, 1), pltpu.roll(side, 1, 1)
            center_down, side_down = (
                pltpu.roll(center, CX - 1, 1),
                pltpu.roll(side, CX - 1, 1),
            )
            result[0].append(
                center
                + jnp.where(first, side_up, center_up)
                + jnp.where(final, side_down, center_down)
            )
            if tiles == 2:
                result[1].append(
                    side
                    + jnp.where(first, center_up, side_up)
                    + jnp.where(final, center_down, side_down)
                )
        return result

    def rows_of(i):
        return pl.multiple_of(PAD - HALO + i * CHUNK, 8)

    def first_sweep(i, carry):
        r = rows_of(i)
        sums = box(c, r)
        for t in (0, 1):
            for z in range(NZ):
                cond = c[t, z, pl.ds(r, CHUNK), :]
                diagonal = 38.5 * cond + 0.5 * sums[t][z]
                inverse = jnp.where(cond > 0.0, 1.0 / diagonal, 0.0)
                inv[t, z, pl.ds(r, CHUNK), :] = inverse
                u = gain0 * f[t, z, pl.ds(r, CHUNK), :] * inverse
                pa[t, z, pl.ds(r, CHUNK), :] = u
                qa[t, z, pl.ds(r, CHUNK), :] = cond * u
        return carry

    def sweep(p, q, r, use, tiles=2):
        p_sums, q_sums = box(p, r, tiles), box(q, r, tiles)
        for t in range(tiles):
            for z in range(NZ):
                at = (t, z, pl.ds(r, CHUNK), slice(None))
                cond = c[at]
                u = p[at]
                scaled = (
                    f[at] + 0.5 * (cond * p_sums[t][z] + q_sums[t][z]) - q[at]
                ) * inv[at] - u
                use(at, cond, u, scaled)

    def second_sweep(i, carry):
        def use(at, cond, u, scaled):
            u = (1.0 + keep1) * u + gain1 * scaled
            pb[at] = u
            qb[at] = cond * u

        sweep(pa, qa, rows_of(i), use)
        return carry

    def third_sweep(i, carry):
        def use(at, cond, u, scaled):
            moved = gain0 * scaled
            u = u + moved
            m[at] = moved
            pa[at] = u
            qa[at] = cond * u

        sweep(pb, qb, rows_of(i), use)
        return carry

    def fourth_sweep(i, carry):
        def use(at, cond, u, scaled):
            pb[at] = u + (keep1 * m[at] + gain1 * scaled)

        sweep(pa, qa, rows_of(i), use, 1)
        return carry

    my_columns = pl.ds(pl.multiple_of(w * CX, CX), CX)

    def share(g, number):
        def to(j, carry):
            pltpu.make_async_remote_copy(
                src_ref=g.at[:, my_columns],
                dst_ref=g.at[:, my_columns],
                send_sem=g_send.at[number],
                recv_sem=g_recv.at[number],
                device_id=device(v, lax.rem(w + j, wide_count), n),
                device_id_type=MESH,
            ).start()
            return carry

        lax.fori_loop(1, wide_count, to, 0)

    def trace():
        return pb[0, NZ - 1, pl.ds(PAD, BY, stride=CY // BY), :].astype(jnp.bfloat16)

    row16 = lax.broadcasted_iota(jnp.int32, (BY, CX), 0)

    def product(g, low, high, fetch=False):
        def add(s, total):
            if fetch:
                op_chunk(s).wait()
            block = opv[:, pl.ds(pl.multiple_of(s * span, span), span)]
            rows = lax.dot_general(
                g[...], block, (((1,), (1,)), ((), ())), preferred_element_type=jnp.float32
            )
            return total + jnp.where(row16 == s, rows, 0.0)

        total = lax.fori_loop(low, high, add, jnp.zeros((BY, CX), jnp.float32))
        return jnp.sum(total, axis=0, keepdims=True)

    lax.fori_loop(0, CHUNKS, first_sweep, 0)
    lax.fori_loop(0, CHUNKS, second_sweep, 0)
    g1[:, my_columns] = trace()
    share(g1, 0)
    lax.fori_loop(0, CHUNKS, third_sweep, 0)
    lax.fori_loop(0, CHUNKS, fourth_sweep, 0)
    g2[:, my_columns] = trace()
    share(g2, 1)

    def store_rows(number, y, count):
        here = out_p.at[v, :, pl.ds(y, count), :]
        own = pltpu.make_async_copy(
            pb.at[0, own_layers, pl.ds(PAD + y, count), :], here, o_local.at[number]
        )
        own.start()
        send(
            pb.at[0, pl.ds(2 * other_v, 2), pl.ds(PAD + y, count), :],
            here,
            o_send.at[number],
            o_recv.at[number],
            device(other_v, w, n),
        )
        return own

    stores = [store_rows(0, 8, CY - 16)]

    wait_bytes(g1.at[:, CX:], g_recv.at[0])
    part1 = product(g1, 0, BY, True)
    part[...] = jnp.broadcast_to(part1, (8, CX))
    for number, (side, narrow) in enumerate(((w, other_n), (left, n), (left, other_n))):
        send(
            part,
            got_part.at[number],
            x_send.at[number],
            x_recv.at[number],
            device(v, side, narrow),
        )
    wait_bytes(g2.at[:, CX:], g_recv.at[1])
    part2 = product(g2, 1, BY)
    for number in range(3):
        wait_bytes(got_part.at[number], x_recv.at[number])

    here = part[...] + got_part[0]
    beyond = got_part[1] + got_part[2]
    here_high, beyond_high = pltpu.roll(here, CX - RX, 1), pltpu.roll(beyond, CX - RX, 1)
    is_first = n == 0
    row8 = lax.broadcasted_iota(jnp.int32, (8, CX), 0)

    def source_row(low, high, width, flag):
        return jnp.where(lane8 < width, couple_gain * jnp.where(flag, low, high), 0.0)[0:1]

    delta_own = source_row(here, here_high, RX, is_first)
    delta_side = source_row(beyond, beyond_high, 1, is_first)
    below = jnp.where(is_first, 1.0, 0.0)
    delta_below = below * source_row(here_high, here_high, RX, is_first)
    delta_below_side = below * source_row(beyond_high, beyond_high, 1, is_first)
    lane1 = lax.broadcasted_iota(jnp.int32, (1, CX), 1)

    def x_sum(center, side):
        return (
            center
            + pltpu.roll(jnp.broadcast_to(center, (8, CX)), 1, 1)[0:1]
            + jnp.where(
                lane1 == CX - 1,
                pltpu.roll(jnp.broadcast_to(side, (8, CX)), CX - 1, 1)[0:1],
                pltpu.roll(jnp.broadcast_to(center, (8, CX)), CX - 1, 1)[0:1],
            )
        )

    def added(delta, side, row, tile_row, near, at_target):
        q_center = gain0 * delta * inv[0, NZ - 1, row : row + 1, :]
        q_side = gain0 * side * inv[1, NZ - 1, row : row + 1, :]
        s_q = jnp.where(near, x_sum(q_center, q_side), 0.0)
        s_cq = jnp.where(
            near,
            x_sum(
                c[0, NZ - 1, row : row + 1, :] * q_center,
                c[1, NZ - 1, row : row + 1, :] * q_side,
            ),
            0.0,
        )
        for z in (NZ - 2, NZ - 1):
            rows = pl.ds(tile_row, 8)
            cond = c[0, z, rows, :]
            inverse = inv[0, z, rows, :]
            change = gain1 * 0.5 * (cond * s_q + s_cq) * inverse
            if z == NZ - 1 and at_target is not None:
                q = jnp.where(at_target, q_center, 0.0)
                source = jnp.where(at_target, delta, 0.0)
                change = (
                    change
                    + (1.0 + keep1) * q
                    + gain1 * ((source - cond * q) * inverse - q)
                )
            pb[0, z, rows, :] = pb[0, z, rows, :] + change

    added(delta_own, delta_side, PAD, PAD, row8 <= 1, row8 == 0)
    added(delta_below, delta_below_side, PAD + CY, PAD + CY - 8, row8 == 7, None)
    g3[:, my_columns] = trace()
    share(g3, 2)
    stores.append(store_rows(1, 0, 8))
    stores.append(store_rows(2, CY - 8, 8))

    wait_bytes(g3.at[:, CX:], g_recv.at[2])
    last = part2 + product(g3, 0, 1)
    last_part[...] = jnp.broadcast_to(last, (8, CX))
    send(last_part, got_last, x_send.at[3], x_recv.at[3], device(v, w, other_n))
    wait_bytes(got_last, x_recv.at[3])
    traction = last_part[...] + got_last[...]
    traction = jnp.where(is_first, traction, pltpu.roll(traction, CX - RX, 1))
    turned = jnp.transpose(jnp.broadcast_to(traction[0:1], (CX, CX)))
    out_t[...] = turned[0:RX, 0:1]

    for own in stores:
        own.wait()
    for number, (y, count) in enumerate(((8, CY - 16), (0, 8), (CY - 8, 8))):
        wait_bytes(out_p.at[other_v, :, pl.ds(y, count), :], o_recv.at[number])
    for copy in sends:
        copy.wait_send()
    for number, g in enumerate((g1, g2, g3)):
        wait_bytes(g.at[:, CX:], g_send.at[number])


def local(forcing, material_ids, materials, boundary_operator):
    wide_count = lax.axis_size("wide")
    field = pltpu.VMEM((2, NZ, ROWS_ALL, CX), jnp.float32)
    gathered = pltpu.VMEM((BY, wide_count * CX), jnp.bfloat16)
    dma = pltpu.SemaphoreType.DMA
    anywhere = pl.BlockSpec(memory_space=pl.ANY)
    rows = boundary_operator.shape[0]
    return pl.pallas_call(
        functools.partial(kernel, wide_count),
        out_shape=(
            jax.ShapeDtypeStruct(forcing.shape, jnp.float32),
            jax.ShapeDtypeStruct((RX, 1), jnp.float32),
        ),
        in_specs=[
            anywhere,
            anywhere,
            pl.BlockSpec(memory_space=pltpu.SMEM),
            anywhere,
        ],
        out_specs=(anywhere, pl.BlockSpec(memory_space=pltpu.VMEM)),
        scratch_shapes=[
            pltpu.VMEM(forcing.shape, jnp.float32),
            pltpu.VMEM(material_ids.shape, jnp.int32),
            field,
            field,
            field,
            field,
            field,
            field,
            field,
            field,
            pltpu.VMEM((2, GROUP_ROWS, CX), jnp.float32),
            pltpu.VMEM((2, 8, CX), jnp.float32),
            pltpu.VMEM((2, 2, GROUP_ROWS, CX), jnp.float32),
            pltpu.VMEM((2, 2, 8, CX), jnp.float32),
            pltpu.VMEM(boundary_operator.shape, jnp.bfloat16),
            gathered,
            gathered,
            gathered,
            pltpu.VMEM((8, CX), jnp.float32),
            pltpu.VMEM((3, 8, CX), jnp.float32),
            pltpu.VMEM((8, CX), jnp.float32),
            pltpu.VMEM((8, CX), jnp.float32),
            dma((3,)),
            dma((BY,)),
            dma((14,)),
            dma((14,)),
            dma((3,)),
            dma((3,)),
            dma((4,)),
            dma((4,)),
            dma((3,)),
            dma((3,)),
            dma((3,)),
        ],
        compiler_params=pltpu.CompilerParams(
            collective_id=0, has_side_effects=True, vmem_limit_bytes=48 * 1024 * 1024
        ),
        cost_estimate=pl.CostEstimate(
            flops=4 * rows * boundary_operator.shape[1],
            bytes_accessed=2 * rows * boundary_operator.shape[1],
            transcendentals=0,
        ),
    )(forcing, material_ids, materials, boundary_operator)


def solution(mesh):
    placed = (
        P(None, "vol", "narrow", "wide"),
        P("vol", "narrow", "wide"),
        P(),
        P("wide", "narrow"),
    )
    return jax.shard_map(
        local,
        mesh=mesh,
        in_specs=placed,
        out_specs=(P(None, "vol", "narrow", "wide"), P(("wide", "narrow"), "vol")),
        check_vma=False,
    )
```

```python
import functools

import jax
import jax.numpy as jnp
from jax import lax
from jax.experimental import pallas as pl
from jax.experimental.pallas import tpu as pltpu
from jax.sharding import PartitionSpec as P

MESH = pl.DeviceIdType.MESH

BY = 16
RX = 64
MAT = 8

lower_edge = 0.25
upper_edge = 1.75
couple_gain = 40.0

middle = (upper_edge + lower_edge) / 2.0
spread = (upper_edge - lower_edge) / 2.0
center_ratio = middle / spread
ratio_0 = 1.0 / center_ratio
ratio_1 = 1.0 / (2.0 * center_ratio - ratio_0)
gain0 = 1.0 / middle
keep1 = ratio_1 * ratio_0
gain1 = 2.0 * ratio_1 / spread

CY = 192
CX = 128
NZ = 4
PAD = 16
ROWS_ALL = PAD + CY + PAD
HALO = 8
CHUNK = 16
CHUNKS = (CY + 2 * HALO) // CHUNK
SLOT = 8
GROUPS = 4
GROUP_ROWS = CY // GROUPS
QUAD = 4


def select_materials(ids, materials):
    value = jnp.full(ids.shape, materials[0], jnp.float32)
    for number in range(1, MAT):
        value = jnp.where(ids == number, materials[number], value)
    return value


def kernel(
    wide_count,
    forcing,
    ids,
    materials,
    op,
    out_p,
    out_t,
    fv,
    iv,
    f,
    c,
    inv,
    m,
    pa,
    qa,
    pb,
    qb,
    strip,
    corner,
    got_strip,
    got_corner,
    opv,
    own_trace,
    g1,
    g2,
    part,
    total,
    coef,
    part2_own,
    part2_got,
    op_other,
    local_sem,
    op_sem,
    s_send,
    s_recv,
    g_send,
    g_recv,
    x_send,
    x_recv,
    o_send,
    o_recv,
    o_local,
    q_recv,
):
    v = lax.axis_index("vol")
    w = lax.axis_index("wide")
    n = lax.axis_index("narrow")
    other_v = 1 - v
    other_n = 1 - n
    right = lax.rem(w + 1, wide_count)
    left = lax.rem(w + wide_count - 1, wide_count)

    def device(vol, wide, narrow):
        return {"vol": vol, "wide": wide, "narrow": narrow}

    barrier = pltpu.get_barrier_semaphore()

    def greet(vol, wide, narrow):
        pl.semaphore_signal(
            barrier, inc=1, device_id=device(vol, wide, narrow), device_id_type=MESH
        )

    for narrow in (n, other_n):
        for side in (left, w, right):
            greet(other_v, side, narrow)
    greet(v, w, other_n)

    def greet_wide(j, carry):
        for narrow in (n, other_n):
            greet(v, lax.rem(w + j, wide_count), narrow)
        return carry

    lax.fori_loop(1, wide_count, greet_wide, 0)

    load_ids = pltpu.make_async_copy(ids, iv, local_sem.at[0])
    load_f = pltpu.make_async_copy(forcing, fv, local_sem.at[1])
    load_own = pltpu.make_async_copy(
        forcing.at[v], f.at[0, pl.ds(2 * v, 2), pl.ds(PAD, CY), :], local_sem.at[2]
    )
    load_ids.start()
    load_f.start()
    load_own.start()

    zeros8 = jnp.zeros((8, CX), jnp.float32)
    for ref in (c, pa, qa, pb, qb):
        for t in (0, 1):
            for z in range(NZ):
                ref[t, z, 0:8, :] = zeros8
                ref[t, z, ROWS_ALL - 8 : ROWS_ALL, :] = zeros8
    outside = pl.multiple_of(PAD - HALO + other_n * 0 + n * (CY + HALO), 8)
    inside = pl.multiple_of(PAD - HALO + other_n * (CY + HALO), 8)
    for ref in (f, c):
        for t in (0, 1):
            for z in range(NZ):
                ref[t, z, pl.ds(outside, 8), :] = zeros8

    load_ids.wait()
    for layer in (0, 1):
        c[0, 2 * v + layer, PAD : PAD + CY, :] = select_materials(iv[layer], materials)
    load_f.wait()

    span = wide_count * CX

    def op_chunk(s):
        columns = pl.ds(pl.multiple_of(s * span, span), span)
        return pltpu.make_async_copy(op.at[:, columns], opv.at[:, columns], op_sem.at[s])

    edge_row = pl.multiple_of(other_n * (CY - 8), 8)
    lane = lax.broadcasted_iota(jnp.int32, (GROUP_ROWS, CX), 1)
    lane8 = lax.broadcasted_iota(jnp.int32, (8, CX), 1)
    for k in (0, 1):
        packed = jnp.zeros((GROUP_ROWS, CX), jnp.float32)
        edge = jnp.zeros((8, CX), jnp.float32)
        for field in range(4):
            for group in range(GROUPS):
                rows = pl.ds(group * GROUP_ROWS, GROUP_ROWS)
                if field < 2:
                    x = fv[k, field, rows, :]
                else:
                    x = c[0, 2 * v + field - 2, pl.ds(PAD + group * GROUP_ROWS, GROUP_ROWS), :]
                at = group * 4 * SLOT + field * SLOT
                x = pltpu.roll(x, (at + 4) % CX, 1)
                packed = jnp.where((lane >= at) & (lane < at + SLOT), x, packed)
            if field < 2:
                x = fv[k, field, pl.ds(edge_row, 8), :]
            else:
                x = c[0, 2 * v + field - 2, pl.ds(PAD + edge_row, 8), :]
            at = field * SLOT
            x = pltpu.roll(x, at + 4, 1)
            edge = jnp.where((lane8 >= at) & (lane8 < at + SLOT), x, edge)
        strip[k] = packed
        corner[k] = edge

    pl.semaphore_wait(barrier, 2 * wide_count - 1 + 6)

    sends = []

    def send(src, dst, send_sem, recv_sem, where):
        copy = pltpu.make_async_remote_copy(
            src_ref=src,
            dst_ref=dst,
            send_sem=send_sem,
            recv_sem=recv_sem,
            device_id=where,
            device_id_type=MESH,
        )
        copy.start()
        sends.append(copy)
        return copy

    own_layers = pl.ds(2 * v, 2)
    there_row = pl.multiple_of(PAD - HALO + n * (CY + HALO), 8)
    for k in (0, 1):
        for direction, side in ((0, right), (1, left)):
            send(
                strip.at[k],
                got_strip.at[direction, v],
                s_send.at[6 + 2 * direction + k],
                s_recv.at[6 + 2 * direction + v],
                device(k, side, n),
            )
    send(
        fv.at[other_v],
        f.at[0, own_layers, pl.ds(PAD, CY), :],
        s_send.at[0],
        s_recv.at[0],
        device(other_v, w, n),
    )
    own_block = c.at[0, own_layers, pl.ds(PAD, CY), :]
    send(own_block, own_block, s_send.at[1], s_recv.at[1], device(other_v, w, n))
    for k in (0, 1):
        send(
            fv.at[k, :, pl.ds(edge_row, 8), :],
            f.at[0, own_layers, pl.ds(there_row, 8), :],
            s_send.at[2 + k],
            s_recv.at[2 + v],
            device(k, w, other_n),
        )
        send(
            c.at[0, own_layers, pl.ds(pl.multiple_of(PAD + edge_row, 8), 8), :],
            c.at[0, own_layers, pl.ds(there_row, 8), :],
            s_send.at[4 + k],
            s_recv.at[4 + v],
            device(k, w, other_n),
        )
        for direction, side in ((0, right), (1, left)):
            send(
                corner.at[k],
                got_corner.at[direction, v],
                s_send.at[10 + 2 * direction + k],
                s_recv.at[10 + 2 * direction + v],
                device(k, side, other_n),
            )

    def start_op(s, carry):
        op_chunk(s).start()
        return carry

    lax.fori_loop(0, BY, start_op, 0)

    def wait_bytes(ref, sem):
        pltpu.make_async_copy(ref, ref, sem).wait()

    has_left = w > 0
    has_right = w < wide_count - 1
    for direction in (0, 1):
        for vol in (0, 1):
            wait_bytes(got_strip.at[direction, vol], s_recv.at[6 + 2 * direction + vol])
            wait_bytes(got_corner.at[direction, vol], s_recv.at[10 + 2 * direction + vol])
    keep_left = jnp.where(has_left, 1.0, 0.0)
    keep_right = jnp.where(has_right, 1.0, 0.0)
    for z in range(NZ):
        vol = z // 2
        from_left = lax.rem(lane, SLOT) < 4
        merged = jnp.where(
            from_left, got_strip[0, vol] * keep_left, got_strip[1, vol] * keep_right
        )
        from_left8 = lax.rem(lane8, SLOT) < 4
        merged8 = jnp.where(
            from_left8, got_corner[0, vol] * keep_left, got_corner[1, vol] * keep_right
        )
        for which, ref in ((0, f), (2, c)):
            field = which + z % 2
            for group in range(GROUPS):
                at = group * 4 * SLOT + field * SLOT
                x = pltpu.roll(merged, (CX - 4 - at) % CX, 1)
                x = jnp.where((lane < 4) | (lane >= CX - 4), x, 0.0)
                ref[1, z, pl.ds(PAD + group * GROUP_ROWS, GROUP_ROWS), :] = x
            at = field * SLOT
            x = pltpu.roll(merged8, (CX - 4 - at) % CX, 1)
            x = jnp.where((lane8 < 4) | (lane8 >= CX - 4), x, 0.0)
            ref[1, z, pl.ds(inside, 8), :] = x
    load_own.wait()
    wait_bytes(f.at[0, pl.ds(2 * other_v, 2), pl.ds(PAD, CY), :], s_recv.at[0])
    wait_bytes(c.at[0, pl.ds(2 * other_v, 2), pl.ds(PAD, CY), :], s_recv.at[1])
    for vol in (0, 1):
        wait_bytes(f.at[0, pl.ds(2 * vol, 2), pl.ds(inside, 8), :], s_recv.at[2 + vol])
        wait_bytes(c.at[0, pl.ds(2 * vol, 2), pl.ds(inside, 8), :], s_recv.at[4 + vol])

    lane_c = lax.broadcasted_iota(jnp.int32, (CHUNK, CX), 1)
    first = lane_c == 0
    final = lane_c == CX - 1

    def box(ref, r, layers, tiles):
        inner = range(max(layers[0] - 1, 0), min(layers[-1] + 2, NZ))
        sums = []
        for t in (0, 1):
            y = {
                z: ref[t, z, pl.ds(r - 1, CHUNK), :]
                + ref[t, z, pl.ds(r, CHUNK), :]
                + ref[t, z, pl.ds(r + 1, CHUNK), :]
                for z in inner
            }
            low = y[0] + y[1] if 0 in layers or 1 in layers else None
            high = y[2] + y[3] if 2 in layers or 3 in layers else None
            made = {}
            for z in layers:
                made[z] = (
                    low if z == 0 else high if z == 3 else low + y[2] if z == 1 else y[1] + high
                )
            sums.append(made)
        result = ({}, {})
        for z in layers:
            center, side = sums[0][z], sums[1][z]
            center_up, side_up = pltpu.roll(center, 1, 1), pltpu.roll(side, 1, 1)
            center_down, side_down = (
                pltpu.roll(center, CX - 1, 1),
                pltpu.roll(side, CX - 1, 1),
            )
            result[0][z] = (
                center
                + jnp.where(first, side_up, center_up)
                + jnp.where(final, side_down, center_down)
            )
            if 1 in tiles:
                result[1][z] = (
                    side
                    + jnp.where(first, center_up, side_up)
                    + jnp.where(final, center_down, side_down)
                )
        return result

    def rows_of(i):
        return pl.multiple_of(PAD - HALO + i * CHUNK, 8)

    both = (0, 1)

    def first_sweep(i, layers):
        r = rows_of(i)
        sums = box(c, r, layers, both)
        for t in both:
            for z in layers:
                at = (t, z, pl.ds(r, CHUNK), slice(None))
                cond = c[at]
                diagonal = 38.5 * cond + 0.5 * sums[t][z]
                inverse = jnp.where(cond > 0.0, 1.0 / diagonal, 0.0)
                inv[at] = inverse
                u = gain0 * f[at] * inverse
                pa[at] = u
                qa[at] = cond * u

    def sweep(p, q, i, use, layers, tiles):
        r = rows_of(i)
        p_sums, q_sums = box(p, r, layers, tiles), box(q, r, layers, tiles)
        for t in tiles:
            for z in layers:
                at = (t, z, pl.ds(r, CHUNK), slice(None))
                cond = c[at]
                u = p[at]
                scaled = (
                    f[at] + 0.5 * (cond * p_sums[t][z] + q_sums[t][z]) - q[at]
                ) * inv[at] - u
                use(at, cond, u, scaled)

    def second_sweep(i, layers, tiles):
        def use(at, cond, u, scaled):
            u = (1.0 + keep1) * u + gain1 * scaled
            pb[at] = u
            qb[at] = cond * u

        sweep(pa, qa, i, use, layers, tiles)

    def third_sweep(i, layers):
        def use(at, cond, u, scaled):
            moved = gain0 * scaled
            u = u + moved
            m[at] = moved
            pa[at] = u
            qa[at] = cond * u

        sweep(pb, qb, i, use, layers, both)

    def fourth_sweep(i, layers):
        def use(at, cond, u, scaled):
            pb[at] = u + (keep1 * m[at] + gain1 * scaled)

        sweep(pa, qa, i, use, layers, (0,))

    def for_chunks(step):
        def body(i, carry):
            step(i)
            return carry

        lax.fori_loop(0, CHUNKS, body, 0, unroll=CHUNKS)

    my_columns = pl.ds(pl.multiple_of(w * CX, CX), CX)

    def share(block, numbers, narrows):
        def to(j, carry):
            for number, narrow in zip(numbers, narrows):
                pltpu.make_async_remote_copy(
                    src_ref=block,
                    dst_ref=block,
                    send_sem=g_send.at[number],
                    recv_sem=g_recv.at[number],
                    device_id=device(v, lax.rem(w + j, wide_count), narrow),
                    device_id_type=MESH,
                ).start()
            return carry

        lax.fori_loop(1, wide_count, to, 0)
        if len(numbers) == 2:
            pltpu.make_async_remote_copy(
                src_ref=block,
                dst_ref=block,
                send_sem=g_send.at[numbers[1]],
                recv_sem=g_recv.at[numbers[1]],
                device_id=device(v, w, other_n),
                device_id_type=MESH,
            ).start()

    def trace():
        return pb[0, NZ - 1, pl.ds(PAD, BY, stride=CY // BY), :].astype(jnp.bfloat16)

    row16 = lax.broadcasted_iota(jnp.int32, (BY, CX), 0)

    def product(g, low, high):
        def add(s, total):
            block = opv[:, pl.ds(pl.multiple_of(s * span, span), span)]
            rows = lax.dot_general(
                g[...], block, (((1,), (1,)), ((), ())), preferred_element_type=jnp.float32
            )
            return total + jnp.where(row16 == s, rows, 0.0)

        total = lax.fori_loop(
            low, high, add, jnp.zeros((BY, CX), jnp.float32), unroll=5
        )
        return jnp.sum(total, axis=0, keepdims=True)

    quads = wide_count // QUAD
    my_quad, my_place = w // QUAD, lax.rem(w, QUAD)

    def quad_at(d, sign):
        if quads % QUAD:
            return lax.rem(my_quad + sign * d + quads, quads)
        high, low = my_quad // QUAD, lax.rem(my_quad, QUAD)
        rings = quads // QUAD
        high = lax.rem(high + sign * (d // QUAD) + rings, rings)
        low = lax.rem(low + sign * lax.rem(d, QUAD) + QUAD, QUAD)
        return high * QUAD + low

    def share_first():
        def to(i, carry):
            d = i // QUAD
            place = lax.rem(my_place + lax.rem(i, QUAD), QUAD)
            pltpu.make_async_remote_copy(
                src_ref=own_trace,
                dst_ref=g1.at[:, my_columns],
                send_sem=g_send.at[0],
                recv_sem=q_recv.at[d],
                device_id=device(v, quad_at(d, 1) * QUAD + place, n),
                device_id_type=MESH,
            ).start()
            return carry

        lax.fori_loop(1, wide_count, lambda i, carry: to(wide_count - i, carry), 0)
        pltpu.make_async_copy(own_trace, g1.at[:, my_columns], q_recv.at[0]).start()

    lanes = QUAD * CX

    def product_first():
        for s in range(BY):
            op_chunk(s).wait()

        def add(i, total):
            step = lax.rem(i, QUAD)
            d = i - step + step + step // 2 - 2 * (step // 3)
            if quads % QUAD:
                d = i
            wait_bytes(g1.at[:, 0:lanes], q_recv.at[d])
            first_lane = quad_at(d, -1) * lanes
            x = g1[:, pl.ds(pl.multiple_of(first_lane, lanes), lanes)]
            for s in range(BY):
                block = opv[:, pl.ds(pl.multiple_of(s * span + first_lane, lanes), lanes)]
                rows = lax.dot_general(
                    x, block, (((1,), (1,)), ((), ())), preferred_element_type=jnp.float32
                )
                total = total + jnp.where(row16 == s, rows, 0.0)
            return total

        total = lax.fori_loop(0, quads, add, jnp.zeros((BY, CX), jnp.float32))
        return jnp.sum(total, axis=0, keepdims=True)

    for_chunks(lambda i: first_sweep(i, (2, 3)))
    for_chunks(lambda i: second_sweep(i, (3,), (0,)))
    own_trace[...] = trace()
    share_first()

    half = span // 2
    my_half = pl.ds(pl.multiple_of(v * half, half), half)
    their_half = pl.ds(pl.multiple_of(other_v * half, half), half)
    send(
        op.at[pl.ds(pl.multiple_of(other_n * RX, RX), RX), my_half],
        op_other.at[:, my_half],
        x_send.at[0],
        x_recv.at[0],
        device(v, w, other_n),
    )

    for_chunks(lambda i: first_sweep(i, (0, 1)))
    for_chunks(lambda i: second_sweep(i, (1, 2, 3), both))
    for_chunks(lambda i: third_sweep(i, (2, 3)))
    for_chunks(lambda i: fourth_sweep(i, (3,)))
    g2[:, my_columns] = trace()
    share(g2.at[:, my_columns], (1,), (n,))

    top = NZ - 1
    lane1 = lax.broadcasted_iota(jnp.int32, (8, CX), 1)

    def tile(ref, t, z, row):
        return ref[t, z, row : row + 8, :]

    def neighbours(ref, z, row):
        center, side = tile(ref, 0, z, row), tile(ref, 1, z, row)
        before = jnp.where(lane1 == 0, pltpu.roll(side, 1, 1), pltpu.roll(center, 1, 1))
        after = jnp.where(
            lane1 == CX - 1, pltpu.roll(side, CX - 1, 1), pltpu.roll(center, CX - 1, 1)
        )
        return before, after

    cond8, inverse8 = tile(c, 0, top, PAD), tile(inv, 0, top, PAD)
    cond_before, cond_after = neighbours(c, top, PAD)
    inverse_before, inverse_after = neighbours(inv, top, PAD)
    here8 = couple_gain * ((1.0 + keep1 - gain1) * gain0 + gain1) * inverse8
    beside = 0.5 * couple_gain * gain1 * gain0 * inverse8
    before8 = beside * (cond8 + cond_before) * inverse_before
    after8 = beside * (cond8 + cond_after) * inverse_after
    coef[n, 0:4, my_columns] = jnp.concatenate(
        [tile(pb, 0, top, PAD)[0:1], here8[0:1], before8[0:1], after8[0:1]], axis=0
    )
    share(coef.at[n, 0:4, my_columns], (2, 3), (n, other_n))

    part[n, 0:1, my_columns] = product_first()
    share(part.at[n, 0:1, my_columns], (4, 5), (n, other_n))

    wait_bytes(op_other.at[:, my_half], x_recv.at[0])
    send(
        op_other.at[:, my_half],
        op_other.at[:, my_half],
        x_send.at[1],
        x_recv.at[1],
        device(other_v, w, n),
    )
    wait_bytes(g2.at[:, CX:], g_recv.at[1])
    part2_own[...] = jnp.broadcast_to(product(g2, 1, BY), (8, CX))
    send(part2_own, part2_got, x_send.at[2], x_recv.at[2], device(v, w, other_n))
    for_chunks(lambda i: second_sweep(i, (0,), both))
    for_chunks(lambda i: third_sweep(i, (0, 1)))
    for_chunks(lambda i: fourth_sweep(i, (0, 1, 2)))

    def store_rows(number, y, count):
        here = out_p.at[v, :, pl.ds(y, count), :]
        own = pltpu.make_async_copy(
            pb.at[0, own_layers, pl.ds(PAD + y, count), :], here, o_local.at[number]
        )
        own.start()
        send(
            pb.at[0, pl.ds(2 * other_v, 2), pl.ds(PAD + y, count), :],
            here,
            o_send.at[number],
            o_recv.at[number],
            device(other_v, w, n),
        )
        return own

    stores = [store_rows(0, 8, CY - 16)]

    wait_bytes(coef.at[0, 0:4, CX:], g_recv.at[2])
    wait_bytes(coef.at[0, 0:4, :], g_recv.at[3])
    wait_bytes(op_other.at[:, their_half], x_recv.at[1])
    wait_bytes(part2_got, x_recv.at[2])
    part2 = part2_own[...] + part2_got[...]
    is_first = n == 0
    part2 = jnp.where(is_first, part2, pltpu.roll(part2, CX - RX, 1))
    part2_turned = jnp.transpose(jnp.broadcast_to(part2[0:1], (CX, CX)))[0:RX, 0:1]

    wait_bytes(part.at[0, 0:1, CX:], g_recv.at[4])
    wait_bytes(part.at[0, 0:1, :], g_recv.at[5])
    total[0:1, :] = part[0, 0:1, :] + part[1, 0:1, :]

    row8 = lax.broadcasted_iota(jnp.int32, (8, CX), 0)
    here = jnp.broadcast_to(total[0:1, my_columns], (8, CX))
    beyond = jnp.broadcast_to(
        total[0:1, pl.ds(pl.multiple_of(right * CX, CX), CX)], (8, CX)
    )
    here_high, beyond_high = pltpu.roll(here, CX - RX, 1), pltpu.roll(beyond, CX - RX, 1)

    def source_rows(low, high, width):
        return jnp.where(lane8 < width, couple_gain * jnp.where(is_first, low, high), 0.0)

    delta_own = source_rows(here, here_high, RX)
    delta_side = source_rows(beyond, beyond_high, 1)
    below = jnp.where(is_first, 1.0, 0.0)
    delta_below = below * source_rows(here_high, here_high, RX)
    delta_below_side = below * source_rows(beyond_high, beyond_high, 1)

    def x_sum(center, side):
        return (
            center
            + pltpu.roll(center, 1, 1)
            + jnp.where(
                lane8 == CX - 1, pltpu.roll(side, CX - 1, 1), pltpu.roll(center, CX - 1, 1)
            )
        )

    def added(delta, side, row, tile_row, near, at_target):
        def spread_row(ref, t):
            return jnp.broadcast_to(ref[t, top, row : row + 1, :], (8, CX))

        q_center = gain0 * delta * spread_row(inv, 0)
        q_side = gain0 * side * spread_row(inv, 1)
        s_q = jnp.where(near, x_sum(q_center, q_side), 0.0)
        s_cq = jnp.where(
            near, x_sum(spread_row(c, 0) * q_center, spread_row(c, 1) * q_side), 0.0
        )
        for z in (top - 1, top):
            rows = pl.ds(tile_row, 8)
            cond = c[0, z, rows, :]
            inverse = inv[0, z, rows, :]
            change = gain1 * 0.5 * (cond * s_q + s_cq) * inverse
            if z == top and at_target is not None:
                q = jnp.where(at_target, q_center, 0.0)
                source = jnp.where(at_target, delta, 0.0)
                change = (
                    change
                    + (1.0 + keep1) * q
                    + gain1 * ((source - cond * q) * inverse - q)
                )
            pb[0, z, rows, :] = pb[0, z, rows, :] + change

    added(delta_own, delta_side, PAD, PAD, row8 <= 1, row8 == 0)
    added(delta_below, delta_below_side, PAD + CY, PAD + CY - 8, row8 == 7, None)
    stores.append(store_rows(1, 0, 8))
    stores.append(store_rows(2, CY - 8, 8))

    lane_all = lax.broadcasted_iota(jnp.int32, (1, span), 1)
    at_targets = lax.rem(lane_all, CX) < RX
    traction = total[0:1, :]
    rows = []
    for half_n in (0, 1):
        value = traction if half_n == 0 else pltpu.roll(traction, span - RX, 1)
        value = jnp.where(at_targets, value, 0.0)
        rows.append(
            coef[half_n, 0:1, :]
            + coef[half_n, 1:2, :] * value
            + coef[half_n, 2:3, :] * pltpu.roll(value, 1, 1)
            + coef[half_n, 3:4, :] * pltpu.roll(value, span - 1, 1)
        )
    own_row = jnp.where(is_first, rows[0], rows[1]).astype(jnp.bfloat16)
    other_row = jnp.where(is_first, rows[1], rows[0]).astype(jnp.bfloat16)

    def against(block, row):
        return lax.dot_general(
            block,
            jnp.broadcast_to(row, (BY, span)),
            (((1,), (1,)), ((), ())),
            preferred_element_type=jnp.float32,
        )

    mine = opv[pl.ds(pl.multiple_of(n * RX, RX), RX), 0:span]
    last = against(mine, own_row) + against(op_other[...], other_row)
    out_t[...] = part2_turned + last[:, 0:1]

    for own in stores:
        own.wait()
    for number, (y, count) in enumerate(((8, CY - 16), (0, 8), (CY - 8, 8))):
        wait_bytes(out_p.at[other_v, :, pl.ds(y, count), :], o_recv.at[number])
    for copy in sends:
        copy.wait_send()
    for number, g in enumerate((g1, g2)):
        wait_bytes(g.at[:, CX:], g_send.at[number])
    for number, ref, count in ((2, coef, 4), (4, part, 1)):
        wait_bytes(ref.at[0, 0:count, CX:], g_send.at[number])
        wait_bytes(ref.at[0, 0:count, :], g_send.at[number + 1])


def local(forcing, material_ids, materials, boundary_operator):
    wide_count = lax.axis_size("wide")
    field = pltpu.VMEM((2, NZ, ROWS_ALL, CX), jnp.float32)
    gathered = pltpu.VMEM((BY, wide_count * CX), jnp.bfloat16)
    dma = pltpu.SemaphoreType.DMA
    anywhere = pl.BlockSpec(memory_space=pl.ANY)
    hbm = pl.BlockSpec(memory_space=pltpu.HBM)
    rows = boundary_operator.shape[0]
    quads = wide_count // QUAD
    return pl.pallas_call(
        functools.partial(kernel, wide_count),
        out_shape=(
            jax.ShapeDtypeStruct(forcing.shape, jnp.float32),
            jax.ShapeDtypeStruct((RX, 1), jnp.float32),
        ),
        in_specs=[
            hbm,
            hbm,
            pl.BlockSpec(memory_space=pltpu.SMEM),
            hbm,
        ],
        out_specs=(anywhere, pl.BlockSpec(memory_space=pltpu.VMEM)),
        scratch_shapes=[
            pltpu.VMEM(forcing.shape, jnp.float32),
            pltpu.VMEM(material_ids.shape, jnp.int32),
            field,
            field,
            field,
            field,
            field,
            field,
            field,
            field,
            pltpu.VMEM((2, GROUP_ROWS, CX), jnp.float32),
            pltpu.VMEM((2, 8, CX), jnp.float32),
            pltpu.VMEM((2, 2, GROUP_ROWS, CX), jnp.float32),
            pltpu.VMEM((2, 2, 8, CX), jnp.float32),
            pltpu.VMEM(boundary_operator.shape, jnp.bfloat16),
            pltpu.VMEM((BY, CX), jnp.bfloat16),
            gathered,
            gathered,
            pltpu.VMEM((2, 8, wide_count * CX), jnp.float32),
            pltpu.VMEM((8, wide_count * CX), jnp.float32),
            pltpu.VMEM((2, 8, wide_count * CX), jnp.float32),
            pltpu.VMEM((8, CX), jnp.float32),
            pltpu.VMEM((8, CX), jnp.float32),
            pltpu.VMEM((RX, wide_count * CX), jnp.bfloat16),
            dma((3,)),
            dma((BY,)),
            dma((14,)),
            dma((14,)),
            dma((6,)),
            dma((6,)),
            dma((3,)),
            dma((3,)),
            dma((3,)),
            dma((3,)),
            dma((3,)),
            dma((quads,)),
        ],
        compiler_params=pltpu.CompilerParams(
            collective_id=0, has_side_effects=True, vmem_limit_bytes=62 * 1024 * 1024
        ),
        cost_estimate=pl.CostEstimate(
            flops=4 * rows * boundary_operator.shape[1],
            bytes_accessed=2 * rows * boundary_operator.shape[1],
            transcendentals=0,
        ),
    )(forcing, material_ids, materials, boundary_operator)


def solution(mesh):
    placed = (
        P(None, "vol", "narrow", "wide"),
        P("vol", "narrow", "wide"),
        P(),
        P("wide", "narrow"),
    )
    return jax.shard_map(
        local,
        mesh=mesh,
        in_specs=placed,
        out_specs=(P(None, "vol", "narrow", "wide"), P(("wide", "narrow"), "vol")),
        check_vma=False,
    )
```

```python
import functools

import jax
import jax.numpy as jnp
from jax import lax
from jax.experimental import pallas as pl
from jax.experimental.pallas import tpu as pltpu
from jax.sharding import PartitionSpec as P

MESH = pl.DeviceIdType.MESH

BY = 16
RX = 64
MAT = 8

lower_edge = 0.25
upper_edge = 1.75
couple_gain = 40.0

middle = (upper_edge + lower_edge) / 2.0
spread = (upper_edge - lower_edge) / 2.0
center_ratio = middle / spread
ratio_0 = 1.0 / center_ratio
ratio_1 = 1.0 / (2.0 * center_ratio - ratio_0)
gain0 = 1.0 / middle
keep1 = ratio_1 * ratio_0
gain1 = 2.0 * ratio_1 / spread

CY = 192
CX = 128
NZ = 4
PAD = 16
ROWS_ALL = PAD + CY + PAD
HALO = 8
CHUNK = 16
CHUNKS = (CY + 2 * HALO) // CHUNK
SLOT = 8
GROUPS = 4
GROUP_ROWS = CY // GROUPS
QUAD = 4


def select_materials(ids, materials):
    value = jnp.full(ids.shape, materials[0], jnp.float32)
    for number in range(1, MAT):
        value = jnp.where(ids == number, materials[number], value)
    return value


def kernel(
    wide_count,
    forcing,
    ids,
    materials,
    op,
    out_p,
    out_t,
    fv,
    iv,
    f,
    c,
    inv,
    m,
    pa,
    qa,
    pb,
    qb,
    strip,
    corner,
    got_strip,
    got_corner,
    opv,
    own_trace,
    g1,
    g2,
    part,
    total,
    coef,
    part2_own,
    part2_got,
    row_t,
    op_other,
    local_sem,
    op_sem,
    s_send,
    s_recv,
    g_send,
    g_recv,
    x_send,
    x_recv,
    o_send,
    o_recv,
    o_local,
    q_recv,
    relay,
):
    v = lax.axis_index("vol")
    w = lax.axis_index("wide")
    n = lax.axis_index("narrow")
    other_v = 1 - v
    other_n = 1 - n
    right = lax.rem(w + 1, wide_count)
    left = lax.rem(w + wide_count - 1, wide_count)

    def device(vol, wide, narrow):
        return {"vol": vol, "wide": wide, "narrow": narrow}

    barrier = pltpu.get_barrier_semaphore()

    def signal(semaphore, vol, wide, narrow):
        pl.semaphore_signal(
            semaphore, inc=1, device_id=device(vol, wide, narrow), device_id_type=MESH
        )

    greeted = []

    def greet(vol, wide, narrow):
        signal(barrier, vol, wide, narrow)
        greeted.append(0)

    for narrow in (n, other_n):
        for side in (left, w, right):
            greet(other_v, side, narrow)
        for side in (left, right):
            greet(v, side, narrow)
    greet(v, w, other_n)

    quads = wide_count // QUAD
    my_quad, my_place = w // QUAD, lax.rem(w, QUAD)
    staged = quads == 2 * QUAD

    def quad_at(d, sign):
        if not staged:
            return lax.rem(my_quad + sign * d + quads, quads)
        high, low = my_quad // QUAD, lax.rem(my_quad, QUAD)
        high = lax.rem(high + d // QUAD, 2)
        low = lax.rem(low + sign * lax.rem(d, QUAD) + QUAD, QUAD)
        return high * QUAD + low

    y_ring = [my_quad * QUAD + lax.rem(my_place + j, QUAD) for j in range(1, QUAD)]
    if staged:
        for j in range(1, QUAD):
            greet(v, y_ring[j - 1], n)
            greet(v, quad_at(j, 1) * QUAD + my_place, n)
        opposite = lax.rem(w + wide_count // 2, wide_count)
        greet(v, opposite, n)
        greet(v, opposite, other_n)
    else:

        def greet_wide(j, carry):
            for narrow in (n, other_n):
                signal(barrier, v, lax.rem(w + j, wide_count), narrow)
            return carry

        lax.fori_loop(1, wide_count, greet_wide, 0)
        greeted.extend([0] * (2 * (wide_count - 1)))

    load_ids = pltpu.make_async_copy(ids, iv, local_sem.at[0])
    load_f = pltpu.make_async_copy(forcing, fv, local_sem.at[1])
    load_own = pltpu.make_async_copy(
        forcing.at[v], f.at[0, pl.ds(2 * v, 2), pl.ds(PAD, CY), :], local_sem.at[2]
    )
    load_ids.start()
    load_f.start()
    load_own.start()

    zeros8 = jnp.zeros((8, CX), jnp.float32)
    for ref in (c, pa, qa, pb, qb):
        for t in (0, 1):
            for z in range(NZ):
                ref[t, z, 0:8, :] = zeros8
                ref[t, z, ROWS_ALL - 8 : ROWS_ALL, :] = zeros8
    outside = pl.multiple_of(PAD - HALO + other_n * 0 + n * (CY + HALO), 8)
    inside = pl.multiple_of(PAD - HALO + other_n * (CY + HALO), 8)
    for ref in (f, c):
        for t in (0, 1):
            for z in range(NZ):
                ref[t, z, pl.ds(outside, 8), :] = zeros8

    load_ids.wait()
    for layer in (0, 1):
        c[0, 2 * v + layer, PAD : PAD + CY, :] = select_materials(iv[layer], materials)
    load_f.wait()

    span = wide_count * CX

    def op_chunk(s):
        columns = pl.ds(pl.multiple_of(s * span, span), span)
        return pltpu.make_async_copy(op.at[:, columns], opv.at[:, columns], op_sem.at[s])

    edge_row = pl.multiple_of(other_n * (CY - 8), 8)
    lane = lax.broadcasted_iota(jnp.int32, (GROUP_ROWS, CX), 1)
    lane8 = lax.broadcasted_iota(jnp.int32, (8, CX), 1)
    for k in (0, 1):
        packed = jnp.zeros((GROUP_ROWS, CX), jnp.float32)
        edge = jnp.zeros((8, CX), jnp.float32)
        for field in range(4):
            for group in range(GROUPS):
                rows = pl.ds(group * GROUP_ROWS, GROUP_ROWS)
                if field < 2:
                    x = fv[k, field, rows, :]
                else:
                    x = c[0, 2 * v + field - 2, pl.ds(PAD + group * GROUP_ROWS, GROUP_ROWS), :]
                at = group * 4 * SLOT + field * SLOT
                x = pltpu.roll(x, (at + 4) % CX, 1)
                packed = jnp.where((lane >= at) & (lane < at + SLOT), x, packed)
            if field < 2:
                x = fv[k, field, pl.ds(edge_row, 8), :]
            else:
                x = c[0, 2 * v + field - 2, pl.ds(PAD + edge_row, 8), :]
            at = field * SLOT
            x = pltpu.roll(x, at + 4, 1)
            edge = jnp.where((lane8 >= at) & (lane8 < at + SLOT), x, edge)
        strip[k] = packed
        corner[k] = edge

    pl.semaphore_wait(barrier, len(greeted))
    if staged:
        for place in y_ring:
            signal(relay.at[0], v, place, n)

    sends = []

    def send(src, dst, send_sem, recv_sem, where):
        copy = pltpu.make_async_remote_copy(
            src_ref=src,
            dst_ref=dst,
            send_sem=send_sem,
            recv_sem=recv_sem,
            device_id=where,
            device_id_type=MESH,
        )
        copy.start()
        sends.append(copy)
        return copy

    own_layers = pl.ds(2 * v, 2)
    there_row = pl.multiple_of(PAD - HALO + n * (CY + HALO), 8)
    for k in (0, 1):
        for direction, side in ((0, right), (1, left)):
            send(
                strip.at[k],
                got_strip.at[direction, v],
                s_send.at[6 + 2 * direction + k],
                s_recv.at[6 + 2 * direction + v],
                device(k, side, n),
            )
    send(
        fv.at[other_v],
        f.at[0, own_layers, pl.ds(PAD, CY), :],
        s_send.at[0],
        s_recv.at[0],
        device(other_v, w, n),
    )
    own_block = c.at[0, own_layers, pl.ds(PAD, CY), :]
    send(own_block, own_block, s_send.at[1], s_recv.at[1], device(other_v, w, n))
    for k in (0, 1):
        send(
            fv.at[k, :, pl.ds(edge_row, 8), :],
            f.at[0, own_layers, pl.ds(there_row, 8), :],
            s_send.at[2 + k],
            s_recv.at[2 + v],
            device(k, w, other_n),
        )
        send(
            c.at[0, own_layers, pl.ds(pl.multiple_of(PAD + edge_row, 8), 8), :],
            c.at[0, own_layers, pl.ds(there_row, 8), :],
            s_send.at[4 + k],
            s_recv.at[4 + v],
            device(k, w, other_n),
        )
        for direction, side in ((0, right), (1, left)):
            send(
                corner.at[k],
                got_corner.at[direction, v],
                s_send.at[10 + 2 * direction + k],
                s_recv.at[10 + 2 * direction + v],
                device(k, side, other_n),
            )

    def start_op(s, carry):
        op_chunk(s).start()
        return carry

    lax.fori_loop(0, BY, start_op, 0)
    if staged:
        pl.semaphore_wait(relay.at[0], QUAD - 1)
        for wide, narrow in ((opposite, n), (opposite, other_n), (w, other_n)):
            signal(relay.at[1], v, wide, narrow)

    def wait_bytes(ref, sem):
        pltpu.make_async_copy(ref, ref, sem).wait()

    has_left = w > 0
    has_right = w < wide_count - 1
    for direction in (0, 1):
        for vol in (0, 1):
            wait_bytes(got_strip.at[direction, vol], s_recv.at[6 + 2 * direction + vol])
            wait_bytes(got_corner.at[direction, vol], s_recv.at[10 + 2 * direction + vol])
    keep_left = jnp.where(has_left, 1.0, 0.0)
    keep_right = jnp.where(has_right, 1.0, 0.0)
    for z in range(NZ):
        vol = z // 2
        from_left = lax.rem(lane, SLOT) < 4
        merged = jnp.where(
            from_left, got_strip[0, vol] * keep_left, got_strip[1, vol] * keep_right
        )
        from_left8 = lax.rem(lane8, SLOT) < 4
        merged8 = jnp.where(
            from_left8, got_corner[0, vol] * keep_left, got_corner[1, vol] * keep_right
        )
        for which, ref in ((0, f), (2, c)):
            field = which + z % 2
            for group in range(GROUPS):
                at = group * 4 * SLOT + field * SLOT
                x = pltpu.roll(merged, (CX - 4 - at) % CX, 1)
                x = jnp.where((lane < 4) | (lane >= CX - 4), x, 0.0)
                ref[1, z, pl.ds(PAD + group * GROUP_ROWS, GROUP_ROWS), :] = x
            at = field * SLOT
            x = pltpu.roll(merged8, (CX - 4 - at) % CX, 1)
            x = jnp.where((lane8 < 4) | (lane8 >= CX - 4), x, 0.0)
            ref[1, z, pl.ds(inside, 8), :] = x
    load_own.wait()
    wait_bytes(f.at[0, pl.ds(2 * other_v, 2), pl.ds(PAD, CY), :], s_recv.at[0])
    wait_bytes(c.at[0, pl.ds(2 * other_v, 2), pl.ds(PAD, CY), :], s_recv.at[1])
    for vol in (0, 1):
        wait_bytes(f.at[0, pl.ds(2 * vol, 2), pl.ds(inside, 8), :], s_recv.at[2 + vol])
        wait_bytes(c.at[0, pl.ds(2 * vol, 2), pl.ds(inside, 8), :], s_recv.at[4 + vol])

    lane_c = lax.broadcasted_iota(jnp.int32, (CHUNK, CX), 1)
    first = lane_c == 0
    final = lane_c == CX - 1

    def box(ref, r, layers, tiles):
        inner = range(max(layers[0] - 1, 0), min(layers[-1] + 2, NZ))
        sums = []
        for t in (0, 1):
            y = {
                z: ref[t, z, pl.ds(r - 1, CHUNK), :]
                + ref[t, z, pl.ds(r, CHUNK), :]
                + ref[t, z, pl.ds(r + 1, CHUNK), :]
                for z in inner
            }
            low = y[0] + y[1] if 0 in layers or 1 in layers else None
            high = y[2] + y[3] if 2 in layers or 3 in layers else None
            made = {}
            for z in layers:
                made[z] = (
                    low if z == 0 else high if z == 3 else low + y[2] if z == 1 else y[1] + high
                )
            sums.append(made)
        result = ({}, {})
        for z in layers:
            center, side = sums[0][z], sums[1][z]
            center_up, side_up = pltpu.roll(center, 1, 1), pltpu.roll(side, 1, 1)
            center_down, side_down = (
                pltpu.roll(center, CX - 1, 1),
                pltpu.roll(side, CX - 1, 1),
            )
            result[0][z] = (
                center
                + jnp.where(first, side_up, center_up)
                + jnp.where(final, side_down, center_down)
            )
            if 1 in tiles:
                result[1][z] = (
                    side
                    + jnp.where(first, center_up, side_up)
                    + jnp.where(final, center_down, side_down)
                )
        return result

    def rows_of(i):
        return pl.multiple_of(PAD - HALO + i * CHUNK, 8)

    both = (0, 1)

    def first_sweep(i, layers):
        r = rows_of(i)
        sums = box(c, r, layers, both)
        for t in both:
            for z in layers:
                at = (t, z, pl.ds(r, CHUNK), slice(None))
                cond = c[at]
                diagonal = 38.5 * cond + 0.5 * sums[t][z]
                inverse = jnp.where(cond > 0.0, 1.0 / diagonal, 0.0)
                inv[at] = inverse
                u = gain0 * f[at] * inverse
                pa[at] = u
                qa[at] = cond * u

    def sweep(p, q, i, use, layers, tiles):
        r = rows_of(i)
        p_sums, q_sums = box(p, r, layers, tiles), box(q, r, layers, tiles)
        for t in tiles:
            for z in layers:
                at = (t, z, pl.ds(r, CHUNK), slice(None))
                cond = c[at]
                u = p[at]
                scaled = (
                    f[at] + 0.5 * (cond * p_sums[t][z] + q_sums[t][z]) - q[at]
                ) * inv[at] - u
                use(at, cond, u, scaled)

    def second_sweep(i, layers, tiles):
        def use(at, cond, u, scaled):
            u = (1.0 + keep1) * u + gain1 * scaled
            pb[at] = u
            qb[at] = cond * u

        sweep(pa, qa, i, use, layers, tiles)

    def third_sweep(i, layers):
        def use(at, cond, u, scaled):
            moved = gain0 * scaled
            u = u + moved
            m[at] = moved
            pa[at] = u
            qa[at] = cond * u

        sweep(pb, qb, i, use, layers, both)

    def fourth_sweep(i, layers):
        def use(at, cond, u, scaled):
            pb[at] = u + (keep1 * m[at] + gain1 * scaled)

        sweep(pa, qa, i, use, layers, (0,))

    def for_chunks(step):
        def body(i, carry):
            step(i)
            return carry

        lax.fori_loop(0, CHUNKS, body, 0, unroll=CHUNKS)

    my_columns = pl.ds(pl.multiple_of(w * CX, CX), CX)

    def share(block, numbers, narrows):
        def to(i, carry):
            j = 1 + lax.rem(i + wide_count // 2 - 1, wide_count - 1)
            for number, narrow in zip(numbers, narrows):
                pltpu.make_async_remote_copy(
                    src_ref=block,
                    dst_ref=block,
                    send_sem=g_send.at[number],
                    recv_sem=g_recv.at[number],
                    device_id=device(v, lax.rem(w + j, wide_count), narrow),
                    device_id_type=MESH,
                ).start()
            return carry

        lax.fori_loop(0, wide_count - 1, to, 0)
        if len(numbers) == 2:
            pltpu.make_async_remote_copy(
                src_ref=block,
                dst_ref=block,
                send_sem=g_send.at[numbers[1]],
                recv_sem=g_recv.at[numbers[1]],
                device_id=device(v, w, other_n),
                device_id_type=MESH,
            ).start()

    def trace():
        return pb[0, NZ - 1, pl.ds(PAD, BY, stride=CY // BY), :].astype(jnp.bfloat16)

    row16 = lax.broadcasted_iota(jnp.int32, (BY, CX), 0)

    def product(g, low, high):
        def add(s, total):
            block = opv[:, pl.ds(pl.multiple_of(s * span, span), span)]
            rows = lax.dot_general(
                g[...], block, (((1,), (1,)), ((), ())), preferred_element_type=jnp.float32
            )
            return total + jnp.where(row16 == s, rows, 0.0)

        total = lax.fori_loop(
            low, high, add, jnp.zeros((BY, CX), jnp.float32), unroll=5
        )
        return jnp.sum(total, axis=0, keepdims=True)

    def share_first():
        def to(i, carry):
            d = i // QUAD
            place = lax.rem(my_place + lax.rem(i, QUAD), QUAD)
            pltpu.make_async_remote_copy(
                src_ref=own_trace,
                dst_ref=g1.at[:, my_columns],
                send_sem=g_send.at[0],
                recv_sem=q_recv.at[d],
                device_id=device(v, quad_at(d, 1) * QUAD + place, n),
                device_id_type=MESH,
            ).start()
            return carry

        lax.fori_loop(1, wide_count, lambda i, carry: to(wide_count - i, carry), 0)
        pltpu.make_async_copy(own_trace, g1.at[:, my_columns], q_recv.at[0]).start()

    lanes = QUAD * CX

    def product_first():
        for s in range(BY):
            op_chunk(s).wait()

        def add(i, total):
            step = lax.rem(i, QUAD)
            d = i - step + step + step // 2 - 2 * (step // 3)
            if not staged:
                d = i
            wait_bytes(g1.at[:, 0:lanes], q_recv.at[d])
            first_lane = quad_at(d, -1) * lanes
            x = g1[:, pl.ds(pl.multiple_of(first_lane, lanes), lanes)]
            for s in range(BY):
                block = opv[:, pl.ds(pl.multiple_of(s * span + first_lane, lanes), lanes)]
                rows = lax.dot_general(
                    x, block, (((1,), (1,)), ((), ())), preferred_element_type=jnp.float32
                )
                total = total + jnp.where(row16 == s, rows, 0.0)
            return total

        total = lax.fori_loop(0, quads, add, jnp.zeros((BY, CX), jnp.float32))
        return jnp.sum(total, axis=0, keepdims=True)

    for_chunks(lambda i: first_sweep(i, (2, 3)))
    for_chunks(lambda i: second_sweep(i, (3,), (0,)))
    own_trace[...] = trace()
    if staged:
        pl.semaphore_wait(relay.at[1], 3)
    share_first()

    half = span // 2
    my_half = pl.ds(pl.multiple_of(v * half, half), half)
    their_half = pl.ds(pl.multiple_of(other_v * half, half), half)
    send(
        op.at[pl.ds(pl.multiple_of(other_n * RX, RX), RX), my_half],
        op_other.at[:, my_half],
        x_send.at[0],
        x_recv.at[0],
        device(v, w, other_n),
    )

    for_chunks(lambda i: first_sweep(i, (0, 1)))
    for_chunks(lambda i: second_sweep(i, (1, 2, 3), both))
    for_chunks(lambda i: third_sweep(i, (2, 3)))
    for_chunks(lambda i: fourth_sweep(i, (3,)))
    g2[:, my_columns] = trace()
    share(g2.at[:, my_columns], (1,), (n,))

    top = NZ - 1
    lane1 = lax.broadcasted_iota(jnp.int32, (8, CX), 1)

    def tile(ref, t, z, row):
        return ref[t, z, row : row + 8, :]

    def neighbours(ref, z, row):
        center, side = tile(ref, 0, z, row), tile(ref, 1, z, row)
        before = jnp.where(lane1 == 0, pltpu.roll(side, 1, 1), pltpu.roll(center, 1, 1))
        after = jnp.where(
            lane1 == CX - 1, pltpu.roll(side, CX - 1, 1), pltpu.roll(center, CX - 1, 1)
        )
        return before, after

    cond8, inverse8 = tile(c, 0, top, PAD), tile(inv, 0, top, PAD)
    cond_before, cond_after = neighbours(c, top, PAD)
    inverse_before, inverse_after = neighbours(inv, top, PAD)
    here8 = couple_gain * ((1.0 + keep1 - gain1) * gain0 + gain1) * inverse8
    beside = 0.5 * couple_gain * gain1 * gain0 * inverse8
    before8 = beside * (cond8 + cond_before) * inverse_before
    after8 = beside * (cond8 + cond_after) * inverse_after
    coef[n, 0:4, my_columns] = jnp.concatenate(
        [tile(pb, 0, top, PAD)[0:1], here8[0:1], before8[0:1], after8[0:1]], axis=0
    )
    share(coef.at[n, 0:4, my_columns], (2, 3), (n, other_n))

    part[n, 0:1, my_columns] = product_first()
    share(part.at[n, 0:1, my_columns], (4, 5), (n, other_n))

    wait_bytes(op_other.at[:, my_half], x_recv.at[0])
    send(
        op_other.at[:, my_half],
        op_other.at[:, my_half],
        x_send.at[1],
        x_recv.at[1],
        device(other_v, w, n),
    )
    wait_bytes(g2.at[:, CX:], g_recv.at[1])
    part2_own[...] = jnp.broadcast_to(product(g2, 1, BY), (8, CX))
    send(part2_own, part2_got, x_send.at[2], x_recv.at[2], device(v, w, other_n))
    for_chunks(lambda i: second_sweep(i, (0,), both))
    for_chunks(lambda i: third_sweep(i, (0, 1)))
    for_chunks(lambda i: fourth_sweep(i, (0, 1, 2)))

    def store_rows(number, y, count):
        here = out_p.at[v, :, pl.ds(y, count), :]
        own = pltpu.make_async_copy(
            pb.at[0, own_layers, pl.ds(PAD + y, count), :], here, o_local.at[number]
        )
        own.start()
        send(
            pb.at[0, pl.ds(2 * other_v, 2), pl.ds(PAD + y, count), :],
            here,
            o_send.at[number],
            o_recv.at[number],
            device(other_v, w, n),
        )
        return own

    stores = [store_rows(0, 8, CY - 16)]

    wait_bytes(coef.at[0, 0:4, CX:], g_recv.at[2])
    wait_bytes(coef.at[0, 0:4, :], g_recv.at[3])
    wait_bytes(op_other.at[:, their_half], x_recv.at[1])
    wait_bytes(part2_got, x_recv.at[2])
    part2 = part2_own[...] + part2_got[...]
    is_first = n == 0
    part2 = jnp.where(is_first, part2, pltpu.roll(part2, CX - RX, 1))

    wait_bytes(part.at[0, 0:1, CX:], g_recv.at[4])
    wait_bytes(part.at[0, 0:1, :], g_recv.at[5])
    total[0:1, :] = part[0, 0:1, :] + part[1, 0:1, :]

    row8 = lax.broadcasted_iota(jnp.int32, (8, CX), 0)
    here = jnp.broadcast_to(total[0:1, my_columns], (8, CX))
    beyond = jnp.broadcast_to(
        total[0:1, pl.ds(pl.multiple_of(right * CX, CX), CX)], (8, CX)
    )
    here_high, beyond_high = pltpu.roll(here, CX - RX, 1), pltpu.roll(beyond, CX - RX, 1)

    def source_rows(low, high, width):
        return jnp.where(lane8 < width, couple_gain * jnp.where(is_first, low, high), 0.0)

    delta_own = source_rows(here, here_high, RX)
    delta_side = source_rows(beyond, beyond_high, 1)
    below = jnp.where(is_first, 1.0, 0.0)
    delta_below = below * source_rows(here_high, here_high, RX)
    delta_below_side = below * source_rows(beyond_high, beyond_high, 1)

    def x_sum(center, side):
        return (
            center
            + pltpu.roll(center, 1, 1)
            + jnp.where(
                lane8 == CX - 1, pltpu.roll(side, CX - 1, 1), pltpu.roll(center, CX - 1, 1)
            )
        )

    def added(delta, side, row, tile_row, near, at_target):
        def spread_row(ref, t):
            return jnp.broadcast_to(ref[t, top, row : row + 1, :], (8, CX))

        q_center = gain0 * delta * spread_row(inv, 0)
        q_side = gain0 * side * spread_row(inv, 1)
        s_q = jnp.where(near, x_sum(q_center, q_side), 0.0)
        s_cq = jnp.where(
            near, x_sum(spread_row(c, 0) * q_center, spread_row(c, 1) * q_side), 0.0
        )
        for z in (top - 1, top):
            rows = pl.ds(tile_row, 8)
            cond = c[0, z, rows, :]
            inverse = inv[0, z, rows, :]
            change = gain1 * 0.5 * (cond * s_q + s_cq) * inverse
            if z == top and at_target is not None:
                q = jnp.where(at_target, q_center, 0.0)
                source = jnp.where(at_target, delta, 0.0)
                change = (
                    change
                    + (1.0 + keep1) * q
                    + gain1 * ((source - cond * q) * inverse - q)
                )
            pb[0, z, rows, :] = pb[0, z, rows, :] + change

    added(delta_own, delta_side, PAD, PAD, row8 <= 1, row8 == 0)
    added(delta_below, delta_below_side, PAD + CY, PAD + CY - 8, row8 == 7, None)
    stores.append(store_rows(1, 0, 8))
    stores.append(store_rows(2, CY - 8, 8))

    lane_all = lax.broadcasted_iota(jnp.int32, (1, span), 1)
    at_targets = lax.rem(lane_all, CX) < RX
    traction = total[0:1, :]
    rows = []
    for half_n in (0, 1):
        value = traction if half_n == 0 else pltpu.roll(traction, span - RX, 1)
        value = jnp.where(at_targets, value, 0.0)
        rows.append(
            coef[half_n, 0:1, :]
            + coef[half_n, 1:2, :] * value
            + coef[half_n, 2:3, :] * pltpu.roll(value, 1, 1)
            + coef[half_n, 3:4, :] * pltpu.roll(value, span - 1, 1)
        )
    own_row = jnp.where(is_first, rows[0], rows[1]).astype(jnp.bfloat16)
    other_row = jnp.where(is_first, rows[1], rows[0]).astype(jnp.bfloat16)

    def against(block, row):
        return lax.dot_general(
            jnp.broadcast_to(row, (BY, span)),
            block,
            (((1,), (1,)), ((), ())),
            preferred_element_type=jnp.float32,
        )

    mine = opv[pl.ds(pl.multiple_of(n * RX, RX), RX), 0:span]
    last = against(mine, own_row) + against(op_other[...], other_row)
    row_t[...] = part2[0:1, 0:RX] + last[0:1, :]
    store_t = pltpu.make_async_copy(row_t, out_t, o_local.at[3])
    store_t.start()
    stores.append(store_t)

    for own in stores:
        own.wait()
    for number, (y, count) in enumerate(((8, CY - 16), (0, 8), (CY - 8, 8))):
        wait_bytes(out_p.at[other_v, :, pl.ds(y, count), :], o_recv.at[number])
    for copy in sends:
        copy.wait_send()
    for number, g in enumerate((g1, g2)):
        wait_bytes(g.at[:, CX:], g_send.at[number])
    for number, ref, count in ((2, coef, 4), (4, part, 1)):
        wait_bytes(ref.at[0, 0:count, CX:], g_send.at[number])
        wait_bytes(ref.at[0, 0:count, :], g_send.at[number + 1])


def hand_over(pressure, traction, out_p, out_t, held_p, held_t, sem_in, sem_out):
    parts = [(pressure.at[k, z], held_p.at[k, z], out_p.at[k, z]) for k in (0, 1) for z in (0, 1)]
    parts.append((traction, held_t, out_t))
    loads = [
        pltpu.make_async_copy(src, held, sem_in.at[i]) for i, (src, held, _) in enumerate(parts)
    ]
    stores = [
        pltpu.make_async_copy(held, dst, sem_out.at[i]) for i, (_, held, dst) in enumerate(parts)
    ]
    for load in loads:
        load.start()
    for load, store in zip(loads, stores):
        load.wait()
        store.start()
    for store in stores:
        store.wait()


def local(forcing, material_ids, materials, boundary_operator):
    wide_count = lax.axis_size("wide")
    field = pltpu.VMEM((2, NZ, ROWS_ALL, CX), jnp.float32)
    gathered = pltpu.VMEM((BY, wide_count * CX), jnp.bfloat16)
    dma = pltpu.SemaphoreType.DMA
    anywhere = pl.BlockSpec(memory_space=pl.ANY)
    rows = boundary_operator.shape[0]
    quads = wide_count // QUAD
    pressure, traction = pl.pallas_call(
        functools.partial(kernel, wide_count),
        out_shape=(
            jax.ShapeDtypeStruct(forcing.shape, jnp.float32),
            jax.ShapeDtypeStruct((1, RX), jnp.float32),
        ),
        in_specs=[
            anywhere,
            anywhere,
            pl.BlockSpec(memory_space=pltpu.SMEM),
            anywhere,
        ],
        out_specs=(anywhere, anywhere),
        scratch_shapes=[
            pltpu.VMEM(forcing.shape, jnp.float32),
            pltpu.VMEM(material_ids.shape, jnp.int32),
            field,
            field,
            field,
            field,
            field,
            field,
            field,
            field,
            pltpu.VMEM((2, GROUP_ROWS, CX), jnp.float32),
            pltpu.VMEM((2, 8, CX), jnp.float32),
            pltpu.VMEM((2, 2, GROUP_ROWS, CX), jnp.float32),
            pltpu.VMEM((2, 2, 8, CX), jnp.float32),
            pltpu.VMEM(boundary_operator.shape, jnp.bfloat16),
            pltpu.VMEM((BY, CX), jnp.bfloat16),
            gathered,
            gathered,
            pltpu.VMEM((2, 8, wide_count * CX), jnp.float32),
            pltpu.VMEM((8, wide_count * CX), jnp.float32),
            pltpu.VMEM((2, 8, wide_count * CX), jnp.float32),
            pltpu.VMEM((8, CX), jnp.float32),
            pltpu.VMEM((8, CX), jnp.float32),
            pltpu.VMEM((1, RX), jnp.float32),
            pltpu.VMEM((RX, wide_count * CX), jnp.bfloat16),
            dma((3,)),
            dma((BY,)),
            dma((14,)),
            dma((14,)),
            dma((6,)),
            dma((6,)),
            dma((3,)),
            dma((3,)),
            dma((3,)),
            dma((3,)),
            dma((4,)),
            dma((quads,)),
            pltpu.SemaphoreType.REGULAR((2,)),
        ],
        compiler_params=pltpu.CompilerParams(
            collective_id=0, has_side_effects=True, vmem_limit_bytes=62 * 1024 * 1024
        ),
        cost_estimate=pl.CostEstimate(
            flops=4 * rows * boundary_operator.shape[1],
            bytes_accessed=2 * rows * boundary_operator.shape[1],
            transcendentals=0,
        ),
    )(forcing, material_ids, materials, boundary_operator)
    pressure, traction = pl.pallas_call(
        hand_over,
        out_shape=(
            jax.ShapeDtypeStruct(pressure.shape, jnp.float32),
            jax.ShapeDtypeStruct(traction.shape, jnp.float32),
        ),
        in_specs=[anywhere, anywhere],
        out_specs=(anywhere, anywhere),
        scratch_shapes=[
            pltpu.VMEM(pressure.shape, jnp.float32),
            pltpu.VMEM(traction.shape, jnp.float32),
            dma((5,)),
            dma((5,)),
        ],
    )(pressure, traction)
    return pressure, traction.reshape(RX, 1)


def solution(mesh):
    placed = (
        P(None, "vol", "narrow", "wide"),
        P("vol", "narrow", "wide"),
        P(),
        P("wide", "narrow"),
    )
    return jax.shard_map(
        local,
        mesh=mesh,
        in_specs=placed,
        out_specs=(P(None, "vol", "narrow", "wide"), P(("wide", "narrow"), "vol")),
        check_vma=False,
    )
```

```python
import functools

import jax
import jax.numpy as jnp
from jax import lax
from jax.experimental import pallas as pl
from jax.experimental.pallas import tpu as pltpu
from jax.sharding import PartitionSpec as P

MESH = pl.DeviceIdType.MESH

BY = 16
RX = 64
MAT = 8

lower_edge = 0.25
upper_edge = 1.75
couple_gain = 40.0

middle = (upper_edge + lower_edge) / 2.0
spread = (upper_edge - lower_edge) / 2.0
center_ratio = middle / spread
ratio_0 = 1.0 / center_ratio
ratio_1 = 1.0 / (2.0 * center_ratio - ratio_0)
gain0 = 1.0 / middle
keep1 = ratio_1 * ratio_0
gain1 = 2.0 * ratio_1 / spread

CY = 192
CX = 128
NZ = 4
PAD = 16
ROWS_ALL = PAD + CY + PAD
HALO = 8
CHUNK = 16
CHUNKS = (CY + 2 * HALO) // CHUNK
SLOT = 8
GROUPS = 4
GROUP_ROWS = CY // GROUPS
QUAD = 4


def select_materials(ids, materials):
    value = jnp.full(ids.shape, materials[0], jnp.float32)
    for number in range(1, MAT):
        value = jnp.where(ids == number, materials[number], value)
    return value


def kernel(
    wide_count,
    forcing,
    ids,
    materials,
    op,
    out_p,
    out_t,
    fv,
    iv,
    f,
    c,
    inv,
    m,
    pa,
    qa,
    pb,
    qb,
    strip,
    corner,
    got_strip,
    got_corner,
    opv,
    own_trace,
    g1,
    g2,
    part,
    total,
    coef,
    part2_own,
    part2_got,
    swap,
    row_t,
    op_mine,
    op_other,
    local_sem,
    op_sem,
    s_send,
    s_recv,
    g_send,
    g_recv,
    x_send,
    x_recv,
    o_send,
    o_recv,
    o_local,
    q_recv,
    relay,
    pair_send,
):
    v = lax.axis_index("vol")
    w = lax.axis_index("wide")
    n = lax.axis_index("narrow")
    other_v = 1 - v
    other_n = 1 - n
    right = lax.rem(w + 1, wide_count)
    left = lax.rem(w + wide_count - 1, wide_count)

    def device(vol, wide, narrow):
        return {"vol": vol, "wide": wide, "narrow": narrow}

    barrier = pltpu.get_barrier_semaphore()

    def signal(semaphore, vol, wide, narrow):
        pl.semaphore_signal(
            semaphore, inc=1, device_id=device(vol, wide, narrow), device_id_type=MESH
        )

    greeted = []

    def greet(vol, wide, narrow):
        signal(barrier, vol, wide, narrow)
        greeted.append(0)

    for narrow in (n, other_n):
        for side in (left, w, right):
            greet(other_v, side, narrow)
        for side in (left, right):
            greet(v, side, narrow)
    greet(v, w, other_n)

    half_count = wide_count // 2
    my_quad, my_place = w // QUAD, lax.rem(w, QUAD)
    my_high, my_low = my_quad // QUAD, lax.rem(my_quad, QUAD)

    def quad_at(d):
        high = lax.rem(my_high + d // QUAD, 2)
        low = lax.rem(my_low + lax.rem(d, QUAD), QUAD)
        return high * QUAD + low

    y_ring = [my_quad * QUAD + lax.rem(my_place + j, QUAD) for j in range(1, QUAD)]
    x_ring = [quad_at(j) * QUAD + my_place for j in range(1, QUAD)]
    opposite = lax.rem(w + half_count, wide_count)
    for vol in (v, other_v):
        for wide in y_ring + x_ring:
            greet(vol, wide, n)
        greet(vol, opposite, n)
        greet(vol, opposite, other_n)

    load_ids = pltpu.make_async_copy(ids, iv, local_sem.at[0])
    load_f = pltpu.make_async_copy(forcing, fv, local_sem.at[1])
    load_own = pltpu.make_async_copy(
        forcing.at[v], f.at[0, pl.ds(2 * v, 2), pl.ds(PAD, CY), :], local_sem.at[2]
    )
    load_ids.start()
    load_f.start()
    load_own.start()

    zeros8 = jnp.zeros((8, CX), jnp.float32)
    for ref in (c, pa, qa, pb, qb):
        for t in (0, 1):
            for z in range(NZ):
                ref[t, z, 0:8, :] = zeros8
                ref[t, z, ROWS_ALL - 8 : ROWS_ALL, :] = zeros8
    outside = pl.multiple_of(PAD - HALO + other_n * 0 + n * (CY + HALO), 8)
    inside = pl.multiple_of(PAD - HALO + other_n * (CY + HALO), 8)
    for ref in (f, c):
        for t in (0, 1):
            for z in range(NZ):
                ref[t, z, pl.ds(outside, 8), :] = zeros8

    load_ids.wait()
    for layer in (0, 1):
        c[0, 2 * v + layer, PAD : PAD + CY, :] = select_materials(iv[layer], materials)
    load_f.wait()

    span = wide_count * CX

    half = span // 2

    def op_chunk(s):
        return pltpu.make_async_copy(
            op.at[:, pl.ds(pl.multiple_of(s * span + v * half, half), half)],
            opv.at[:, pl.ds(pl.multiple_of(s * half, half), half)],
            op_sem.at[s],
        )

    load_mine = pltpu.make_async_copy(
        op.at[pl.ds(pl.multiple_of(n * RX, RX), RX), 0:span], op_mine, local_sem.at[3]
    )

    edge_row = pl.multiple_of(other_n * (CY - 8), 8)
    lane = lax.broadcasted_iota(jnp.int32, (GROUP_ROWS, CX), 1)
    lane8 = lax.broadcasted_iota(jnp.int32, (8, CX), 1)
    for k in (0, 1):
        packed = jnp.zeros((GROUP_ROWS, CX), jnp.float32)
        edge = jnp.zeros((8, CX), jnp.float32)
        for field in range(4):
            for group in range(GROUPS):
                rows = pl.ds(group * GROUP_ROWS, GROUP_ROWS)
                if field < 2:
                    x = fv[k, field, rows, :]
                else:
                    x = c[0, 2 * v + field - 2, pl.ds(PAD + group * GROUP_ROWS, GROUP_ROWS), :]
                at = group * 4 * SLOT + field * SLOT
                x = pltpu.roll(x, (at + 4) % CX, 1)
                packed = jnp.where((lane >= at) & (lane < at + SLOT), x, packed)
            if field < 2:
                x = fv[k, field, pl.ds(edge_row, 8), :]
            else:
                x = c[0, 2 * v + field - 2, pl.ds(PAD + edge_row, 8), :]
            at = field * SLOT
            x = pltpu.roll(x, at + 4, 1)
            edge = jnp.where((lane8 >= at) & (lane8 < at + SLOT), x, edge)
        strip[k] = packed
        corner[k] = edge

    pl.semaphore_wait(barrier, len(greeted))
    for wide in y_ring:
        signal(relay.at[0], v, wide, n)

    sends = []

    def send(src, dst, send_sem, recv_sem, where):
        copy = pltpu.make_async_remote_copy(
            src_ref=src,
            dst_ref=dst,
            send_sem=send_sem,
            recv_sem=recv_sem,
            device_id=where,
            device_id_type=MESH,
        )
        copy.start()
        sends.append(copy)
        return copy

    own_layers = pl.ds(2 * v, 2)
    there_row = pl.multiple_of(PAD - HALO + n * (CY + HALO), 8)
    for k in (0, 1):
        for direction, side in ((0, right), (1, left)):
            send(
                strip.at[k],
                got_strip.at[direction, v],
                s_send.at[6 + 2 * direction + k],
                s_recv.at[6 + 2 * direction + v],
                device(k, side, n),
            )
    send(
        fv.at[other_v],
        f.at[0, own_layers, pl.ds(PAD, CY), :],
        s_send.at[0],
        s_recv.at[0],
        device(other_v, w, n),
    )
    own_block = c.at[0, own_layers, pl.ds(PAD, CY), :]
    send(own_block, own_block, s_send.at[1], s_recv.at[1], device(other_v, w, n))
    for k in (0, 1):
        send(
            fv.at[k, :, pl.ds(edge_row, 8), :],
            f.at[0, own_layers, pl.ds(there_row, 8), :],
            s_send.at[2 + k],
            s_recv.at[2 + v],
            device(k, w, other_n),
        )
        send(
            c.at[0, own_layers, pl.ds(pl.multiple_of(PAD + edge_row, 8), 8), :],
            c.at[0, own_layers, pl.ds(there_row, 8), :],
            s_send.at[4 + k],
            s_recv.at[4 + v],
            device(k, w, other_n),
        )
        for direction, side in ((0, right), (1, left)):
            send(
                corner.at[k],
                got_corner.at[direction, v],
                s_send.at[10 + 2 * direction + k],
                s_recv.at[10 + 2 * direction + v],
                device(k, side, other_n),
            )

    def start_op(s, carry):
        op_chunk(s).start()
        return carry

    lax.fori_loop(0, BY, start_op, 0)
    load_mine.start()
    pl.semaphore_wait(relay.at[0], QUAD - 1)
    for wide, narrow in ((opposite, n), (opposite, other_n), (w, other_n)):
        signal(relay.at[1], v, wide, narrow)

    def wait_bytes(ref, sem):
        pltpu.make_async_copy(ref, ref, sem).wait()

    has_left = w > 0
    has_right = w < wide_count - 1
    for direction in (0, 1):
        for vol in (0, 1):
            wait_bytes(got_strip.at[direction, vol], s_recv.at[6 + 2 * direction + vol])
            wait_bytes(got_corner.at[direction, vol], s_recv.at[10 + 2 * direction + vol])
    keep_left = jnp.where(has_left, 1.0, 0.0)
    keep_right = jnp.where(has_right, 1.0, 0.0)
    for z in range(NZ):
        vol = z // 2
        from_left = lax.rem(lane, SLOT) < 4
        merged = jnp.where(
            from_left, got_strip[0, vol] * keep_left, got_strip[1, vol] * keep_right
        )
        from_left8 = lax.rem(lane8, SLOT) < 4
        merged8 = jnp.where(
            from_left8, got_corner[0, vol] * keep_left, got_corner[1, vol] * keep_right
        )
        for which, ref in ((0, f), (2, c)):
            field = which + z % 2
            for group in range(GROUPS):
                at = group * 4 * SLOT + field * SLOT
                x = pltpu.roll(merged, (CX - 4 - at) % CX, 1)
                x = jnp.where((lane < 4) | (lane >= CX - 4), x, 0.0)
                ref[1, z, pl.ds(PAD + group * GROUP_ROWS, GROUP_ROWS), :] = x
            at = field * SLOT
            x = pltpu.roll(merged8, (CX - 4 - at) % CX, 1)
            x = jnp.where((lane8 < 4) | (lane8 >= CX - 4), x, 0.0)
            ref[1, z, pl.ds(inside, 8), :] = x
    load_own.wait()
    wait_bytes(f.at[0, pl.ds(2 * other_v, 2), pl.ds(PAD, CY), :], s_recv.at[0])
    wait_bytes(c.at[0, pl.ds(2 * other_v, 2), pl.ds(PAD, CY), :], s_recv.at[1])
    for vol in (0, 1):
        wait_bytes(f.at[0, pl.ds(2 * vol, 2), pl.ds(inside, 8), :], s_recv.at[2 + vol])
        wait_bytes(c.at[0, pl.ds(2 * vol, 2), pl.ds(inside, 8), :], s_recv.at[4 + vol])

    lane_c = lax.broadcasted_iota(jnp.int32, (CHUNK, CX), 1)
    first = lane_c == 0
    final = lane_c == CX - 1

    def box(ref, r, layers, tiles):
        inner = range(max(layers[0] - 1, 0), min(layers[-1] + 2, NZ))
        sums = []
        for t in (0, 1):
            y = {
                z: ref[t, z, pl.ds(r - 1, CHUNK), :]
                + ref[t, z, pl.ds(r, CHUNK), :]
                + ref[t, z, pl.ds(r + 1, CHUNK), :]
                for z in inner
            }
            low = y[0] + y[1] if 0 in layers or 1 in layers else None
            high = y[2] + y[3] if 2 in layers or 3 in layers else None
            made = {}
            for z in layers:
                made[z] = (
                    low if z == 0 else high if z == 3 else low + y[2] if z == 1 else y[1] + high
                )
            sums.append(made)
        result = ({}, {})
        for z in layers:
            center, side = sums[0][z], sums[1][z]
            center_up, side_up = pltpu.roll(center, 1, 1), pltpu.roll(side, 1, 1)
            center_down, side_down = (
                pltpu.roll(center, CX - 1, 1),
                pltpu.roll(side, CX - 1, 1),
            )
            result[0][z] = (
                center
                + jnp.where(first, side_up, center_up)
                + jnp.where(final, side_down, center_down)
            )
            if 1 in tiles:
                result[1][z] = (
                    side
                    + jnp.where(first, center_up, side_up)
                    + jnp.where(final, center_down, side_down)
                )
        return result

    def rows_of(i):
        return pl.multiple_of(PAD - HALO + i * CHUNK, 8)

    both = (0, 1)

    def first_sweep(i, layers):
        r = rows_of(i)
        sums = box(c, r, layers, both)
        for t in both:
            for z in layers:
                at = (t, z, pl.ds(r, CHUNK), slice(None))
                cond = c[at]
                diagonal = 38.5 * cond + 0.5 * sums[t][z]
                inverse = jnp.where(cond > 0.0, 1.0 / diagonal, 0.0)
                inv[at] = inverse
                u = gain0 * f[at] * inverse
                pa[at] = u
                qa[at] = cond * u

    def sweep(p, q, i, use, layers, tiles):
        r = rows_of(i)
        p_sums, q_sums = box(p, r, layers, tiles), box(q, r, layers, tiles)
        for t in tiles:
            for z in layers:
                at = (t, z, pl.ds(r, CHUNK), slice(None))
                cond = c[at]
                u = p[at]
                scaled = (
                    f[at] + 0.5 * (cond * p_sums[t][z] + q_sums[t][z]) - q[at]
                ) * inv[at] - u
                use(at, cond, u, scaled)

    def second_sweep(i, layers, tiles):
        def use(at, cond, u, scaled):
            u = (1.0 + keep1) * u + gain1 * scaled
            pb[at] = u
            qb[at] = cond * u

        sweep(pa, qa, i, use, layers, tiles)

    def third_sweep(i, layers):
        def use(at, cond, u, scaled):
            moved = gain0 * scaled
            u = u + moved
            m[at] = moved
            pa[at] = u
            qa[at] = cond * u

        sweep(pb, qb, i, use, layers, both)

    def fourth_sweep(i, layers):
        def use(at, cond, u, scaled):
            pb[at] = u + (keep1 * m[at] + gain1 * scaled)

        sweep(pa, qa, i, use, layers, (0,))

    def for_chunks(step):
        def body(i, carry):
            step(i)
            return carry

        lax.fori_loop(0, CHUNKS, body, 0, unroll=CHUNKS)

    my_columns = pl.ds(pl.multiple_of(w * CX, CX), CX)

    def share(block, numbers, narrows):
        def to(i, carry):
            j = 1 + lax.rem(i + wide_count // 2 - 1, wide_count - 1)
            for number, narrow in zip(numbers, narrows):
                pltpu.make_async_remote_copy(
                    src_ref=block,
                    dst_ref=block,
                    send_sem=g_send.at[number],
                    recv_sem=g_recv.at[number],
                    device_id=device(v, lax.rem(w + j, wide_count), narrow),
                    device_id_type=MESH,
                ).start()
            return carry

        lax.fori_loop(0, wide_count - 1, to, 0)
        if len(numbers) == 2:
            pltpu.make_async_remote_copy(
                src_ref=block,
                dst_ref=block,
                send_sem=g_send.at[numbers[1]],
                recv_sem=g_recv.at[numbers[1]],
                device_id=device(v, w, other_n),
                device_id_type=MESH,
            ).start()

    def trace():
        return pb[0, NZ - 1, pl.ds(PAD, BY, stride=CY // BY), :].astype(jnp.bfloat16)

    row_of = lax.rem(lax.broadcasted_iota(jnp.int32, (2 * BY, CX), 0), BY)

    owner = my_high
    elsewhere = owner != v
    half_columns = pl.ds(pl.multiple_of(lax.rem(w, half_count) * CX, CX), CX)

    def trace_copy(block, g, send_sem, recv_sem, wide):
        return pltpu.make_async_remote_copy(
            src_ref=block,
            dst_ref=g.at[v, :, half_columns],
            send_sem=send_sem,
            recv_sem=recv_sem,
            device_id=device(owner, wide, n),
            device_id_type=MESH,
        )

    def share_trace(block, g, number, recv_sem):
        def to(i, carry):
            i = wide_count - i
            place = lax.rem(my_place + lax.rem(i, QUAD), QUAD)
            wide = quad_at(i // QUAD) * QUAD + place
            trace_copy(block, g, g_send.at[number], recv_sem, wide).start()
            return carry

        lax.fori_loop(1, wide_count, to, 0)

        @pl.when(elsewhere)
        def _():
            trace_copy(block, g, pair_send.at[number], recv_sem, w).start()

        @pl.when(jnp.logical_not(elsewhere))
        def _():
            pltpu.make_async_copy(block, g.at[v, :, half_columns], recv_sem).start()

    lanes = QUAD * CX

    def against_quad(x, first_lane, total, first_row):
        for s in range(first_row, BY):
            block = opv[:, pl.ds(pl.multiple_of(s * half + first_lane, lanes), lanes)]
            rows = lax.dot_general(
                x, block, (((1,), (1,)), ((), ())), preferred_element_type=jnp.float32
            )
            total = total + jnp.where(row_of == s, rows, 0.0)
        return total

    def product(g, first_row, arriving):
        def add(i, total):
            low = lax.rem(my_low + i + i // 2 - 2 * (i // 3), QUAD)
            if arriving:
                wait_bytes(g.at[:, :, 0:lanes], q_recv.at[low])
            x = g[:, :, pl.ds(pl.multiple_of(low * lanes, lanes), lanes)]
            return against_quad(x.reshape(2 * BY, lanes), low * lanes, total, first_row)

        total = lax.fori_loop(0, QUAD, add, jnp.zeros((2 * BY, CX), jnp.float32))
        return [
            jnp.sum(total[k * BY : (k + 1) * BY], axis=0, keepdims=True) for k in (0, 1)
        ]

    is_low = v == 0

    def mine_and_theirs(parts):
        return (
            jnp.where(is_low, parts[0], parts[1]),
            jnp.where(is_low, parts[1], parts[0]),
        )

    for_chunks(lambda i: first_sweep(i, (2, 3)))
    for_chunks(lambda i: second_sweep(i, (3,), (0,)))
    own_trace[0] = trace()
    pl.semaphore_wait(relay.at[1], 3)
    share_trace(own_trace.at[0], g1, 0, q_recv.at[my_low])

    my_half = pl.ds(pl.multiple_of(v * half, half), half)
    their_half = pl.ds(pl.multiple_of(other_v * half, half), half)
    send(
        op.at[pl.ds(pl.multiple_of(other_n * RX, RX), RX), my_half],
        op_other.at[:, my_half],
        x_send.at[0],
        x_recv.at[0],
        device(v, w, other_n),
    )

    for_chunks(lambda i: first_sweep(i, (0, 1)))
    for_chunks(lambda i: second_sweep(i, (1, 2, 3), both))
    for_chunks(lambda i: third_sweep(i, (2, 3)))
    for_chunks(lambda i: fourth_sweep(i, (3,)))
    own_trace[1] = trace()
    share_trace(own_trace.at[1], g2, 1, g_recv.at[1])

    top = NZ - 1
    lane1 = lax.broadcasted_iota(jnp.int32, (8, CX), 1)

    def tile(ref, t, z, row):
        return ref[t, z, row : row + 8, :]

    def neighbours(ref, z, row):
        center, side = tile(ref, 0, z, row), tile(ref, 1, z, row)
        before = jnp.where(lane1 == 0, pltpu.roll(side, 1, 1), pltpu.roll(center, 1, 1))
        after = jnp.where(
            lane1 == CX - 1, pltpu.roll(side, CX - 1, 1), pltpu.roll(center, CX - 1, 1)
        )
        return before, after

    cond8, inverse8 = tile(c, 0, top, PAD), tile(inv, 0, top, PAD)
    cond_before, cond_after = neighbours(c, top, PAD)
    inverse_before, inverse_after = neighbours(inv, top, PAD)
    here8 = couple_gain * ((1.0 + keep1 - gain1) * gain0 + gain1) * inverse8
    beside = 0.5 * couple_gain * gain1 * gain0 * inverse8
    before8 = beside * (cond8 + cond_before) * inverse_before
    after8 = beside * (cond8 + cond_after) * inverse_after
    coef[n, 0:4, my_columns] = jnp.concatenate(
        [tile(pb, 0, top, PAD)[0:1], here8[0:1], before8[0:1], after8[0:1]], axis=0
    )
    share(coef.at[n, 0:4, my_columns], (2, 3), (n, other_n))

    for s in range(BY):
        op_chunk(s).wait()
    mine1, theirs1 = mine_and_theirs(product(g1, 0, True))
    swap[0] = jnp.broadcast_to(theirs1, (8, CX))
    send(swap.at[0], swap.at[1], x_send.at[3], x_recv.at[3], device(other_v, w, n))
    for_chunks(lambda i: second_sweep(i, (0,), both))
    for_chunks(lambda i: third_sweep(i, (0, 1)))
    wait_bytes(swap.at[1], x_recv.at[3])
    part[n, 0:1, my_columns] = mine1 + swap[1, 0:1, :]
    share(part.at[n, 0:1, my_columns], (4, 5), (n, other_n))

    wait_bytes(op_other.at[:, my_half], x_recv.at[0])
    send(
        op_other.at[:, my_half],
        op_other.at[:, my_half],
        x_send.at[1],
        x_recv.at[1],
        device(other_v, w, n),
    )
    wait_bytes(g2, g_recv.at[1])
    mine2, theirs2 = mine_and_theirs(product(g2, 1, False))
    part2_own[0] = jnp.broadcast_to(mine2, (8, CX))
    part2_own[1] = jnp.broadcast_to(theirs2, (8, CX))
    for number, (which, vol, narrow) in enumerate(
        ((0, v, other_n), (1, other_v, n), (1, other_v, other_n))
    ):
        send(
            part2_own.at[which],
            part2_got.at[number],
            x_send.at[4 + number],
            x_recv.at[4 + number],
            device(vol, w, narrow),
        )
    for_chunks(lambda i: fourth_sweep(i, (0, 1, 2)))

    def store_rows(number, y, count):
        here = out_p.at[v, :, pl.ds(y, count), :]
        own = pltpu.make_async_copy(
            pb.at[0, own_layers, pl.ds(PAD + y, count), :], here, o_local.at[number]
        )
        own.start()
        send(
            pb.at[0, pl.ds(2 * other_v, 2), pl.ds(PAD + y, count), :],
            here,
            o_send.at[number],
            o_recv.at[number],
            device(other_v, w, n),
        )
        return own

    stores = [store_rows(0, 8, CY - 16)]

    wait_bytes(coef.at[0, 0:4, CX:], g_recv.at[2])
    wait_bytes(coef.at[0, 0:4, :], g_recv.at[3])
    wait_bytes(op_other.at[:, their_half], x_recv.at[1])
    for number in range(3):
        wait_bytes(part2_got.at[number], x_recv.at[4 + number])
    part2 = part2_own[0] + part2_got[0] + part2_got[1] + part2_got[2]
    is_first = n == 0
    part2 = jnp.where(is_first, part2, pltpu.roll(part2, CX - RX, 1))

    wait_bytes(part.at[0, 0:1, CX:], g_recv.at[4])
    wait_bytes(part.at[0, 0:1, :], g_recv.at[5])
    total[0:1, :] = part[0, 0:1, :] + part[1, 0:1, :]

    row8 = lax.broadcasted_iota(jnp.int32, (8, CX), 0)
    here = jnp.broadcast_to(total[0:1, my_columns], (8, CX))
    beyond = jnp.broadcast_to(
        total[0:1, pl.ds(pl.multiple_of(right * CX, CX), CX)], (8, CX)
    )
    here_high, beyond_high = pltpu.roll(here, CX - RX, 1), pltpu.roll(beyond, CX - RX, 1)

    def source_rows(low, high, width):
        return jnp.where(lane8 < width, couple_gain * jnp.where(is_first, low, high), 0.0)

    delta_own = source_rows(here, here_high, RX)
    delta_side = source_rows(beyond, beyond_high, 1)
    below = jnp.where(is_first, 1.0, 0.0)
    delta_below = below * source_rows(here_high, here_high, RX)
    delta_below_side = below * source_rows(beyond_high, beyond_high, 1)

    def x_sum(center, side):
        return (
            center
            + pltpu.roll(center, 1, 1)
            + jnp.where(
                lane8 == CX - 1, pltpu.roll(side, CX - 1, 1), pltpu.roll(center, CX - 1, 1)
            )
        )

    def added(delta, side, row, tile_row, near, at_target):
        def spread_row(ref, t):
            return jnp.broadcast_to(ref[t, top, row : row + 1, :], (8, CX))

        q_center = gain0 * delta * spread_row(inv, 0)
        q_side = gain0 * side * spread_row(inv, 1)
        s_q = jnp.where(near, x_sum(q_center, q_side), 0.0)
        s_cq = jnp.where(
            near, x_sum(spread_row(c, 0) * q_center, spread_row(c, 1) * q_side), 0.0
        )
        for z in (top - 1, top):
            rows = pl.ds(tile_row, 8)
            cond = c[0, z, rows, :]
            inverse = inv[0, z, rows, :]
            change = gain1 * 0.5 * (cond * s_q + s_cq) * inverse
            if z == top and at_target is not None:
                q = jnp.where(at_target, q_center, 0.0)
                source = jnp.where(at_target, delta, 0.0)
                change = (
                    change
                    + (1.0 + keep1) * q
                    + gain1 * ((source - cond * q) * inverse - q)
                )
            pb[0, z, rows, :] = pb[0, z, rows, :] + change

    added(delta_own, delta_side, PAD, PAD, row8 <= 1, row8 == 0)
    added(delta_below, delta_below_side, PAD + CY, PAD + CY - 8, row8 == 7, None)
    stores.append(store_rows(1, 0, 8))
    stores.append(store_rows(2, CY - 8, 8))

    lane_all = lax.broadcasted_iota(jnp.int32, (1, span), 1)
    at_targets = lax.rem(lane_all, CX) < RX
    traction = total[0:1, :]
    rows = []
    for half_n in (0, 1):
        value = traction if half_n == 0 else pltpu.roll(traction, span - RX, 1)
        value = jnp.where(at_targets, value, 0.0)
        rows.append(
            coef[half_n, 0:1, :]
            + coef[half_n, 1:2, :] * value
            + coef[half_n, 2:3, :] * pltpu.roll(value, 1, 1)
            + coef[half_n, 3:4, :] * pltpu.roll(value, span - 1, 1)
        )
    own_row = jnp.where(is_first, rows[0], rows[1]).astype(jnp.bfloat16)
    other_row = jnp.where(is_first, rows[1], rows[0]).astype(jnp.bfloat16)

    def against(block, row):
        return lax.dot_general(
            jnp.broadcast_to(row, (BY, span)),
            block,
            (((1,), (1,)), ((), ())),
            preferred_element_type=jnp.float32,
        )

    load_mine.wait()
    last = against(op_mine[...], own_row) + against(op_other[...], other_row)
    row_t[...] = part2[0:1, 0:RX] + last[0:1, :]
    store_t = pltpu.make_async_copy(row_t, out_t, o_local.at[3])
    store_t.start()
    stores.append(store_t)

    for own in stores:
        own.wait()
    for number, (y, count) in enumerate(((8, CY - 16), (0, 8), (CY - 8, 8))):
        wait_bytes(out_p.at[other_v, :, pl.ds(y, count), :], o_recv.at[number])
    for copy in sends:
        copy.wait_send()
    for number, g in enumerate((g1, g2)):
        wait_bytes(g.at[0, :, 0 : (half_count - 1) * CX], g_send.at[number])
        wait_bytes(g.at[0], g_send.at[number])

        @pl.when(elsewhere)
        def _(number=number):
            wait_bytes(own_trace.at[number], pair_send.at[number])

    for number, ref, count in ((2, coef, 4), (4, part, 1)):
        wait_bytes(ref.at[0, 0:count, CX:], g_send.at[number])
        wait_bytes(ref.at[0, 0:count, :], g_send.at[number + 1])


def hand_over(pressure, traction, out_p, out_t, held_p, held_t, sem_in, sem_out):
    parts = [(pressure.at[k, z], held_p.at[k, z], out_p.at[k, z]) for k in (0, 1) for z in (0, 1)]
    parts.append((traction, held_t, out_t))
    loads = [
        pltpu.make_async_copy(src, held, sem_in.at[i]) for i, (src, held, _) in enumerate(parts)
    ]
    stores = [
        pltpu.make_async_copy(held, dst, sem_out.at[i]) for i, (_, held, dst) in enumerate(parts)
    ]
    for load in loads:
        load.start()
    for load, store in zip(loads, stores):
        load.wait()
        store.start()
    for store in stores:
        store.wait()


def local(forcing, material_ids, materials, boundary_operator):
    wide_count = lax.axis_size("wide")
    field = pltpu.VMEM((2, NZ, ROWS_ALL, CX), jnp.float32)
    gathered = pltpu.VMEM((2, BY, wide_count * CX // 2), jnp.bfloat16)
    dma = pltpu.SemaphoreType.DMA
    anywhere = pl.BlockSpec(memory_space=pl.ANY)
    rows = boundary_operator.shape[0]
    pressure, traction = pl.pallas_call(
        functools.partial(kernel, wide_count),
        out_shape=(
            jax.ShapeDtypeStruct(forcing.shape, jnp.float32),
            jax.ShapeDtypeStruct((1, RX), jnp.float32),
        ),
        in_specs=[
            anywhere,
            anywhere,
            pl.BlockSpec(memory_space=pltpu.SMEM),
            anywhere,
        ],
        out_specs=(anywhere, anywhere),
        scratch_shapes=[
            pltpu.VMEM(forcing.shape, jnp.float32),
            pltpu.VMEM(material_ids.shape, jnp.int32),
            field,
            field,
            field,
            field,
            field,
            field,
            field,
            field,
            pltpu.VMEM((2, GROUP_ROWS, CX), jnp.float32),
            pltpu.VMEM((2, 8, CX), jnp.float32),
            pltpu.VMEM((2, 2, GROUP_ROWS, CX), jnp.float32),
            pltpu.VMEM((2, 2, 8, CX), jnp.float32),
            pltpu.VMEM((rows, boundary_operator.shape[1] // 2), jnp.bfloat16),
            pltpu.VMEM((2, BY, CX), jnp.bfloat16),
            gathered,
            gathered,
            pltpu.VMEM((2, 8, wide_count * CX), jnp.float32),
            pltpu.VMEM((8, wide_count * CX), jnp.float32),
            pltpu.VMEM((2, 8, wide_count * CX), jnp.float32),
            pltpu.VMEM((2, 8, CX), jnp.float32),
            pltpu.VMEM((3, 8, CX), jnp.float32),
            pltpu.VMEM((2, 8, CX), jnp.float32),
            pltpu.VMEM((1, RX), jnp.float32),
            pltpu.VMEM((RX, wide_count * CX), jnp.bfloat16),
            pltpu.VMEM((RX, wide_count * CX), jnp.bfloat16),
            dma((4,)),
            dma((BY,)),
            dma((14,)),
            dma((14,)),
            dma((6,)),
            dma((6,)),
            dma((7,)),
            dma((7,)),
            dma((3,)),
            dma((3,)),
            dma((4,)),
            dma((QUAD,)),
            pltpu.SemaphoreType.REGULAR((2,)),
            dma((2,)),
        ],
        compiler_params=pltpu.CompilerParams(
            collective_id=0, has_side_effects=True, vmem_limit_bytes=62 * 1024 * 1024
        ),
        cost_estimate=pl.CostEstimate(
            flops=4 * rows * boundary_operator.shape[1],
            bytes_accessed=2 * rows * boundary_operator.shape[1],
            transcendentals=0,
        ),
    )(forcing, material_ids, materials, boundary_operator)
    pressure, traction = pl.pallas_call(
        hand_over,
        out_shape=(
            jax.ShapeDtypeStruct(pressure.shape, jnp.float32),
            jax.ShapeDtypeStruct(traction.shape, jnp.float32),
        ),
        in_specs=[anywhere, anywhere],
        out_specs=(anywhere, anywhere),
        scratch_shapes=[
            pltpu.VMEM(pressure.shape, jnp.float32),
            pltpu.VMEM(traction.shape, jnp.float32),
            dma((5,)),
            dma((5,)),
        ],
    )(pressure, traction)
    return pressure, traction.reshape(RX, 1)


def solution(mesh):
    placed = (
        P(None, "vol", "narrow", "wide"),
        P("vol", "narrow", "wide"),
        P(),
        P("wide", "narrow"),
    )
    return jax.shard_map(
        local,
        mesh=mesh,
        in_specs=placed,
        out_specs=(P(None, "vol", "narrow", "wide"), P(("wide", "narrow"), "vol")),
        check_vma=False,
    )
```

```python
import functools

import jax
import jax.numpy as jnp
from jax import lax
from jax.experimental import pallas as pl
from jax.experimental.pallas import tpu as pltpu
from jax.sharding import PartitionSpec as P

MESH = pl.DeviceIdType.MESH

BY = 16
RX = 64
MAT = 8

lower_edge = 0.25
upper_edge = 1.75
couple_gain = 40.0

middle = (upper_edge + lower_edge) / 2.0
spread = (upper_edge - lower_edge) / 2.0
center_ratio = middle / spread
ratio_0 = 1.0 / center_ratio
ratio_1 = 1.0 / (2.0 * center_ratio - ratio_0)
gain0 = 1.0 / middle
keep1 = ratio_1 * ratio_0
gain1 = 2.0 * ratio_1 / spread

CY = 192
CX = 128
NZ = 4
PAD = 16
ROWS_ALL = PAD + CY + PAD
HALO = 8
CHUNK = 16
CHUNKS = (CY + 2 * HALO) // CHUNK
SLOT = 8
GROUPS = 4
GROUP_ROWS = CY // GROUPS
QUAD = 4


def select_materials(ids, materials):
    value = jnp.full(ids.shape, materials[0], jnp.float32)
    for number in range(1, MAT):
        value = jnp.where(ids == number, materials[number], value)
    return value


def kernel(
    wide_count,
    forcing,
    ids,
    materials,
    op,
    out_p,
    out_t,
    fv,
    iv,
    f,
    c,
    inv,
    m,
    pa,
    qa,
    pb,
    qb,
    strip,
    corner,
    got_strip,
    got_corner,
    opv,
    own_trace,
    g1,
    g2,
    part,
    total,
    coef,
    part2_own,
    part2_got,
    swap,
    row_t,
    op_mine,
    op_other,
    local_sem,
    op_sem,
    s_send,
    s_recv,
    g_send,
    g_recv,
    x_send,
    x_recv,
    o_send,
    o_recv,
    o_local,
    q_recv,
    relay,
    pair_send,
):
    v = lax.axis_index("vol")
    w = lax.axis_index("wide")
    n = lax.axis_index("narrow")
    other_v = 1 - v
    other_n = 1 - n
    right = lax.rem(w + 1, wide_count)
    left = lax.rem(w + wide_count - 1, wide_count)

    def device(vol, wide, narrow):
        return {"vol": vol, "wide": wide, "narrow": narrow}

    barrier = pltpu.get_barrier_semaphore()

    def signal(semaphore, vol, wide, narrow):
        pl.semaphore_signal(
            semaphore, inc=1, device_id=device(vol, wide, narrow), device_id_type=MESH
        )

    greeted = []

    def greet(vol, wide, narrow):
        signal(barrier, vol, wide, narrow)
        greeted.append(0)

    has_left = w > 0
    has_right = w < wide_count - 1
    for has_side, side in ((has_left, left), (has_right, right)):

        @pl.when(has_side)
        def _(side=side):
            for vol in (v, other_v):
                for narrow in (n, other_n):
                    signal(barrier, vol, side, narrow)

    greet(other_v, w, n)
    greet(other_v, w, other_n)
    greet(v, w, other_n)

    half_count = wide_count // 2
    my_quad, my_place = w // QUAD, lax.rem(w, QUAD)
    my_high, my_low = my_quad // QUAD, lax.rem(my_quad, QUAD)

    def quad_at(d):
        high = lax.rem(my_high + d // QUAD, 2)
        low = lax.rem(my_low + lax.rem(d, QUAD), QUAD)
        return high * QUAD + low

    y_ring = [my_quad * QUAD + lax.rem(my_place + j, QUAD) for j in range(1, QUAD)]
    x_ring = [quad_at(j) * QUAD + my_place for j in range(1, QUAD)]
    opposite = lax.rem(w + half_count, wide_count)
    for vol in (v, other_v):
        for wide in y_ring + x_ring:
            greet(vol, wide, n)
        greet(vol, opposite, n)
        greet(vol, opposite, other_n)

    load_ids = pltpu.make_async_copy(ids, iv, local_sem.at[0])
    load_f = pltpu.make_async_copy(forcing, fv, local_sem.at[1])
    load_own = pltpu.make_async_copy(
        forcing.at[v], f.at[0, pl.ds(2 * v, 2), pl.ds(PAD, CY), :], local_sem.at[2]
    )
    load_ids.start()
    load_f.start()
    load_own.start()

    zeros8 = jnp.zeros((8, CX), jnp.float32)
    for ref in (c, pa, qa, pb, qb):
        for t in (0, 1):
            for z in range(NZ):
                ref[t, z, 0:8, :] = zeros8
                ref[t, z, ROWS_ALL - 8 : ROWS_ALL, :] = zeros8
    outside = pl.multiple_of(PAD - HALO + other_n * 0 + n * (CY + HALO), 8)
    inside = pl.multiple_of(PAD - HALO + other_n * (CY + HALO), 8)
    for ref in (f, c):
        for t in (0, 1):
            for z in range(NZ):
                ref[t, z, pl.ds(outside, 8), :] = zeros8

    load_ids.wait()
    for layer in (0, 1):
        c[0, 2 * v + layer, PAD : PAD + CY, :] = select_materials(iv[layer], materials)
    load_f.wait()

    span = wide_count * CX

    half = span // 2

    def op_chunk(s):
        return pltpu.make_async_copy(
            op.at[:, pl.ds(pl.multiple_of(s * span + v * half, half), half)],
            opv.at[:, pl.ds(pl.multiple_of(s * half, half), half)],
            op_sem.at[s],
        )

    load_mine = pltpu.make_async_copy(
        op.at[pl.ds(pl.multiple_of(n * RX, RX), RX), 0:span], op_mine, local_sem.at[3]
    )

    edge_row = pl.multiple_of(other_n * (CY - 8), 8)
    lane = lax.broadcasted_iota(jnp.int32, (GROUP_ROWS, CX), 1)
    lane8 = lax.broadcasted_iota(jnp.int32, (8, CX), 1)
    early = lax.rem(lane[: GROUP_ROWS // 2], SLOT) < 4
    for direction, has_side in ((0, has_left), (1, has_right)):

        @pl.when(jnp.logical_not(has_side))
        def _(direction=direction):
            for vol in (0, 1):
                got_strip[direction, vol] = jnp.zeros((GROUP_ROWS // 2, CX), jnp.float32)
                got_corner[direction, vol] = zeros8

    for k in (0, 1):
        packed = jnp.zeros((GROUP_ROWS, CX), jnp.float32)
        edge = jnp.zeros((8, CX), jnp.float32)
        for field in range(4):
            for group in range(GROUPS):
                rows = pl.ds(group * GROUP_ROWS, GROUP_ROWS)
                if field < 2:
                    x = fv[k, field, rows, :]
                else:
                    x = c[0, 2 * v + field - 2, pl.ds(PAD + group * GROUP_ROWS, GROUP_ROWS), :]
                at = group * 4 * SLOT + field * SLOT
                x = pltpu.roll(x, (at + 4) % CX, 1)
                packed = jnp.where((lane >= at) & (lane < at + SLOT), x, packed)
            if field < 2:
                x = fv[k, field, pl.ds(edge_row, 8), :]
            else:
                x = c[0, 2 * v + field - 2, pl.ds(PAD + edge_row, 8), :]
            at = field * SLOT
            x = pltpu.roll(x, at + 4, 1)
            edge = jnp.where((lane8 >= at) & (lane8 < at + SLOT), x, edge)
        a, b = packed[: GROUP_ROWS // 2], packed[GROUP_ROWS // 2 :]
        strip[k, 0] = jnp.where(early, a, pltpu.roll(b, 4, 1))
        strip[k, 1] = jnp.where(early, pltpu.roll(a, CX - 4, 1), b)
        corner[k] = edge

    sides = jnp.where(has_left, 4, 0) + jnp.where(has_right, 4, 0)
    pl.semaphore_wait(barrier, len(greeted) + sides)
    for wide in y_ring:
        signal(relay.at[0], v, wide, n)

    sends = []

    def send(src, dst, send_sem, recv_sem, where, only=None):
        copy = pltpu.make_async_remote_copy(
            src_ref=src,
            dst_ref=dst,
            send_sem=send_sem,
            recv_sem=recv_sem,
            device_id=where,
            device_id_type=MESH,
        )
        if only is None:
            copy.start()
        else:

            @pl.when(only)
            def _():
                copy.start()

        sends.append((copy, only))

    own_layers = pl.ds(2 * v, 2)
    there_row = pl.multiple_of(PAD - HALO + n * (CY + HALO), 8)
    for k in (0, 1):
        for direction, side, has_side in ((0, right, has_right), (1, left, has_left)):
            send(
                strip.at[k, direction],
                got_strip.at[direction, v],
                s_send.at[6 + 2 * direction + k],
                s_recv.at[6 + 2 * direction + v],
                device(k, side, n),
                has_side,
            )
    send(
        fv.at[other_v],
        f.at[0, own_layers, pl.ds(PAD, CY), :],
        s_send.at[0],
        s_recv.at[0],
        device(other_v, w, n),
    )
    own_block = c.at[0, own_layers, pl.ds(PAD, CY), :]
    send(own_block, own_block, s_send.at[1], s_recv.at[1], device(other_v, w, n))
    for k in (0, 1):
        send(
            fv.at[k, :, pl.ds(edge_row, 8), :],
            f.at[0, own_layers, pl.ds(there_row, 8), :],
            s_send.at[2 + k],
            s_recv.at[2 + v],
            device(k, w, other_n),
        )
        send(
            c.at[0, own_layers, pl.ds(pl.multiple_of(PAD + edge_row, 8), 8), :],
            c.at[0, own_layers, pl.ds(there_row, 8), :],
            s_send.at[4 + k],
            s_recv.at[4 + v],
            device(k, w, other_n),
        )
        for direction, side, has_side in ((0, right, has_right), (1, left, has_left)):
            send(
                corner.at[k],
                got_corner.at[direction, v],
                s_send.at[10 + 2 * direction + k],
                s_recv.at[10 + 2 * direction + v],
                device(k, side, other_n),
                has_side,
            )

    def start_op(s, carry):
        op_chunk(s).start()
        return carry

    lax.fori_loop(0, BY, start_op, 0)
    load_mine.start()
    pl.semaphore_wait(relay.at[0], QUAD - 1)
    for wide, narrow in ((opposite, n), (opposite, other_n), (w, other_n)):
        signal(relay.at[1], v, wide, narrow)

    def wait_bytes(ref, sem):
        pltpu.make_async_copy(ref, ref, sem).wait()

    for direction, has_side in ((0, has_left), (1, has_right)):

        @pl.when(has_side)
        def _(direction=direction):
            for vol in (0, 1):
                wait_bytes(got_strip.at[direction, vol], s_recv.at[6 + 2 * direction + vol])
                wait_bytes(got_corner.at[direction, vol], s_recv.at[10 + 2 * direction + vol])

    for z in range(NZ):
        vol = z // 2
        a, b = got_strip[0, vol], got_strip[1, vol]
        merged = jnp.concatenate(
            [
                jnp.where(early, a, pltpu.roll(b, 4, 1)),
                jnp.where(early, pltpu.roll(a, CX - 4, 1), b),
            ],
            axis=0,
        )
        from_left8 = lax.rem(lane8, SLOT) < 4
        merged8 = jnp.where(from_left8, got_corner[0, vol], got_corner[1, vol])
        for which, ref in ((0, f), (2, c)):
            field = which + z % 2
            for group in range(GROUPS):
                at = group * 4 * SLOT + field * SLOT
                x = pltpu.roll(merged, (CX - 4 - at) % CX, 1)
                x = jnp.where((lane < 4) | (lane >= CX - 4), x, 0.0)
                ref[1, z, pl.ds(PAD + group * GROUP_ROWS, GROUP_ROWS), :] = x
            at = field * SLOT
            x = pltpu.roll(merged8, (CX - 4 - at) % CX, 1)
            x = jnp.where((lane8 < 4) | (lane8 >= CX - 4), x, 0.0)
            ref[1, z, pl.ds(inside, 8), :] = x
    load_own.wait()
    wait_bytes(f.at[0, pl.ds(2 * other_v, 2), pl.ds(PAD, CY), :], s_recv.at[0])
    wait_bytes(c.at[0, pl.ds(2 * other_v, 2), pl.ds(PAD, CY), :], s_recv.at[1])
    for vol in (0, 1):
        wait_bytes(f.at[0, pl.ds(2 * vol, 2), pl.ds(inside, 8), :], s_recv.at[2 + vol])
        wait_bytes(c.at[0, pl.ds(2 * vol, 2), pl.ds(inside, 8), :], s_recv.at[4 + vol])

    lane_c = lax.broadcasted_iota(jnp.int32, (CHUNK, CX), 1)
    first = lane_c == 0
    final = lane_c == CX - 1

    def box(ref, r, layers, tiles):
        inner = range(max(layers[0] - 1, 0), min(layers[-1] + 2, NZ))
        sums = []
        for t in (0, 1):
            y = {
                z: ref[t, z, pl.ds(r - 1, CHUNK), :]
                + ref[t, z, pl.ds(r, CHUNK), :]
                + ref[t, z, pl.ds(r + 1, CHUNK), :]
                for z in inner
            }
            low = y[0] + y[1] if 0 in layers or 1 in layers else None
            high = y[2] + y[3] if 2 in layers or 3 in layers else None
            made = {}
            for z in layers:
                made[z] = (
                    low if z == 0 else high if z == 3 else low + y[2] if z == 1 else y[1] + high
                )
            sums.append(made)
        result = ({}, {})
        for z in layers:
            center, side = sums[0][z], sums[1][z]
            center_up, side_up = pltpu.roll(center, 1, 1), pltpu.roll(side, 1, 1)
            center_down, side_down = (
                pltpu.roll(center, CX - 1, 1),
                pltpu.roll(side, CX - 1, 1),
            )
            result[0][z] = (
                center
                + jnp.where(first, side_up, center_up)
                + jnp.where(final, side_down, center_down)
            )
            if 1 in tiles:
                result[1][z] = (
                    side
                    + jnp.where(first, center_up, side_up)
                    + jnp.where(final, center_down, side_down)
                )
        return result

    def rows_of(i):
        return pl.multiple_of(PAD - HALO + i * CHUNK, 8)

    both = (0, 1)

    def first_sweep(i, layers):
        r = rows_of(i)
        sums = box(c, r, layers, both)
        for t in both:
            for z in layers:
                at = (t, z, pl.ds(r, CHUNK), slice(None))
                cond = c[at]
                diagonal = 38.5 * cond + 0.5 * sums[t][z]
                inverse = jnp.where(cond > 0.0, 1.0 / diagonal, 0.0)
                inv[at] = inverse
                u = gain0 * f[at] * inverse
                pa[at] = u
                qa[at] = cond * u

    def sweep(p, q, i, use, layers, tiles):
        r = rows_of(i)
        p_sums, q_sums = box(p, r, layers, tiles), box(q, r, layers, tiles)
        for t in tiles:
            for z in layers:
                at = (t, z, pl.ds(r, CHUNK), slice(None))
                cond = c[at]
                u = p[at]
                scaled = (
                    f[at] + 0.5 * (cond * p_sums[t][z] + q_sums[t][z]) - q[at]
                ) * inv[at] - u
                use(at, cond, u, scaled)

    def second_sweep(i, layers, tiles):
        def use(at, cond, u, scaled):
            u = (1.0 + keep1) * u + gain1 * scaled
            pb[at] = u
            qb[at] = cond * u

        sweep(pa, qa, i, use, layers, tiles)

    def third_sweep(i, layers):
        def use(at, cond, u, scaled):
            moved = gain0 * scaled
            u = u + moved
            m[at] = moved
            pa[at] = u
            qa[at] = cond * u

        sweep(pb, qb, i, use, layers, both)

    def fourth_sweep(i, layers):
        def use(at, cond, u, scaled):
            pb[at] = u + (keep1 * m[at] + gain1 * scaled)

        sweep(pa, qa, i, use, layers, (0,))

    def for_chunks(step):
        def body(i, carry):
            step(i)
            return carry

        lax.fori_loop(0, CHUNKS, body, 0, unroll=CHUNKS)

    my_columns = pl.ds(pl.multiple_of(w * CX, CX), CX)

    def share(block, numbers, narrows):
        def to(i, carry):
            j = 1 + lax.rem(i + wide_count // 2 - 1, wide_count - 1)
            for number, narrow in zip(numbers, narrows):
                pltpu.make_async_remote_copy(
                    src_ref=block,
                    dst_ref=block,
                    send_sem=g_send.at[number],
                    recv_sem=g_recv.at[number],
                    device_id=device(v, lax.rem(w + j, wide_count), narrow),
                    device_id_type=MESH,
                ).start()
            return carry

        lax.fori_loop(0, wide_count - 1, to, 0)
        if len(numbers) == 2:
            pltpu.make_async_remote_copy(
                src_ref=block,
                dst_ref=block,
                send_sem=g_send.at[numbers[1]],
                recv_sem=g_recv.at[numbers[1]],
                device_id=device(v, w, other_n),
                device_id_type=MESH,
            ).start()

    def trace():
        return pb[0, NZ - 1, pl.ds(PAD, BY, stride=CY // BY), :].astype(jnp.bfloat16)

    row_of = lax.rem(lax.broadcasted_iota(jnp.int32, (2 * BY, CX), 0), BY)

    owner = my_high
    elsewhere = owner != v
    half_columns = pl.ds(pl.multiple_of(lax.rem(w, half_count) * CX, CX), CX)

    def trace_copy(block, g, send_sem, recv_sem, wide):
        return pltpu.make_async_remote_copy(
            src_ref=block,
            dst_ref=g.at[v, :, half_columns],
            send_sem=send_sem,
            recv_sem=recv_sem,
            device_id=device(owner, wide, n),
            device_id_type=MESH,
        )

    def share_trace(block, g, number, recv_sem):
        def to(i, carry):
            i = wide_count - i
            place = lax.rem(my_place + lax.rem(i, QUAD), QUAD)
            wide = quad_at(i // QUAD) * QUAD + place
            trace_copy(block, g, g_send.at[number], recv_sem, wide).start()
            return carry

        lax.fori_loop(1, wide_count, to, 0)

        @pl.when(elsewhere)
        def _():
            trace_copy(block, g, pair_send.at[number], recv_sem, w).start()

        @pl.when(jnp.logical_not(elsewhere))
        def _():
            pltpu.make_async_copy(block, g.at[v, :, half_columns], recv_sem).start()

    lanes = QUAD * CX

    def against_quad(x, first_lane, total, first_row):
        for s in range(first_row, BY):
            block = opv[:, pl.ds(pl.multiple_of(s * half + first_lane, lanes), lanes)]
            rows = lax.dot_general(
                x, block, (((1,), (1,)), ((), ())), preferred_element_type=jnp.float32
            )
            total = total + jnp.where(row_of == s, rows, 0.0)
        return total

    def product(g, first_row, arriving):
        def add(i, total):
            low = lax.rem(my_low + i + i // 2 - 2 * (i // 3), QUAD)
            if arriving:
                wait_bytes(g.at[:, :, 0:lanes], q_recv.at[low])
            x = g[:, :, pl.ds(pl.multiple_of(low * lanes, lanes), lanes)]
            return against_quad(x.reshape(2 * BY, lanes), low * lanes, total, first_row)

        total = lax.fori_loop(0, QUAD, add, jnp.zeros((2 * BY, CX), jnp.float32))
        return [
            jnp.sum(total[k * BY : (k + 1) * BY], axis=0, keepdims=True) for k in (0, 1)
        ]

    is_low = v == 0

    def mine_and_theirs(parts):
        return (
            jnp.where(is_low, parts[0], parts[1]),
            jnp.where(is_low, parts[1], parts[0]),
        )

    for_chunks(lambda i: first_sweep(i, (2, 3)))
    for_chunks(lambda i: second_sweep(i, (3,), (0,)))
    own_trace[0] = trace()
    pl.semaphore_wait(relay.at[1], 3)
    share_trace(own_trace.at[0], g1, 0, q_recv.at[my_low])

    my_half = pl.ds(pl.multiple_of(v * half, half), half)
    their_half = pl.ds(pl.multiple_of(other_v * half, half), half)
    send(
        op.at[pl.ds(pl.multiple_of(other_n * RX, RX), RX), my_half],
        op_other.at[:, my_half],
        x_send.at[0],
        x_recv.at[0],
        device(v, w, other_n),
    )

    for_chunks(lambda i: first_sweep(i, (0, 1)))
    for_chunks(lambda i: second_sweep(i, (1, 2, 3), both))
    for_chunks(lambda i: third_sweep(i, (2, 3)))
    for_chunks(lambda i: fourth_sweep(i, (3,)))
    own_trace[1] = trace()
    share_trace(own_trace.at[1], g2, 1, g_recv.at[1])

    for s in range(BY):
        op_chunk(s).wait()
    mine1, theirs1 = mine_and_theirs(product(g1, 0, True))
    swap[0] = jnp.broadcast_to(theirs1, (8, CX))
    send(swap.at[0], swap.at[1], x_send.at[3], x_recv.at[3], device(other_v, w, n))
    top = NZ - 1
    lane1 = lax.broadcasted_iota(jnp.int32, (8, CX), 1)

    def tile(ref, t, z, row):
        return ref[t, z, row : row + 8, :]

    def neighbours(ref, z, row):
        center, side = tile(ref, 0, z, row), tile(ref, 1, z, row)
        before = jnp.where(lane1 == 0, pltpu.roll(side, 1, 1), pltpu.roll(center, 1, 1))
        after = jnp.where(
            lane1 == CX - 1, pltpu.roll(side, CX - 1, 1), pltpu.roll(center, CX - 1, 1)
        )
        return before, after

    cond8, inverse8 = tile(c, 0, top, PAD), tile(inv, 0, top, PAD)
    cond_before, cond_after = neighbours(c, top, PAD)
    inverse_before, inverse_after = neighbours(inv, top, PAD)
    here8 = couple_gain * ((1.0 + keep1 - gain1) * gain0 + gain1) * inverse8
    beside = 0.5 * couple_gain * gain1 * gain0 * inverse8
    before8 = beside * (cond8 + cond_before) * inverse_before
    after8 = beside * (cond8 + cond_after) * inverse_after
    coef[n, 0:4, my_columns] = jnp.concatenate(
        [tile(pb, 0, top, PAD)[0:1], here8[0:1], before8[0:1], after8[0:1]], axis=0
    )
    share(coef.at[n, 0:4, my_columns], (2, 3), (n, other_n))

    wait_bytes(swap.at[1], x_recv.at[3])
    part[n, 0:1, my_columns] = mine1 + swap[1, 0:1, :]
    share(part.at[n, 0:1, my_columns], (4, 5), (n, other_n))

    wait_bytes(op_other.at[:, my_half], x_recv.at[0])
    send(
        op_other.at[:, my_half],
        op_other.at[:, my_half],
        x_send.at[1],
        x_recv.at[1],
        device(other_v, w, n),
    )
    for_chunks(lambda i: second_sweep(i, (0,), both))
    for_chunks(lambda i: third_sweep(i, (0, 1)))
    for_chunks(lambda i: fourth_sweep(i, (0, 1, 2)))

    def store_rows(number, y, count):
        here = out_p.at[v, :, pl.ds(y, count), :]
        own = pltpu.make_async_copy(
            pb.at[0, own_layers, pl.ds(PAD + y, count), :], here, o_local.at[number]
        )
        own.start()
        send(
            pb.at[0, pl.ds(2 * other_v, 2), pl.ds(PAD + y, count), :],
            here,
            o_send.at[number],
            o_recv.at[number],
            device(other_v, w, n),
        )
        return own

    stores = [store_rows(0, 8, CY - 16)]

    wait_bytes(g2, g_recv.at[1])
    mine2, theirs2 = mine_and_theirs(product(g2, 1, False))
    part2_own[0] = jnp.broadcast_to(mine2, (8, CX))
    part2_own[1] = jnp.broadcast_to(theirs2, (8, CX))
    for number, (which, vol, narrow) in enumerate(
        ((0, v, other_n), (1, other_v, n), (1, other_v, other_n))
    ):
        send(
            part2_own.at[which],
            part2_got.at[number],
            x_send.at[4 + number],
            x_recv.at[4 + number],
            device(vol, w, narrow),
        )
    wait_bytes(coef.at[0, 0:4, CX:], g_recv.at[2])
    wait_bytes(coef.at[0, 0:4, :], g_recv.at[3])
    wait_bytes(op_other.at[:, their_half], x_recv.at[1])
    wait_bytes(part.at[0, 0:1, CX:], g_recv.at[4])
    wait_bytes(part.at[0, 0:1, :], g_recv.at[5])
    total[0:1, :] = part[0, 0:1, :] + part[1, 0:1, :]

    is_first = n == 0
    row8 = lax.broadcasted_iota(jnp.int32, (8, CX), 0)
    here = jnp.broadcast_to(total[0:1, my_columns], (8, CX))
    beyond = jnp.broadcast_to(
        total[0:1, pl.ds(pl.multiple_of(right * CX, CX), CX)], (8, CX)
    )
    here_high, beyond_high = pltpu.roll(here, CX - RX, 1), pltpu.roll(beyond, CX - RX, 1)

    def source_rows(low, high, width):
        return jnp.where(lane8 < width, couple_gain * jnp.where(is_first, low, high), 0.0)

    delta_own = source_rows(here, here_high, RX)
    delta_side = source_rows(beyond, beyond_high, 1)
    below = jnp.where(is_first, 1.0, 0.0)
    delta_below = below * source_rows(here_high, here_high, RX)
    delta_below_side = below * source_rows(beyond_high, beyond_high, 1)

    def x_sum(center, side):
        return (
            center
            + pltpu.roll(center, 1, 1)
            + jnp.where(
                lane8 == CX - 1, pltpu.roll(side, CX - 1, 1), pltpu.roll(center, CX - 1, 1)
            )
        )

    def added(delta, side, row, tile_row, near, at_target):
        def spread_row(ref, t):
            return jnp.broadcast_to(ref[t, top, row : row + 1, :], (8, CX))

        q_center = gain0 * delta * spread_row(inv, 0)
        q_side = gain0 * side * spread_row(inv, 1)
        s_q = jnp.where(near, x_sum(q_center, q_side), 0.0)
        s_cq = jnp.where(
            near, x_sum(spread_row(c, 0) * q_center, spread_row(c, 1) * q_side), 0.0
        )
        for z in (top - 1, top):
            rows = pl.ds(tile_row, 8)
            cond = c[0, z, rows, :]
            inverse = inv[0, z, rows, :]
            change = gain1 * 0.5 * (cond * s_q + s_cq) * inverse
            if z == top and at_target is not None:
                q = jnp.where(at_target, q_center, 0.0)
                source = jnp.where(at_target, delta, 0.0)
                change = (
                    change
                    + (1.0 + keep1) * q
                    + gain1 * ((source - cond * q) * inverse - q)
                )
            pb[0, z, rows, :] = pb[0, z, rows, :] + change

    added(delta_own, delta_side, PAD, PAD, row8 <= 1, row8 == 0)
    added(delta_below, delta_below_side, PAD + CY, PAD + CY - 8, row8 == 7, None)
    stores.append(store_rows(1, 0, 8))
    stores.append(store_rows(2, CY - 8, 8))

    lane_all = lax.broadcasted_iota(jnp.int32, (1, span), 1)
    at_targets = lax.rem(lane_all, CX) < RX
    traction = total[0:1, :]
    rows = []
    for half_n in (0, 1):
        value = traction if half_n == 0 else pltpu.roll(traction, span - RX, 1)
        value = jnp.where(at_targets, value, 0.0)
        rows.append(
            coef[half_n, 0:1, :]
            + coef[half_n, 1:2, :] * value
            + coef[half_n, 2:3, :] * pltpu.roll(value, 1, 1)
            + coef[half_n, 3:4, :] * pltpu.roll(value, span - 1, 1)
        )
    own_row = jnp.where(is_first, rows[0], rows[1]).astype(jnp.bfloat16)
    other_row = jnp.where(is_first, rows[1], rows[0]).astype(jnp.bfloat16)

    def against(block, row):
        return lax.dot_general(
            jnp.broadcast_to(row, (BY, span)),
            block,
            (((1,), (1,)), ((), ())),
            preferred_element_type=jnp.float32,
        )

    load_mine.wait()
    last = against(op_mine[...], own_row) + against(op_other[...], other_row)
    for number in range(3):
        wait_bytes(part2_got.at[number], x_recv.at[4 + number])
    part2 = part2_own[0] + part2_got[0] + part2_got[1] + part2_got[2]
    part2 = jnp.where(is_first, part2, pltpu.roll(part2, CX - RX, 1))
    row_t[...] = part2[0:1, 0:RX] + last[0:1, :]
    store_t = pltpu.make_async_copy(row_t, out_t, o_local.at[3])
    store_t.start()
    stores.append(store_t)

    for own in stores:
        own.wait()
    for number, (y, count) in enumerate(((8, CY - 16), (0, 8), (CY - 8, 8))):
        wait_bytes(out_p.at[other_v, :, pl.ds(y, count), :], o_recv.at[number])
    for copy, only in sends:
        if only is None:
            copy.wait_send()
        else:

            @pl.when(only)
            def _(copy=copy):
                copy.wait_send()

    for number, g in enumerate((g1, g2)):
        wait_bytes(g.at[0, :, 0 : (half_count - 1) * CX], g_send.at[number])
        wait_bytes(g.at[0], g_send.at[number])

        @pl.when(elsewhere)
        def _(number=number):
            wait_bytes(own_trace.at[number], pair_send.at[number])

    for number, ref, count in ((2, coef, 4), (4, part, 1)):
        wait_bytes(ref.at[0, 0:count, CX:], g_send.at[number])
        wait_bytes(ref.at[0, 0:count, :], g_send.at[number + 1])


def hand_over(pressure, traction, out_p, out_t, held_p, held_t, sem_in, sem_out):
    parts = [(pressure.at[k, z], held_p.at[k, z], out_p.at[k, z]) for k in (0, 1) for z in (0, 1)]
    parts.append((traction, held_t, out_t))
    loads = [
        pltpu.make_async_copy(src, held, sem_in.at[i]) for i, (src, held, _) in enumerate(parts)
    ]
    stores = [
        pltpu.make_async_copy(held, dst, sem_out.at[i]) for i, (_, held, dst) in enumerate(parts)
    ]
    for load in loads:
        load.start()
    for load, store in zip(loads, stores):
        load.wait()
        store.start()
    for store in stores:
        store.wait()


def local(forcing, material_ids, materials, boundary_operator):
    wide_count = lax.axis_size("wide")
    field = pltpu.VMEM((2, NZ, ROWS_ALL, CX), jnp.float32)
    gathered = pltpu.VMEM((2, BY, wide_count * CX // 2), jnp.bfloat16)
    dma = pltpu.SemaphoreType.DMA
    anywhere = pl.BlockSpec(memory_space=pl.ANY)
    rows = boundary_operator.shape[0]
    pressure, traction = pl.pallas_call(
        functools.partial(kernel, wide_count),
        out_shape=(
            jax.ShapeDtypeStruct(forcing.shape, jnp.float32),
            jax.ShapeDtypeStruct((1, RX), jnp.float32),
        ),
        in_specs=[
            anywhere,
            anywhere,
            pl.BlockSpec(memory_space=pltpu.SMEM),
            anywhere,
        ],
        out_specs=(anywhere, anywhere),
        scratch_shapes=[
            pltpu.VMEM(forcing.shape, jnp.float32),
            pltpu.VMEM(material_ids.shape, jnp.int32),
            field,
            field,
            field,
            field,
            field,
            field,
            field,
            field,
            pltpu.VMEM((2, 2, GROUP_ROWS // 2, CX), jnp.float32),
            pltpu.VMEM((2, 8, CX), jnp.float32),
            pltpu.VMEM((2, 2, GROUP_ROWS // 2, CX), jnp.float32),
            pltpu.VMEM((2, 2, 8, CX), jnp.float32),
            pltpu.VMEM((rows, boundary_operator.shape[1] // 2), jnp.bfloat16),
            pltpu.VMEM((2, BY, CX), jnp.bfloat16),
            gathered,
            gathered,
            pltpu.VMEM((2, 8, wide_count * CX), jnp.float32),
            pltpu.VMEM((8, wide_count * CX), jnp.float32),
            pltpu.VMEM((2, 8, wide_count * CX), jnp.float32),
            pltpu.VMEM((2, 8, CX), jnp.float32),
            pltpu.VMEM((3, 8, CX), jnp.float32),
            pltpu.VMEM((2, 8, CX), jnp.float32),
            pltpu.VMEM((1, RX), jnp.float32),
            pltpu.VMEM((RX, wide_count * CX), jnp.bfloat16),
            pltpu.VMEM((RX, wide_count * CX), jnp.bfloat16),
            dma((4,)),
            dma((BY,)),
            dma((14,)),
            dma((14,)),
            dma((6,)),
            dma((6,)),
            dma((7,)),
            dma((7,)),
            dma((3,)),
            dma((3,)),
            dma((4,)),
            dma((QUAD,)),
            pltpu.SemaphoreType.REGULAR((2,)),
            dma((2,)),
        ],
        compiler_params=pltpu.CompilerParams(
            collective_id=0, has_side_effects=True, vmem_limit_bytes=62 * 1024 * 1024
        ),
        cost_estimate=pl.CostEstimate(
            flops=4 * rows * boundary_operator.shape[1],
            bytes_accessed=2 * rows * boundary_operator.shape[1],
            transcendentals=0,
        ),
    )(forcing, material_ids, materials, boundary_operator)
    pressure, traction = pl.pallas_call(
        hand_over,
        out_shape=(
            jax.ShapeDtypeStruct(pressure.shape, jnp.float32),
            jax.ShapeDtypeStruct(traction.shape, jnp.float32),
        ),
        in_specs=[anywhere, anywhere],
        out_specs=(anywhere, anywhere),
        scratch_shapes=[
            pltpu.VMEM(pressure.shape, jnp.float32),
            pltpu.VMEM(traction.shape, jnp.float32),
            dma((5,)),
            dma((5,)),
        ],
    )(pressure, traction)
    return pressure, traction.reshape(RX, 1)


def solution(mesh):
    placed = (
        P(None, "vol", "narrow", "wide"),
        P("vol", "narrow", "wide"),
        P(),
        P("wide", "narrow"),
    )
    return jax.shard_map(
        local,
        mesh=mesh,
        in_specs=placed,
        out_specs=(P(None, "vol", "narrow", "wide"), P(("wide", "narrow"), "vol")),
        check_vma=False,
    )
```

```python
import functools

import jax
import jax.numpy as jnp
from jax import lax
from jax.experimental import pallas as pl
from jax.experimental.pallas import tpu as pltpu
from jax.sharding import PartitionSpec as P

MESH = pl.DeviceIdType.MESH

BY = 16
RX = 64
MAT = 8

lower_edge = 0.25
upper_edge = 1.75
couple_gain = 40.0

middle = (upper_edge + lower_edge) / 2.0
spread = (upper_edge - lower_edge) / 2.0
center_ratio = middle / spread
ratio_0 = 1.0 / center_ratio
ratio_1 = 1.0 / (2.0 * center_ratio - ratio_0)
gain0 = 1.0 / middle
keep1 = ratio_1 * ratio_0
gain1 = 2.0 * ratio_1 / spread

CY = 192
CX = 128
NZ = 4
PAD = 16
ROWS_ALL = PAD + CY + PAD
HALO = 8
CHUNK = 16
CHUNKS = (CY + 2 * HALO) // CHUNK
SLOT = 8
GROUPS = 4
GROUP_ROWS = CY // GROUPS
QUAD = 4


def select_materials(ids, materials):
    value = jnp.full(ids.shape, materials[0], jnp.float32)
    for number in range(1, MAT):
        value = jnp.where(ids == number, materials[number], value)
    return value


def kernel(
    wide_count,
    forcing,
    ids,
    materials,
    op,
    out_p,
    out_t,
    fv,
    iv,
    f,
    c,
    inv,
    m,
    pa,
    qa,
    pb,
    qb,
    strip,
    corner,
    got_strip,
    got_corner,
    opv,
    own_trace,
    g1,
    g2,
    part,
    total,
    coef,
    part2_own,
    part2_got,
    swap,
    row_t,
    op_mine,
    op_other,
    local_sem,
    op_sem,
    s_send,
    s_recv,
    g_send,
    g_recv,
    x_send,
    x_recv,
    o_send,
    o_recv,
    o_local,
    q_recv,
    relay,
    pair_send,
):
    v = lax.axis_index("vol")
    w = lax.axis_index("wide")
    n = lax.axis_index("narrow")
    other_v = 1 - v
    other_n = 1 - n
    right = lax.rem(w + 1, wide_count)
    left = lax.rem(w + wide_count - 1, wide_count)

    def device(vol, wide, narrow):
        return {"vol": vol, "wide": wide, "narrow": narrow}

    barrier = pltpu.get_barrier_semaphore()

    def signal(semaphore, vol, wide, narrow):
        pl.semaphore_signal(
            semaphore, inc=1, device_id=device(vol, wide, narrow), device_id_type=MESH
        )

    greeted = []

    def greet(vol, wide, narrow):
        signal(barrier, vol, wide, narrow)
        greeted.append(0)

    has_left = w > 0
    has_right = w < wide_count - 1
    for has_side, side in ((has_left, left), (has_right, right)):

        @pl.when(has_side)
        def _(side=side):
            for vol in (v, other_v):
                for narrow in (n, other_n):
                    signal(barrier, vol, side, narrow)

    greet(other_v, w, n)
    greet(other_v, w, other_n)
    greet(v, w, other_n)

    half_count = wide_count // 2
    my_quad, my_place = w // QUAD, lax.rem(w, QUAD)
    my_high, my_low = my_quad // QUAD, lax.rem(my_quad, QUAD)

    def quad_at(d):
        high = lax.rem(my_high + d // QUAD, 2)
        low = lax.rem(my_low + lax.rem(d, QUAD), QUAD)
        return high * QUAD + low

    y_ring = [my_quad * QUAD + lax.rem(my_place + j, QUAD) for j in range(1, QUAD)]
    x_ring = [quad_at(j) * QUAD + my_place for j in range(1, QUAD)]
    opposite = lax.rem(w + half_count, wide_count)
    for vol in (v, other_v):
        for wide in y_ring + x_ring:
            greet(vol, wide, n)
        greet(vol, opposite, n)
        greet(vol, opposite, other_n)

    load_ids = pltpu.make_async_copy(ids, iv, local_sem.at[0])
    load_f = pltpu.make_async_copy(forcing, fv, local_sem.at[1])
    load_own = pltpu.make_async_copy(
        forcing.at[v], f.at[0, pl.ds(2 * v, 2), pl.ds(PAD, CY), :], local_sem.at[2]
    )
    load_ids.start()
    load_f.start()
    load_own.start()

    zeros8 = jnp.zeros((8, CX), jnp.float32)
    for ref in (c, pa, qa, pb, qb):
        for t in (0, 1):
            for z in range(NZ):
                ref[t, z, 0:8, :] = zeros8
                ref[t, z, ROWS_ALL - 8 : ROWS_ALL, :] = zeros8
    outside = pl.multiple_of(PAD - HALO + other_n * 0 + n * (CY + HALO), 8)
    inside = pl.multiple_of(PAD - HALO + other_n * (CY + HALO), 8)
    for ref in (f, c):
        for t in (0, 1):
            for z in range(NZ):
                ref[t, z, pl.ds(outside, 8), :] = zeros8

    load_ids.wait()
    for layer in (0, 1):
        c[0, 2 * v + layer, PAD : PAD + CY, :] = select_materials(iv[layer], materials)
    load_f.wait()

    span = wide_count * CX

    half = span // 2

    def op_chunk(s):
        return pltpu.make_async_copy(
            op.at[:, pl.ds(pl.multiple_of(s * span + v * half, half), half)],
            opv.at[:, pl.ds(pl.multiple_of(s * half, half), half)],
            op_sem.at[s],
        )

    load_mine = pltpu.make_async_copy(
        op.at[pl.ds(pl.multiple_of(n * RX, RX), RX), 0:span], op_mine, local_sem.at[3]
    )

    edge_row = pl.multiple_of(other_n * (CY - 8), 8)
    lane = lax.broadcasted_iota(jnp.int32, (GROUP_ROWS, CX), 1)
    lane8 = lax.broadcasted_iota(jnp.int32, (8, CX), 1)
    early = lax.rem(lane[: GROUP_ROWS // 2], SLOT) < 4
    for direction, has_side in ((0, has_left), (1, has_right)):

        @pl.when(jnp.logical_not(has_side))
        def _(direction=direction):
            for vol in (0, 1):
                got_strip[direction, vol] = jnp.zeros((GROUP_ROWS // 2, CX), jnp.float32)
                got_corner[direction, vol] = zeros8

    for k in (0, 1):
        packed = jnp.zeros((GROUP_ROWS, CX), jnp.float32)
        edge = jnp.zeros((8, CX), jnp.float32)
        for field in range(4):
            for group in range(GROUPS):
                rows = pl.ds(group * GROUP_ROWS, GROUP_ROWS)
                if field < 2:
                    x = fv[k, field, rows, :]
                else:
                    x = c[0, 2 * v + field - 2, pl.ds(PAD + group * GROUP_ROWS, GROUP_ROWS), :]
                at = group * 4 * SLOT + field * SLOT
                x = pltpu.roll(x, (at + 4) % CX, 1)
                packed = jnp.where((lane >= at) & (lane < at + SLOT), x, packed)
            if field < 2:
                x = fv[k, field, pl.ds(edge_row, 8), :]
            else:
                x = c[0, 2 * v + field - 2, pl.ds(PAD + edge_row, 8), :]
            at = field * SLOT
            x = pltpu.roll(x, at + 4, 1)
            edge = jnp.where((lane8 >= at) & (lane8 < at + SLOT), x, edge)
        a, b = packed[: GROUP_ROWS // 2], packed[GROUP_ROWS // 2 :]
        strip[k, 0] = jnp.where(early, a, pltpu.roll(b, 4, 1))
        strip[k, 1] = jnp.where(early, pltpu.roll(a, CX - 4, 1), b)
        corner[k] = edge

    sides = jnp.where(has_left, 4, 0) + jnp.where(has_right, 4, 0)
    pl.semaphore_wait(barrier, len(greeted) + sides)
    for wide in y_ring:
        signal(relay.at[0], v, wide, n)

    sends = []

    def send(src, dst, send_sem, recv_sem, where, only=None):
        copy = pltpu.make_async_remote_copy(
            src_ref=src,
            dst_ref=dst,
            send_sem=send_sem,
            recv_sem=recv_sem,
            device_id=where,
            device_id_type=MESH,
        )
        if only is None:
            copy.start()
        else:

            @pl.when(only)
            def _():
                copy.start()

        sends.append((copy, only))

    own_layers = pl.ds(2 * v, 2)
    there_row = pl.multiple_of(PAD - HALO + n * (CY + HALO), 8)
    for k in (0, 1):
        for direction, side, has_side in ((0, right, has_right), (1, left, has_left)):
            send(
                strip.at[k, direction],
                got_strip.at[direction, v],
                s_send.at[6 + 2 * direction + k],
                s_recv.at[6 + 2 * direction + v],
                device(k, side, n),
                has_side,
            )
    send(
        fv.at[other_v],
        f.at[0, own_layers, pl.ds(PAD, CY), :],
        s_send.at[0],
        s_recv.at[0],
        device(other_v, w, n),
    )
    own_block = c.at[0, own_layers, pl.ds(PAD, CY), :]
    send(own_block, own_block, s_send.at[1], s_recv.at[1], device(other_v, w, n))
    for k in (0, 1):
        send(
            fv.at[k, :, pl.ds(edge_row, 8), :],
            f.at[0, own_layers, pl.ds(there_row, 8), :],
            s_send.at[2 + k],
            s_recv.at[2 + v],
            device(k, w, other_n),
        )
        send(
            c.at[0, own_layers, pl.ds(pl.multiple_of(PAD + edge_row, 8), 8), :],
            c.at[0, own_layers, pl.ds(there_row, 8), :],
            s_send.at[4 + k],
            s_recv.at[4 + v],
            device(k, w, other_n),
        )
        for direction, side, has_side in ((0, right, has_right), (1, left, has_left)):
            send(
                corner.at[k],
                got_corner.at[direction, v],
                s_send.at[10 + 2 * direction + k],
                s_recv.at[10 + 2 * direction + v],
                device(k, side, other_n),
                has_side,
            )

    def start_op(s, carry):
        op_chunk(s).start()
        return carry

    lax.fori_loop(0, BY, start_op, 0)
    load_mine.start()
    pl.semaphore_wait(relay.at[0], QUAD - 1)
    for wide, narrow in ((opposite, n), (opposite, other_n), (w, other_n)):
        signal(relay.at[1], v, wide, narrow)

    def wait_bytes(ref, sem):
        pltpu.make_async_copy(ref, ref, sem).wait()

    for direction, has_side in ((0, has_left), (1, has_right)):

        @pl.when(has_side)
        def _(direction=direction):
            for vol in (0, 1):
                wait_bytes(got_strip.at[direction, vol], s_recv.at[6 + 2 * direction + vol])
                wait_bytes(got_corner.at[direction, vol], s_recv.at[10 + 2 * direction + vol])

    for z in range(NZ):
        vol = z // 2
        a, b = got_strip[0, vol], got_strip[1, vol]
        merged = jnp.concatenate(
            [
                jnp.where(early, a, pltpu.roll(b, 4, 1)),
                jnp.where(early, pltpu.roll(a, CX - 4, 1), b),
            ],
            axis=0,
        )
        from_left8 = lax.rem(lane8, SLOT) < 4
        merged8 = jnp.where(from_left8, got_corner[0, vol], got_corner[1, vol])
        for which, ref in ((0, f), (2, c)):
            field = which + z % 2
            for group in range(GROUPS):
                at = group * 4 * SLOT + field * SLOT
                x = pltpu.roll(merged, (CX - 4 - at) % CX, 1)
                x = jnp.where((lane < 4) | (lane >= CX - 4), x, 0.0)
                ref[1, z, pl.ds(PAD + group * GROUP_ROWS, GROUP_ROWS), :] = x
            at = field * SLOT
            x = pltpu.roll(merged8, (CX - 4 - at) % CX, 1)
            x = jnp.where((lane8 < 4) | (lane8 >= CX - 4), x, 0.0)
            ref[1, z, pl.ds(inside, 8), :] = x
    load_own.wait()
    wait_bytes(f.at[0, pl.ds(2 * other_v, 2), pl.ds(PAD, CY), :], s_recv.at[0])
    wait_bytes(c.at[0, pl.ds(2 * other_v, 2), pl.ds(PAD, CY), :], s_recv.at[1])
    for vol in (0, 1):
        wait_bytes(f.at[0, pl.ds(2 * vol, 2), pl.ds(inside, 8), :], s_recv.at[2 + vol])
        wait_bytes(c.at[0, pl.ds(2 * vol, 2), pl.ds(inside, 8), :], s_recv.at[4 + vol])

    lane_c = lax.broadcasted_iota(jnp.int32, (CHUNK, CX), 1)
    first = lane_c == 0
    final = lane_c == CX - 1

    def box(ref, r, layers, tiles):
        inner = range(max(layers[0] - 1, 0), min(layers[-1] + 2, NZ))
        sums = []
        for t in (0, 1):
            y = {
                z: ref[t, z, pl.ds(r - 1, CHUNK), :]
                + ref[t, z, pl.ds(r, CHUNK), :]
                + ref[t, z, pl.ds(r + 1, CHUNK), :]
                for z in inner
            }
            low = y[0] + y[1] if 0 in layers or 1 in layers else None
            high = y[2] + y[3] if 2 in layers or 3 in layers else None
            made = {}
            for z in layers:
                made[z] = (
                    low if z == 0 else high if z == 3 else low + y[2] if z == 1 else y[1] + high
                )
            sums.append(made)
        result = ({}, {})
        for z in layers:
            center, side = sums[0][z], sums[1][z]
            center_up, side_up = pltpu.roll(center, 1, 1), pltpu.roll(side, 1, 1)
            center_down, side_down = (
                pltpu.roll(center, CX - 1, 1),
                pltpu.roll(side, CX - 1, 1),
            )
            result[0][z] = (
                center
                + jnp.where(first, side_up, center_up)
                + jnp.where(final, side_down, center_down)
            )
            if 1 in tiles:
                result[1][z] = (
                    side
                    + jnp.where(first, center_up, side_up)
                    + jnp.where(final, center_down, side_down)
                )
        return result

    def rows_of(i):
        return pl.multiple_of(PAD - HALO + i * CHUNK, 8)

    both = (0, 1)

    def first_sweep(i, layers):
        r = rows_of(i)
        sums = box(c, r, layers, both)
        for t in both:
            for z in layers:
                at = (t, z, pl.ds(r, CHUNK), slice(None))
                cond = c[at]
                diagonal = 38.5 * cond + 0.5 * sums[t][z]
                inverse = jnp.where(cond > 0.0, 1.0 / diagonal, 0.0)
                inv[at] = inverse
                u = gain0 * f[at] * inverse
                pa[at] = u
                qa[at] = cond * u

    def sweep(p, q, i, use, layers, tiles):
        r = rows_of(i)
        p_sums, q_sums = box(p, r, layers, tiles), box(q, r, layers, tiles)
        for t in tiles:
            for z in layers:
                at = (t, z, pl.ds(r, CHUNK), slice(None))
                cond = c[at]
                u = p[at]
                scaled = (
                    f[at] + 0.5 * (cond * p_sums[t][z] + q_sums[t][z]) - q[at]
                ) * inv[at] - u
                use(at, cond, u, scaled)

    def second_sweep(i, layers, tiles):
        def use(at, cond, u, scaled):
            u = (1.0 + keep1) * u + gain1 * scaled
            pb[at] = u
            qb[at] = cond * u

        sweep(pa, qa, i, use, layers, tiles)

    def third_sweep(i, layers):
        def use(at, cond, u, scaled):
            moved = gain0 * scaled
            u = u + moved
            m[at] = moved
            pa[at] = u
            qa[at] = cond * u

        sweep(pb, qb, i, use, layers, both)

    def fourth_sweep(i, layers):
        def use(at, cond, u, scaled):
            pb[at] = u + (keep1 * m[at] + gain1 * scaled)

        sweep(pa, qa, i, use, layers, (0,))

    def for_chunks(step):
        def body(i, carry):
            step(i)
            return carry

        lax.fori_loop(0, CHUNKS, body, 0, unroll=CHUNKS)

    my_columns = pl.ds(pl.multiple_of(w * CX, CX), CX)

    def share(block, numbers, narrows):
        def to(i, carry):
            j = 1 + lax.rem(i + wide_count // 2 - 1, wide_count - 1)
            for number, narrow in zip(numbers, narrows):
                pltpu.make_async_remote_copy(
                    src_ref=block,
                    dst_ref=block,
                    send_sem=g_send.at[number],
                    recv_sem=g_recv.at[number],
                    device_id=device(v, lax.rem(w + j, wide_count), narrow),
                    device_id_type=MESH,
                ).start()
            return carry

        lax.fori_loop(0, wide_count - 1, to, 0, unroll=wide_count - 1)
        if len(numbers) == 2:
            pltpu.make_async_remote_copy(
                src_ref=block,
                dst_ref=block,
                send_sem=g_send.at[numbers[1]],
                recv_sem=g_recv.at[numbers[1]],
                device_id=device(v, w, other_n),
                device_id_type=MESH,
            ).start()

    def trace():
        return pb[0, NZ - 1, pl.ds(PAD, BY, stride=CY // BY), :].astype(jnp.bfloat16)

    row_of = lax.rem(lax.broadcasted_iota(jnp.int32, (2 * BY, CX), 0), BY)

    owner = my_high
    elsewhere = owner != v
    half_columns = pl.ds(pl.multiple_of(lax.rem(w, half_count) * CX, CX), CX)

    def trace_copy(block, g, send_sem, recv_sem, wide):
        return pltpu.make_async_remote_copy(
            src_ref=block,
            dst_ref=g.at[v, :, half_columns],
            send_sem=send_sem,
            recv_sem=recv_sem,
            device_id=device(owner, wide, n),
            device_id_type=MESH,
        )

    def share_trace(block, g, number, recv_sem):
        def to(i, carry):
            i = wide_count - i
            place = lax.rem(my_place + lax.rem(i, QUAD), QUAD)
            wide = quad_at(i // QUAD) * QUAD + place
            trace_copy(block, g, g_send.at[number], recv_sem, wide).start()
            return carry

        lax.fori_loop(1, wide_count, to, 0, unroll=wide_count - 1)

        @pl.when(elsewhere)
        def _():
            trace_copy(block, g, pair_send.at[number], recv_sem, w).start()

        @pl.when(jnp.logical_not(elsewhere))
        def _():
            pltpu.make_async_copy(block, g.at[v, :, half_columns], recv_sem).start()

    lanes = QUAD * CX

    def against_quad(x, first_lane, total, first_row):
        for s in range(first_row, BY):
            block = opv[:, pl.ds(pl.multiple_of(s * half + first_lane, lanes), lanes)]
            rows = lax.dot_general(
                x, block, (((1,), (1,)), ((), ())), preferred_element_type=jnp.float32
            )
            total = total + jnp.where(row_of == s, rows, 0.0)
        return total

    def product(g, first_row, arriving):
        def add(i, total):
            low = lax.rem(my_low + i + i // 2 - 2 * (i // 3), QUAD)
            if arriving:
                wait_bytes(g.at[:, :, 0:lanes], q_recv.at[low])
            x = g[:, :, pl.ds(pl.multiple_of(low * lanes, lanes), lanes)]
            return against_quad(x.reshape(2 * BY, lanes), low * lanes, total, first_row)

        total = lax.fori_loop(0, QUAD, add, jnp.zeros((2 * BY, CX), jnp.float32))
        return [
            jnp.sum(total[k * BY : (k + 1) * BY], axis=0, keepdims=True) for k in (0, 1)
        ]

    is_low = v == 0

    def mine_and_theirs(parts):
        return (
            jnp.where(is_low, parts[0], parts[1]),
            jnp.where(is_low, parts[1], parts[0]),
        )

    for_chunks(lambda i: first_sweep(i, (2, 3)))
    for_chunks(lambda i: second_sweep(i, (3,), (0,)))
    own_trace[0] = trace()
    pl.semaphore_wait(relay.at[1], 3)
    share_trace(own_trace.at[0], g1, 0, q_recv.at[my_low])

    my_half = pl.ds(pl.multiple_of(v * half, half), half)
    their_half = pl.ds(pl.multiple_of(other_v * half, half), half)
    send(
        op.at[pl.ds(pl.multiple_of(other_n * RX, RX), RX), my_half],
        op_other.at[:, my_half],
        x_send.at[0],
        x_recv.at[0],
        device(v, w, other_n),
    )

    for_chunks(lambda i: first_sweep(i, (0, 1)))
    for_chunks(lambda i: second_sweep(i, (1, 2, 3), both))
    for_chunks(lambda i: third_sweep(i, (2, 3)))
    for_chunks(lambda i: fourth_sweep(i, (3,)))
    own_trace[1] = trace()
    share_trace(own_trace.at[1], g2, 1, g_recv.at[1])

    for s in range(BY):
        op_chunk(s).wait()
    mine1, theirs1 = mine_and_theirs(product(g1, 0, True))
    swap[0] = jnp.broadcast_to(theirs1, (8, CX))
    send(swap.at[0], swap.at[1], x_send.at[3], x_recv.at[3], device(other_v, w, n))
    top = NZ - 1
    lane1 = lax.broadcasted_iota(jnp.int32, (8, CX), 1)

    def tile(ref, t, z, row):
        return ref[t, z, row : row + 8, :]

    def neighbours(ref, z, row):
        center, side = tile(ref, 0, z, row), tile(ref, 1, z, row)
        before = jnp.where(lane1 == 0, pltpu.roll(side, 1, 1), pltpu.roll(center, 1, 1))
        after = jnp.where(
            lane1 == CX - 1, pltpu.roll(side, CX - 1, 1), pltpu.roll(center, CX - 1, 1)
        )
        return before, after

    cond8, inverse8 = tile(c, 0, top, PAD), tile(inv, 0, top, PAD)
    cond_before, cond_after = neighbours(c, top, PAD)
    inverse_before, inverse_after = neighbours(inv, top, PAD)
    here8 = couple_gain * ((1.0 + keep1 - gain1) * gain0 + gain1) * inverse8
    beside = 0.5 * couple_gain * gain1 * gain0 * inverse8
    before8 = beside * (cond8 + cond_before) * inverse_before
    after8 = beside * (cond8 + cond_after) * inverse_after
    coef[n, 0:4, my_columns] = jnp.concatenate(
        [tile(pb, 0, top, PAD)[0:1], here8[0:1], before8[0:1], after8[0:1]], axis=0
    )
    share(coef.at[n, 0:4, my_columns], (2, 3), (n, other_n))

    wait_bytes(swap.at[1], x_recv.at[3])
    part[n, 0:1, my_columns] = mine1 + swap[1, 0:1, :]
    share(part.at[n, 0:1, my_columns], (4, 5), (n, other_n))

    wait_bytes(op_other.at[:, my_half], x_recv.at[0])
    send(
        op_other.at[:, my_half],
        op_other.at[:, my_half],
        x_send.at[1],
        x_recv.at[1],
        device(other_v, w, n),
    )
    for_chunks(lambda i: second_sweep(i, (0,), both))
    for_chunks(lambda i: third_sweep(i, (0, 1)))
    for_chunks(lambda i: fourth_sweep(i, (0, 1, 2)))

    def store_rows(number, y, count):
        here = out_p.at[v, :, pl.ds(y, count), :]
        own = pltpu.make_async_copy(
            pb.at[0, own_layers, pl.ds(PAD + y, count), :], here, o_local.at[number]
        )
        own.start()
        send(
            pb.at[0, pl.ds(2 * other_v, 2), pl.ds(PAD + y, count), :],
            here,
            o_send.at[number],
            o_recv.at[number],
            device(other_v, w, n),
        )
        return own

    stores = [store_rows(0, 8, CY - 16)]

    wait_bytes(g2, g_recv.at[1])
    mine2, theirs2 = mine_and_theirs(product(g2, 1, False))
    part2_own[0] = jnp.broadcast_to(mine2, (8, CX))
    part2_own[1] = jnp.broadcast_to(theirs2, (8, CX))
    for number, (which, vol, narrow) in enumerate(
        ((0, v, other_n), (1, other_v, n), (1, other_v, other_n))
    ):
        send(
            part2_own.at[which],
            part2_got.at[number],
            x_send.at[4 + number],
            x_recv.at[4 + number],
            device(vol, w, narrow),
        )
    wait_bytes(coef.at[0, 0:4, CX:], g_recv.at[2])
    wait_bytes(coef.at[0, 0:4, :], g_recv.at[3])
    wait_bytes(op_other.at[:, their_half], x_recv.at[1])
    wait_bytes(part.at[0, 0:1, CX:], g_recv.at[4])
    wait_bytes(part.at[0, 0:1, :], g_recv.at[5])
    total[0:1, :] = part[0, 0:1, :] + part[1, 0:1, :]

    is_first = n == 0
    row8 = lax.broadcasted_iota(jnp.int32, (8, CX), 0)
    here = jnp.broadcast_to(total[0:1, my_columns], (8, CX))
    beyond = jnp.broadcast_to(
        total[0:1, pl.ds(pl.multiple_of(right * CX, CX), CX)], (8, CX)
    )
    here_high, beyond_high = pltpu.roll(here, CX - RX, 1), pltpu.roll(beyond, CX - RX, 1)

    def source_rows(low, high, width):
        return jnp.where(lane8 < width, couple_gain * jnp.where(is_first, low, high), 0.0)

    delta_own = source_rows(here, here_high, RX)
    delta_side = source_rows(beyond, beyond_high, 1)
    below = jnp.where(is_first, 1.0, 0.0)
    delta_below = below * source_rows(here_high, here_high, RX)
    delta_below_side = below * source_rows(beyond_high, beyond_high, 1)

    def x_sum(center, side):
        return (
            center
            + pltpu.roll(center, 1, 1)
            + jnp.where(
                lane8 == CX - 1, pltpu.roll(side, CX - 1, 1), pltpu.roll(center, CX - 1, 1)
            )
        )

    def added(delta, side, row, tile_row, near, at_target):
        def spread_row(ref, t):
            return jnp.broadcast_to(ref[t, top, row : row + 1, :], (8, CX))

        q_center = gain0 * delta * spread_row(inv, 0)
        q_side = gain0 * side * spread_row(inv, 1)
        s_q = jnp.where(near, x_sum(q_center, q_side), 0.0)
        s_cq = jnp.where(
            near, x_sum(spread_row(c, 0) * q_center, spread_row(c, 1) * q_side), 0.0
        )
        for z in (top - 1, top):
            rows = pl.ds(tile_row, 8)
            cond = c[0, z, rows, :]
            inverse = inv[0, z, rows, :]
            change = gain1 * 0.5 * (cond * s_q + s_cq) * inverse
            if z == top and at_target is not None:
                q = jnp.where(at_target, q_center, 0.0)
                source = jnp.where(at_target, delta, 0.0)
                change = (
                    change
                    + (1.0 + keep1) * q
                    + gain1 * ((source - cond * q) * inverse - q)
                )
            pb[0, z, rows, :] = pb[0, z, rows, :] + change

    added(delta_own, delta_side, PAD, PAD, row8 <= 1, row8 == 0)
    added(delta_below, delta_below_side, PAD + CY, PAD + CY - 8, row8 == 7, None)
    stores.append(store_rows(1, 0, 8))
    stores.append(store_rows(2, CY - 8, 8))

    lane_all = lax.broadcasted_iota(jnp.int32, (1, span), 1)
    at_targets = lax.rem(lane_all, CX) < RX
    traction = total[0:1, :]
    rows = []
    for half_n in (0, 1):
        value = traction if half_n == 0 else pltpu.roll(traction, span - RX, 1)
        value = jnp.where(at_targets, value, 0.0)
        rows.append(
            coef[half_n, 0:1, :]
            + coef[half_n, 1:2, :] * value
            + coef[half_n, 2:3, :] * pltpu.roll(value, 1, 1)
            + coef[half_n, 3:4, :] * pltpu.roll(value, span - 1, 1)
        )
    own_row = jnp.where(is_first, rows[0], rows[1]).astype(jnp.bfloat16)
    other_row = jnp.where(is_first, rows[1], rows[0]).astype(jnp.bfloat16)

    def against(block, row):
        return lax.dot_general(
            jnp.broadcast_to(row, (BY, span)),
            block,
            (((1,), (1,)), ((), ())),
            preferred_element_type=jnp.float32,
        )

    load_mine.wait()
    last = against(op_mine[...], own_row) + against(op_other[...], other_row)
    for number in range(3):
        wait_bytes(part2_got.at[number], x_recv.at[4 + number])
    part2 = part2_own[0] + part2_got[0] + part2_got[1] + part2_got[2]
    part2 = jnp.where(is_first, part2, pltpu.roll(part2, CX - RX, 1))
    row_t[...] = part2[0:1, 0:RX] + last[0:1, :]
    store_t = pltpu.make_async_copy(row_t, out_t, o_local.at[3])
    store_t.start()
    stores.append(store_t)

    for own in stores:
        own.wait()
    for number, (y, count) in enumerate(((8, CY - 16), (0, 8), (CY - 8, 8))):
        wait_bytes(out_p.at[other_v, :, pl.ds(y, count), :], o_recv.at[number])
    for copy, only in sends:
        if only is None:
            copy.wait_send()
        else:

            @pl.when(only)
            def _(copy=copy):
                copy.wait_send()

    for number, g in enumerate((g1, g2)):
        wait_bytes(g.at[0, :, 0 : (half_count - 1) * CX], g_send.at[number])
        wait_bytes(g.at[0], g_send.at[number])

        @pl.when(elsewhere)
        def _(number=number):
            wait_bytes(own_trace.at[number], pair_send.at[number])

    for number, ref, count in ((2, coef, 4), (4, part, 1)):
        wait_bytes(ref.at[0, 0:count, CX:], g_send.at[number])
        wait_bytes(ref.at[0, 0:count, :], g_send.at[number + 1])


def hand_over(pressure, traction, out_p, out_t, held_p, held_t, sem_in, sem_out):
    parts = [(pressure.at[k, z], held_p.at[k, z], out_p.at[k, z]) for k in (0, 1) for z in (0, 1)]
    parts.append((traction, held_t, out_t))
    loads = [
        pltpu.make_async_copy(src, held, sem_in.at[i]) for i, (src, held, _) in enumerate(parts)
    ]
    stores = [
        pltpu.make_async_copy(held, dst, sem_out.at[i]) for i, (_, held, dst) in enumerate(parts)
    ]
    for load in loads:
        load.start()
    for load, store in zip(loads, stores):
        load.wait()
        store.start()
    for store in stores:
        store.wait()


def local(forcing, material_ids, materials, boundary_operator):
    wide_count = lax.axis_size("wide")
    field = pltpu.VMEM((2, NZ, ROWS_ALL, CX), jnp.float32)
    gathered = pltpu.VMEM((2, BY, wide_count * CX // 2), jnp.bfloat16)
    dma = pltpu.SemaphoreType.DMA
    anywhere = pl.BlockSpec(memory_space=pl.ANY)
    rows = boundary_operator.shape[0]
    pressure, traction = pl.pallas_call(
        functools.partial(kernel, wide_count),
        out_shape=(
            jax.ShapeDtypeStruct(forcing.shape, jnp.float32),
            jax.ShapeDtypeStruct((1, RX), jnp.float32),
        ),
        in_specs=[
            anywhere,
            anywhere,
            pl.BlockSpec(memory_space=pltpu.SMEM),
            anywhere,
        ],
        out_specs=(anywhere, anywhere),
        scratch_shapes=[
            pltpu.VMEM(forcing.shape, jnp.float32),
            pltpu.VMEM(material_ids.shape, jnp.int32),
            field,
            field,
            field,
            field,
            field,
            field,
            field,
            field,
            pltpu.VMEM((2, 2, GROUP_ROWS // 2, CX), jnp.float32),
            pltpu.VMEM((2, 8, CX), jnp.float32),
            pltpu.VMEM((2, 2, GROUP_ROWS // 2, CX), jnp.float32),
            pltpu.VMEM((2, 2, 8, CX), jnp.float32),
            pltpu.VMEM((rows, boundary_operator.shape[1] // 2), jnp.bfloat16),
            pltpu.VMEM((2, BY, CX), jnp.bfloat16),
            gathered,
            gathered,
            pltpu.VMEM((2, 8, wide_count * CX), jnp.float32),
            pltpu.VMEM((8, wide_count * CX), jnp.float32),
            pltpu.VMEM((2, 8, wide_count * CX), jnp.float32),
            pltpu.VMEM((2, 8, CX), jnp.float32),
            pltpu.VMEM((3, 8, CX), jnp.float32),
            pltpu.VMEM((2, 8, CX), jnp.float32),
            pltpu.VMEM((1, RX), jnp.float32),
            pltpu.VMEM((RX, wide_count * CX), jnp.bfloat16),
            pltpu.VMEM((RX, wide_count * CX), jnp.bfloat16),
            dma((4,)),
            dma((BY,)),
            dma((14,)),
            dma((14,)),
            dma((6,)),
            dma((6,)),
            dma((7,)),
            dma((7,)),
            dma((3,)),
            dma((3,)),
            dma((4,)),
            dma((QUAD,)),
            pltpu.SemaphoreType.REGULAR((2,)),
            dma((2,)),
        ],
        compiler_params=pltpu.CompilerParams(
            collective_id=0, has_side_effects=True, vmem_limit_bytes=62 * 1024 * 1024
        ),
        cost_estimate=pl.CostEstimate(
            flops=4 * rows * boundary_operator.shape[1],
            bytes_accessed=2 * rows * boundary_operator.shape[1],
            transcendentals=0,
        ),
    )(forcing, material_ids, materials, boundary_operator)
    pressure, traction = pl.pallas_call(
        hand_over,
        out_shape=(
            jax.ShapeDtypeStruct(pressure.shape, jnp.float32),
            jax.ShapeDtypeStruct(traction.shape, jnp.float32),
        ),
        in_specs=[anywhere, anywhere],
        out_specs=(anywhere, anywhere),
        scratch_shapes=[
            pltpu.VMEM(pressure.shape, jnp.float32),
            pltpu.VMEM(traction.shape, jnp.float32),
            dma((5,)),
            dma((5,)),
        ],
    )(pressure, traction)
    return pressure, traction.reshape(RX, 1)


def solution(mesh):
    placed = (
        P(None, "vol", "narrow", "wide"),
        P("vol", "narrow", "wide"),
        P(),
        P("wide", "narrow"),
    )
    return jax.shard_map(
        local,
        mesh=mesh,
        in_specs=placed,
        out_specs=(P(None, "vol", "narrow", "wide"), P(("wide", "narrow"), "vol")),
        check_vma=False,
    )
```

```python
import functools

import jax
import jax.numpy as jnp
from jax import lax
from jax.experimental import pallas as pl
from jax.experimental.pallas import tpu as pltpu
from jax.sharding import PartitionSpec as P

MESH = pl.DeviceIdType.MESH

BY = 16
RX = 64
MAT = 8

lower_edge = 0.25
upper_edge = 1.75
couple_gain = 40.0

middle = (upper_edge + lower_edge) / 2.0
spread = (upper_edge - lower_edge) / 2.0
center_ratio = middle / spread
ratio_0 = 1.0 / center_ratio
ratio_1 = 1.0 / (2.0 * center_ratio - ratio_0)
gain0 = 1.0 / middle
keep1 = ratio_1 * ratio_0
gain1 = 2.0 * ratio_1 / spread

CY = 192
CX = 128
NZ = 4
PAD = 16
ROWS_ALL = PAD + CY + PAD
HALO = 8
CHUNK = 16
CHUNKS = (CY + 2 * HALO) // CHUNK
SLOT = 8
GROUPS = 4
GROUP_ROWS = CY // GROUPS
QUAD = 4


def select_materials(ids, materials):
    value = jnp.full(ids.shape, materials[0], jnp.float32)
    for number in range(1, MAT):
        value = jnp.where(ids == number, materials[number], value)
    return value


def kernel(
    wide_count,
    forcing,
    ids,
    materials,
    op,
    out_p,
    out_t,
    fv,
    iv,
    f,
    c,
    inv,
    m,
    pa,
    qa,
    pb,
    qb,
    strip,
    corner,
    got_strip,
    got_corner,
    opv,
    own_trace,
    g1,
    g2,
    part,
    total,
    coef,
    part2_own,
    part2_got,
    swap,
    row_t,
    op_mine,
    op_other,
    local_sem,
    op_sem,
    s_send,
    s_recv,
    g_send,
    g_recv,
    x_send,
    x_recv,
    o_send,
    o_recv,
    o_local,
    q_recv,
    relay,
    pair_send,
):
    v = lax.axis_index("vol")
    w = lax.axis_index("wide")
    n = lax.axis_index("narrow")
    other_v = 1 - v
    other_n = 1 - n
    right = lax.rem(w + 1, wide_count)
    left = lax.rem(w + wide_count - 1, wide_count)

    def device(vol, wide, narrow):
        return {"vol": vol, "wide": wide, "narrow": narrow}

    barrier = pltpu.get_barrier_semaphore()

    def signal(semaphore, vol, wide, narrow):
        pl.semaphore_signal(
            semaphore, inc=1, device_id=device(vol, wide, narrow), device_id_type=MESH
        )

    greeted = []

    def greet(vol, wide, narrow):
        signal(barrier, vol, wide, narrow)
        greeted.append(0)

    has_left = w > 0
    has_right = w < wide_count - 1
    for has_side, side in ((has_left, left), (has_right, right)):

        @pl.when(has_side)
        def _(side=side):
            for vol in (v, other_v):
                for narrow in (n, other_n):
                    signal(barrier, vol, side, narrow)

    greet(other_v, w, n)
    greet(other_v, w, other_n)
    greet(v, w, other_n)

    half_count = wide_count // 2
    my_quad, my_place = w // QUAD, lax.rem(w, QUAD)
    my_high, my_low = my_quad // QUAD, lax.rem(my_quad, QUAD)

    def quad_at(d):
        high = lax.rem(my_high + d // QUAD, 2)
        low = lax.rem(my_low + lax.rem(d, QUAD), QUAD)
        return high * QUAD + low

    y_ring = [my_quad * QUAD + lax.rem(my_place + j, QUAD) for j in range(1, QUAD)]
    x_ring = [quad_at(j) * QUAD + my_place for j in range(1, QUAD)]
    opposite = lax.rem(w + half_count, wide_count)
    for vol in (v, other_v):
        for wide in y_ring + x_ring:
            greet(vol, wide, n)
        greet(vol, opposite, n)
        greet(vol, opposite, other_n)

    load_ids = pltpu.make_async_copy(ids, iv, local_sem.at[0])
    load_f = pltpu.make_async_copy(forcing, fv, local_sem.at[1])
    load_own = pltpu.make_async_copy(
        forcing.at[v], f.at[0, pl.ds(2 * v, 2), pl.ds(PAD, CY), :], local_sem.at[2]
    )
    load_ids.start()
    load_f.start()
    load_own.start()

    zeros8 = jnp.zeros((8, CX), jnp.float32)
    for ref in (c, pa, qa, pb, qb):
        for t in (0, 1):
            for z in range(NZ):
                ref[t, z, 0:8, :] = zeros8
                ref[t, z, ROWS_ALL - 8 : ROWS_ALL, :] = zeros8
    outside = pl.multiple_of(PAD - HALO + other_n * 0 + n * (CY + HALO), 8)
    inside = pl.multiple_of(PAD - HALO + other_n * (CY + HALO), 8)
    for ref in (f, c):
        for t in (0, 1):
            for z in range(NZ):
                ref[t, z, pl.ds(outside, 8), :] = zeros8

    load_ids.wait()
    for layer in (0, 1):
        c[0, 2 * v + layer, PAD : PAD + CY, :] = select_materials(iv[layer], materials)
    load_f.wait()

    span = wide_count * CX

    half = span // 2

    def op_chunk(s):
        return pltpu.make_async_copy(
            op.at[:, pl.ds(pl.multiple_of(s * span + v * half, half), half)],
            opv.at[:, pl.ds(pl.multiple_of(s * half, half), half)],
            op_sem.at[s],
        )

    load_mine = pltpu.make_async_copy(
        op.at[pl.ds(pl.multiple_of(n * RX, RX), RX), 0:span], op_mine, local_sem.at[3]
    )

    edge_row = pl.multiple_of(other_n * (CY - 8), 8)
    lane = lax.broadcasted_iota(jnp.int32, (GROUP_ROWS, CX), 1)
    lane8 = lax.broadcasted_iota(jnp.int32, (8, CX), 1)
    early = lax.rem(lane[: GROUP_ROWS // 2], SLOT) < 4
    for direction, has_side in ((0, has_left), (1, has_right)):

        @pl.when(jnp.logical_not(has_side))
        def _(direction=direction):
            for vol in (0, 1):
                got_strip[direction, vol] = jnp.zeros((GROUP_ROWS // 2, CX), jnp.float32)
                got_corner[direction, vol] = zeros8

    for k in (0, 1):
        packed = jnp.zeros((GROUP_ROWS, CX), jnp.float32)
        edge = jnp.zeros((8, CX), jnp.float32)
        for field in range(4):
            for group in range(GROUPS):
                rows = pl.ds(group * GROUP_ROWS, GROUP_ROWS)
                if field < 2:
                    x = fv[k, field, rows, :]
                else:
                    x = c[0, 2 * v + field - 2, pl.ds(PAD + group * GROUP_ROWS, GROUP_ROWS), :]
                at = group * 4 * SLOT + field * SLOT
                x = pltpu.roll(x, (at + 4) % CX, 1)
                packed = jnp.where((lane >= at) & (lane < at + SLOT), x, packed)
            if field < 2:
                x = fv[k, field, pl.ds(edge_row, 8), :]
            else:
                x = c[0, 2 * v + field - 2, pl.ds(PAD + edge_row, 8), :]
            at = field * SLOT
            x = pltpu.roll(x, at + 4, 1)
            edge = jnp.where((lane8 >= at) & (lane8 < at + SLOT), x, edge)
        a, b = packed[: GROUP_ROWS // 2], packed[GROUP_ROWS // 2 :]
        strip[k, 0] = jnp.where(early, a, pltpu.roll(b, 4, 1))
        strip[k, 1] = jnp.where(early, pltpu.roll(a, CX - 4, 1), b)
        corner[k] = edge

    sides = jnp.where(has_left, 4, 0) + jnp.where(has_right, 4, 0)
    pl.semaphore_wait(barrier, len(greeted) + sides)
    for wide in y_ring:
        signal(relay.at[0], v, wide, n)

    sends = []

    def send(src, dst, send_sem, recv_sem, where, only=None):
        copy = pltpu.make_async_remote_copy(
            src_ref=src,
            dst_ref=dst,
            send_sem=send_sem,
            recv_sem=recv_sem,
            device_id=where,
            device_id_type=MESH,
        )
        if only is None:
            copy.start()
        else:

            @pl.when(only)
            def _():
                copy.start()

        sends.append((copy, only))

    own_layers = pl.ds(2 * v, 2)
    there_row = pl.multiple_of(PAD - HALO + n * (CY + HALO), 8)
    for k in (0, 1):
        for direction, side, has_side in ((0, right, has_right), (1, left, has_left)):
            send(
                strip.at[k, direction],
                got_strip.at[direction, v],
                s_send.at[6 + 2 * direction + k],
                s_recv.at[6 + 2 * direction + v],
                device(k, side, n),
                has_side,
            )
    send(
        fv.at[other_v],
        f.at[0, own_layers, pl.ds(PAD, CY), :],
        s_send.at[0],
        s_recv.at[0],
        device(other_v, w, n),
    )
    own_block = c.at[0, own_layers, pl.ds(PAD, CY), :]
    send(own_block, own_block, s_send.at[1], s_recv.at[1], device(other_v, w, n))
    for k in (0, 1):
        send(
            fv.at[k, :, pl.ds(edge_row, 8), :],
            f.at[0, own_layers, pl.ds(there_row, 8), :],
            s_send.at[2 + k],
            s_recv.at[2 + v],
            device(k, w, other_n),
        )
        send(
            c.at[0, own_layers, pl.ds(pl.multiple_of(PAD + edge_row, 8), 8), :],
            c.at[0, own_layers, pl.ds(there_row, 8), :],
            s_send.at[4 + k],
            s_recv.at[4 + v],
            device(k, w, other_n),
        )
        for direction, side, has_side in ((0, right, has_right), (1, left, has_left)):
            send(
                corner.at[k],
                got_corner.at[direction, v],
                s_send.at[10 + 2 * direction + k],
                s_recv.at[10 + 2 * direction + v],
                device(k, side, other_n),
                has_side,
            )

    def start_op(s, carry):
        op_chunk(s).start()
        return carry

    lax.fori_loop(0, BY, start_op, 0)
    load_mine.start()
    pl.semaphore_wait(relay.at[0], QUAD - 1)
    for wide, narrow in ((opposite, n), (opposite, other_n), (w, other_n)):
        signal(relay.at[1], v, wide, narrow)

    def wait_bytes(ref, sem):
        pltpu.make_async_copy(ref, ref, sem).wait()

    for direction, has_side in ((0, has_left), (1, has_right)):

        @pl.when(has_side)
        def _(direction=direction):
            for vol in (0, 1):
                wait_bytes(got_strip.at[direction, vol], s_recv.at[6 + 2 * direction + vol])
                wait_bytes(got_corner.at[direction, vol], s_recv.at[10 + 2 * direction + vol])

    for z in range(NZ):
        vol = z // 2
        a, b = got_strip[0, vol], got_strip[1, vol]
        merged = jnp.concatenate(
            [
                jnp.where(early, a, pltpu.roll(b, 4, 1)),
                jnp.where(early, pltpu.roll(a, CX - 4, 1), b),
            ],
            axis=0,
        )
        from_left8 = lax.rem(lane8, SLOT) < 4
        merged8 = jnp.where(from_left8, got_corner[0, vol], got_corner[1, vol])
        for which, ref in ((0, f), (2, c)):
            field = which + z % 2
            for group in range(GROUPS):
                at = group * 4 * SLOT + field * SLOT
                x = pltpu.roll(merged, (CX - 4 - at) % CX, 1)
                x = jnp.where((lane < 4) | (lane >= CX - 4), x, 0.0)
                ref[1, z, pl.ds(PAD + group * GROUP_ROWS, GROUP_ROWS), :] = x
            at = field * SLOT
            x = pltpu.roll(merged8, (CX - 4 - at) % CX, 1)
            x = jnp.where((lane8 < 4) | (lane8 >= CX - 4), x, 0.0)
            ref[1, z, pl.ds(inside, 8), :] = x
    load_own.wait()
    wait_bytes(f.at[0, pl.ds(2 * other_v, 2), pl.ds(PAD, CY), :], s_recv.at[0])
    wait_bytes(c.at[0, pl.ds(2 * other_v, 2), pl.ds(PAD, CY), :], s_recv.at[1])
    for vol in (0, 1):
        wait_bytes(f.at[0, pl.ds(2 * vol, 2), pl.ds(inside, 8), :], s_recv.at[2 + vol])
        wait_bytes(c.at[0, pl.ds(2 * vol, 2), pl.ds(inside, 8), :], s_recv.at[4 + vol])

    lane_c = lax.broadcasted_iota(jnp.int32, (CHUNK, CX), 1)
    first = lane_c == 0
    final = lane_c == CX - 1

    def box(ref, r, layers, tiles):
        inner = range(max(layers[0] - 1, 0), min(layers[-1] + 2, NZ))
        sums = []
        for t in (0, 1):
            y = {
                z: ref[t, z, pl.ds(r - 1, CHUNK), :]
                + ref[t, z, pl.ds(r, CHUNK), :]
                + ref[t, z, pl.ds(r + 1, CHUNK), :]
                for z in inner
            }
            low = y[0] + y[1] if 0 in layers or 1 in layers else None
            high = y[2] + y[3] if 2 in layers or 3 in layers else None
            made = {}
            for z in layers:
                made[z] = (
                    low if z == 0 else high if z == 3 else low + y[2] if z == 1 else y[1] + high
                )
            sums.append(made)
        result = ({}, {})
        for z in layers:
            center, side = sums[0][z], sums[1][z]
            center_up, side_up = pltpu.roll(center, 1, 1), pltpu.roll(side, 1, 1)
            center_down, side_down = (
                pltpu.roll(center, CX - 1, 1),
                pltpu.roll(side, CX - 1, 1),
            )
            result[0][z] = (
                center
                + jnp.where(first, side_up, center_up)
                + jnp.where(final, side_down, center_down)
            )
            if 1 in tiles:
                result[1][z] = (
                    side
                    + jnp.where(first, center_up, side_up)
                    + jnp.where(final, center_down, side_down)
                )
        return result

    def rows_of(i):
        return pl.multiple_of(PAD - HALO + i * CHUNK, 8)

    both = (0, 1)

    def first_sweep(i, layers):
        r = rows_of(i)
        sums = box(c, r, layers, both)
        for t in both:
            for z in layers:
                at = (t, z, pl.ds(r, CHUNK), slice(None))
                cond = c[at]
                diagonal = 38.5 * cond + 0.5 * sums[t][z]
                inverse = jnp.where(cond > 0.0, 1.0 / diagonal, 0.0)
                inv[at] = inverse
                u = gain0 * f[at] * inverse
                pa[at] = u
                qa[at] = cond * u

    def sweep(p, q, i, use, layers, tiles):
        r = rows_of(i)
        p_sums, q_sums = box(p, r, layers, tiles), box(q, r, layers, tiles)
        for t in tiles:
            for z in layers:
                at = (t, z, pl.ds(r, CHUNK), slice(None))
                cond = c[at]
                u = p[at]
                scaled = (
                    f[at] + 0.5 * (cond * p_sums[t][z] + q_sums[t][z]) - q[at]
                ) * inv[at] - u
                use(at, cond, u, scaled)

    def second_sweep(i, layers, tiles):
        def use(at, cond, u, scaled):
            u = (1.0 + keep1) * u + gain1 * scaled
            pb[at] = u
            qb[at] = cond * u

        sweep(pa, qa, i, use, layers, tiles)

    def third_sweep(i, layers):
        def use(at, cond, u, scaled):
            moved = gain0 * scaled
            u = u + moved
            m[at] = moved
            pa[at] = u
            qa[at] = cond * u

        sweep(pb, qb, i, use, layers, both)

    def fourth_sweep(i, layers):
        def use(at, cond, u, scaled):
            pb[at] = u + (keep1 * m[at] + gain1 * scaled)

        sweep(pa, qa, i, use, layers, (0,))

    def for_chunks(step):
        def body(i, carry):
            step(i)
            return carry

        lax.fori_loop(0, CHUNKS, body, 0, unroll=CHUNKS)

    my_columns = pl.ds(pl.multiple_of(w * CX, CX), CX)

    def share(block, numbers, narrows):
        def to(i, carry):
            j = 1 + lax.rem(i + wide_count // 2 - 1, wide_count - 1)
            for number, narrow in zip(numbers, narrows):
                pltpu.make_async_remote_copy(
                    src_ref=block,
                    dst_ref=block,
                    send_sem=g_send.at[number],
                    recv_sem=g_recv.at[number],
                    device_id=device(v, lax.rem(w + j, wide_count), narrow),
                    device_id_type=MESH,
                ).start()
            return carry

        lax.fori_loop(0, wide_count - 1, to, 0, unroll=wide_count - 1)
        if len(numbers) == 2:
            pltpu.make_async_remote_copy(
                src_ref=block,
                dst_ref=block,
                send_sem=g_send.at[numbers[1]],
                recv_sem=g_recv.at[numbers[1]],
                device_id=device(v, w, other_n),
                device_id_type=MESH,
            ).start()

    def trace():
        return pb[0, NZ - 1, pl.ds(PAD, BY, stride=CY // BY), :].astype(jnp.bfloat16)

    row_of = lax.rem(lax.broadcasted_iota(jnp.int32, (2 * BY, CX), 0), BY)

    owner = my_high
    elsewhere = owner != v
    half_columns = pl.ds(pl.multiple_of(lax.rem(w, half_count) * CX, CX), CX)

    def trace_copy(block, g, send_sem, recv_sem, wide):
        return pltpu.make_async_remote_copy(
            src_ref=block,
            dst_ref=g.at[v, :, half_columns],
            send_sem=send_sem,
            recv_sem=recv_sem,
            device_id=device(owner, wide, n),
            device_id_type=MESH,
        )

    def share_trace(block, g, number, recv_sem):
        def to(i, carry):
            i = wide_count - i
            place = lax.rem(my_place + lax.rem(i, QUAD), QUAD)
            wide = quad_at(i // QUAD) * QUAD + place
            trace_copy(block, g, g_send.at[number], recv_sem, wide).start()
            return carry

        lax.fori_loop(1, wide_count, to, 0, unroll=wide_count - 1)

        @pl.when(elsewhere)
        def _():
            trace_copy(block, g, pair_send.at[number], recv_sem, w).start()

        @pl.when(jnp.logical_not(elsewhere))
        def _():
            pltpu.make_async_copy(block, g.at[v, :, half_columns], recv_sem).start()

    lanes = QUAD * CX

    def against_quad(x, first_lane, total, first_row):
        for s in range(first_row, BY):
            block = opv[:, pl.ds(pl.multiple_of(s * half + first_lane, lanes), lanes)]
            rows = lax.dot_general(
                x, block, (((1,), (1,)), ((), ())), preferred_element_type=jnp.float32
            )
            total = total + jnp.where(row_of == s, rows, 0.0)
        return total

    def product(g, first_row, arriving):
        def add(i, total):
            low = lax.rem(my_low + i + i // 2 - 2 * (i // 3), QUAD)
            if arriving:
                wait_bytes(g.at[:, :, 0:lanes], q_recv.at[low])
            x = g[:, :, pl.ds(pl.multiple_of(low * lanes, lanes), lanes)]
            return against_quad(x.reshape(2 * BY, lanes), low * lanes, total, first_row)

        total = lax.fori_loop(
            0, QUAD, add, jnp.zeros((2 * BY, CX), jnp.float32), unroll=QUAD
        )
        return [
            jnp.sum(total[k * BY : (k + 1) * BY], axis=0, keepdims=True) for k in (0, 1)
        ]

    is_low = v == 0

    def mine_and_theirs(parts):
        return (
            jnp.where(is_low, parts[0], parts[1]),
            jnp.where(is_low, parts[1], parts[0]),
        )

    for_chunks(lambda i: first_sweep(i, (2, 3)))
    for_chunks(lambda i: second_sweep(i, (3,), (0,)))
    own_trace[0] = trace()
    pl.semaphore_wait(relay.at[1], 3)
    share_trace(own_trace.at[0], g1, 0, q_recv.at[my_low])

    my_half = pl.ds(pl.multiple_of(v * half, half), half)
    their_half = pl.ds(pl.multiple_of(other_v * half, half), half)
    send(
        op.at[pl.ds(pl.multiple_of(other_n * RX, RX), RX), my_half],
        op_other.at[:, my_half],
        x_send.at[0],
        x_recv.at[0],
        device(v, w, other_n),
    )

    for_chunks(lambda i: first_sweep(i, (0, 1)))
    for_chunks(lambda i: (second_sweep(i, (1, 2), both), second_sweep(i, (3,), (1,))))
    for_chunks(lambda i: third_sweep(i, (2, 3)))
    for_chunks(lambda i: fourth_sweep(i, (3,)))
    own_trace[1] = trace()
    share_trace(own_trace.at[1], g2, 1, g_recv.at[1])

    for s in range(BY):
        op_chunk(s).wait()
    mine1, theirs1 = mine_and_theirs(product(g1, 0, True))
    swap[0] = jnp.broadcast_to(theirs1, (8, CX))
    send(swap.at[0], swap.at[1], x_send.at[3], x_recv.at[3], device(other_v, w, n))
    top = NZ - 1
    lane1 = lax.broadcasted_iota(jnp.int32, (8, CX), 1)

    def tile(ref, t, z, row):
        return ref[t, z, row : row + 8, :]

    def neighbours(ref, z, row):
        center, side = tile(ref, 0, z, row), tile(ref, 1, z, row)
        before = jnp.where(lane1 == 0, pltpu.roll(side, 1, 1), pltpu.roll(center, 1, 1))
        after = jnp.where(
            lane1 == CX - 1, pltpu.roll(side, CX - 1, 1), pltpu.roll(center, CX - 1, 1)
        )
        return before, after

    cond8, inverse8 = tile(c, 0, top, PAD), tile(inv, 0, top, PAD)
    cond_before, cond_after = neighbours(c, top, PAD)
    inverse_before, inverse_after = neighbours(inv, top, PAD)
    here8 = couple_gain * ((1.0 + keep1 - gain1) * gain0 + gain1) * inverse8
    beside = 0.5 * couple_gain * gain1 * gain0 * inverse8
    before8 = beside * (cond8 + cond_before) * inverse_before
    after8 = beside * (cond8 + cond_after) * inverse_after
    coef[n, 0:4, my_columns] = jnp.concatenate(
        [tile(pb, 0, top, PAD)[0:1], here8[0:1], before8[0:1], after8[0:1]], axis=0
    )
    share(coef.at[n, 0:4, my_columns], (2, 3), (n, other_n))

    wait_bytes(swap.at[1], x_recv.at[3])
    part[n, 0:1, my_columns] = mine1 + swap[1, 0:1, :]
    share(part.at[n, 0:1, my_columns], (4, 5), (n, other_n))

    wait_bytes(op_other.at[:, my_half], x_recv.at[0])
    send(
        op_other.at[:, my_half],
        op_other.at[:, my_half],
        x_send.at[1],
        x_recv.at[1],
        device(other_v, w, n),
    )
    for_chunks(lambda i: second_sweep(i, (0,), both))
    for_chunks(lambda i: third_sweep(i, (0, 1)))
    for_chunks(lambda i: fourth_sweep(i, (0, 1, 2)))

    def store_rows(number, y, count):
        here = out_p.at[v, :, pl.ds(y, count), :]
        own = pltpu.make_async_copy(
            pb.at[0, own_layers, pl.ds(PAD + y, count), :], here, o_local.at[number]
        )
        own.start()
        send(
            pb.at[0, pl.ds(2 * other_v, 2), pl.ds(PAD + y, count), :],
            here,
            o_send.at[number],
            o_recv.at[number],
            device(other_v, w, n),
        )
        return own

    stores = [store_rows(0, 8, CY - 16)]

    wait_bytes(g2, g_recv.at[1])
    mine2, theirs2 = mine_and_theirs(product(g2, 1, False))
    part2_own[0] = jnp.broadcast_to(mine2, (8, CX))
    part2_own[1] = jnp.broadcast_to(theirs2, (8, CX))
    for number, (which, vol, narrow) in enumerate(
        ((0, v, other_n), (1, other_v, n), (1, other_v, other_n))
    ):
        send(
            part2_own.at[which],
            part2_got.at[number],
            x_send.at[4 + number],
            x_recv.at[4 + number],
            device(vol, w, narrow),
        )
    wait_bytes(coef.at[0, 0:4, CX:], g_recv.at[2])
    wait_bytes(coef.at[0, 0:4, :], g_recv.at[3])
    wait_bytes(op_other.at[:, their_half], x_recv.at[1])
    wait_bytes(part.at[0, 0:1, CX:], g_recv.at[4])
    wait_bytes(part.at[0, 0:1, :], g_recv.at[5])
    total[0:1, :] = part[0, 0:1, :] + part[1, 0:1, :]

    is_first = n == 0
    row8 = lax.broadcasted_iota(jnp.int32, (8, CX), 0)
    here = jnp.broadcast_to(total[0:1, my_columns], (8, CX))
    beyond = jnp.broadcast_to(
        total[0:1, pl.ds(pl.multiple_of(right * CX, CX), CX)], (8, CX)
    )
    here_high, beyond_high = pltpu.roll(here, CX - RX, 1), pltpu.roll(beyond, CX - RX, 1)

    def source_rows(low, high, width):
        return jnp.where(lane8 < width, couple_gain * jnp.where(is_first, low, high), 0.0)

    delta_own = source_rows(here, here_high, RX)
    delta_side = source_rows(beyond, beyond_high, 1)
    below = jnp.where(is_first, 1.0, 0.0)
    delta_below = below * source_rows(here_high, here_high, RX)
    delta_below_side = below * source_rows(beyond_high, beyond_high, 1)

    def x_sum(center, side):
        return (
            center
            + pltpu.roll(center, 1, 1)
            + jnp.where(
                lane8 == CX - 1, pltpu.roll(side, CX - 1, 1), pltpu.roll(center, CX - 1, 1)
            )
        )

    def added(delta, side, row, tile_row, near, at_target):
        def spread_row(ref, t):
            return jnp.broadcast_to(ref[t, top, row : row + 1, :], (8, CX))

        q_center = gain0 * delta * spread_row(inv, 0)
        q_side = gain0 * side * spread_row(inv, 1)
        s_q = jnp.where(near, x_sum(q_center, q_side), 0.0)
        s_cq = jnp.where(
            near, x_sum(spread_row(c, 0) * q_center, spread_row(c, 1) * q_side), 0.0
        )
        for z in (top - 1, top):
            rows = pl.ds(tile_row, 8)
            cond = c[0, z, rows, :]
            inverse = inv[0, z, rows, :]
            change = gain1 * 0.5 * (cond * s_q + s_cq) * inverse
            if z == top and at_target is not None:
                q = jnp.where(at_target, q_center, 0.0)
                source = jnp.where(at_target, delta, 0.0)
                change = (
                    change
                    + (1.0 + keep1) * q
                    + gain1 * ((source - cond * q) * inverse - q)
                )
            pb[0, z, rows, :] = pb[0, z, rows, :] + change

    added(delta_own, delta_side, PAD, PAD, row8 <= 1, row8 == 0)
    added(delta_below, delta_below_side, PAD + CY, PAD + CY - 8, row8 == 7, None)
    stores.append(store_rows(1, 0, 8))
    stores.append(store_rows(2, CY - 8, 8))

    lane_all = lax.broadcasted_iota(jnp.int32, (1, span), 1)
    at_targets = lax.rem(lane_all, CX) < RX
    traction = total[0:1, :]
    rows = []
    for half_n in (0, 1):
        value = traction if half_n == 0 else pltpu.roll(traction, span - RX, 1)
        value = jnp.where(at_targets, value, 0.0)
        rows.append(
            coef[half_n, 0:1, :]
            + coef[half_n, 1:2, :] * value
            + coef[half_n, 2:3, :] * pltpu.roll(value, 1, 1)
            + coef[half_n, 3:4, :] * pltpu.roll(value, span - 1, 1)
        )
    own_row = jnp.where(is_first, rows[0], rows[1]).astype(jnp.bfloat16)
    other_row = jnp.where(is_first, rows[1], rows[0]).astype(jnp.bfloat16)

    def against(block, row):
        return lax.dot_general(
            jnp.broadcast_to(row, (BY, span)),
            block,
            (((1,), (1,)), ((), ())),
            preferred_element_type=jnp.float32,
        )

    load_mine.wait()
    last = against(op_mine[...], own_row) + against(op_other[...], other_row)
    for number in range(3):
        wait_bytes(part2_got.at[number], x_recv.at[4 + number])
    part2 = part2_own[0] + part2_got[0] + part2_got[1] + part2_got[2]
    part2 = jnp.where(is_first, part2, pltpu.roll(part2, CX - RX, 1))
    row_t[...] = part2[0:1, 0:RX] + last[0:1, :]
    store_t = pltpu.make_async_copy(row_t, out_t, o_local.at[3])
    store_t.start()
    stores.append(store_t)

    for own in stores:
        own.wait()
    for number, (y, count) in enumerate(((8, CY - 16), (0, 8), (CY - 8, 8))):
        wait_bytes(out_p.at[other_v, :, pl.ds(y, count), :], o_recv.at[number])
    for copy, only in sends:
        if only is None:
            copy.wait_send()
        else:

            @pl.when(only)
            def _(copy=copy):
                copy.wait_send()

    for number, g in enumerate((g1, g2)):
        wait_bytes(g.at[0, :, 0 : (half_count - 1) * CX], g_send.at[number])
        wait_bytes(g.at[0], g_send.at[number])

        @pl.when(elsewhere)
        def _(number=number):
            wait_bytes(own_trace.at[number], pair_send.at[number])

    for number, ref, count in ((2, coef, 4), (4, part, 1)):
        wait_bytes(ref.at[0, 0:count, CX:], g_send.at[number])
        wait_bytes(ref.at[0, 0:count, :], g_send.at[number + 1])


def hand_over(pressure, traction, out_p, out_t, held_p, held_t, sem_in, sem_out):
    parts = [(pressure.at[k, z], held_p.at[k, z], out_p.at[k, z]) for k in (0, 1) for z in (0, 1)]
    parts.append((traction, held_t, out_t))
    loads = [
        pltpu.make_async_copy(src, held, sem_in.at[i]) for i, (src, held, _) in enumerate(parts)
    ]
    stores = [
        pltpu.make_async_copy(held, dst, sem_out.at[i]) for i, (_, held, dst) in enumerate(parts)
    ]
    for load in loads:
        load.start()
    for load, store in zip(loads, stores):
        load.wait()
        store.start()
    for store in stores:
        store.wait()


def local(forcing, material_ids, materials, boundary_operator):
    wide_count = lax.axis_size("wide")
    field = pltpu.VMEM((2, NZ, ROWS_ALL, CX), jnp.float32)
    gathered = pltpu.VMEM((2, BY, wide_count * CX // 2), jnp.bfloat16)
    dma = pltpu.SemaphoreType.DMA
    anywhere = pl.BlockSpec(memory_space=pl.ANY)
    rows = boundary_operator.shape[0]
    pressure, traction = pl.pallas_call(
        functools.partial(kernel, wide_count),
        out_shape=(
            jax.ShapeDtypeStruct(forcing.shape, jnp.float32),
            jax.ShapeDtypeStruct((1, RX), jnp.float32),
        ),
        in_specs=[
            anywhere,
            anywhere,
            pl.BlockSpec(memory_space=pltpu.SMEM),
            anywhere,
        ],
        out_specs=(anywhere, anywhere),
        scratch_shapes=[
            pltpu.VMEM(forcing.shape, jnp.float32),
            pltpu.VMEM(material_ids.shape, jnp.int32),
            field,
            field,
            field,
            field,
            field,
            field,
            field,
            field,
            pltpu.VMEM((2, 2, GROUP_ROWS // 2, CX), jnp.float32),
            pltpu.VMEM((2, 8, CX), jnp.float32),
            pltpu.VMEM((2, 2, GROUP_ROWS // 2, CX), jnp.float32),
            pltpu.VMEM((2, 2, 8, CX), jnp.float32),
            pltpu.VMEM((rows, boundary_operator.shape[1] // 2), jnp.bfloat16),
            pltpu.VMEM((2, BY, CX), jnp.bfloat16),
            gathered,
            gathered,
            pltpu.VMEM((2, 8, wide_count * CX), jnp.float32),
            pltpu.VMEM((8, wide_count * CX), jnp.float32),
            pltpu.VMEM((2, 8, wide_count * CX), jnp.float32),
            pltpu.VMEM((2, 8, CX), jnp.float32),
            pltpu.VMEM((3, 8, CX), jnp.float32),
            pltpu.VMEM((2, 8, CX), jnp.float32),
            pltpu.VMEM((1, RX), jnp.float32),
            pltpu.VMEM((RX, wide_count * CX), jnp.bfloat16),
            pltpu.VMEM((RX, wide_count * CX), jnp.bfloat16),
            dma((4,)),
            dma((BY,)),
            dma((14,)),
            dma((14,)),
            dma((6,)),
            dma((6,)),
            dma((7,)),
            dma((7,)),
            dma((3,)),
            dma((3,)),
            dma((4,)),
            dma((QUAD,)),
            pltpu.SemaphoreType.REGULAR((2,)),
            dma((2,)),
        ],
        compiler_params=pltpu.CompilerParams(
            collective_id=0, has_side_effects=True, vmem_limit_bytes=62 * 1024 * 1024
        ),
        cost_estimate=pl.CostEstimate(
            flops=4 * rows * boundary_operator.shape[1],
            bytes_accessed=2 * rows * boundary_operator.shape[1],
            transcendentals=0,
        ),
    )(forcing, material_ids, materials, boundary_operator)
    pressure, traction = pl.pallas_call(
        hand_over,
        out_shape=(
            jax.ShapeDtypeStruct(pressure.shape, jnp.float32),
            jax.ShapeDtypeStruct(traction.shape, jnp.float32),
        ),
        in_specs=[anywhere, anywhere],
        out_specs=(anywhere, anywhere),
        scratch_shapes=[
            pltpu.VMEM(pressure.shape, jnp.float32),
            pltpu.VMEM(traction.shape, jnp.float32),
            dma((5,)),
            dma((5,)),
        ],
    )(pressure, traction)
    return pressure, traction.reshape(RX, 1)


def solution(mesh):
    placed = (
        P(None, "vol", "narrow", "wide"),
        P("vol", "narrow", "wide"),
        P(),
        P("wide", "narrow"),
    )
    return jax.shard_map(
        local,
        mesh=mesh,
        in_specs=placed,
        out_specs=(P(None, "vol", "narrow", "wide"), P(("wide", "narrow"), "vol")),
        check_vma=False,
    )
```
